32 devices in a mesh: row: 4 (over x, core), col: 8 (over z, y).
Axes of the slice: x: 2, y: 2, z: 4, core: 2. Of those that a mesh axis runs over, the one named last changes fastest.
Arguments:
- pair_input: bfloat16 [192, 384, 128], P('row', 'col'), may hold values from -6 to 6
- bin_features: bfloat16 [192, 512], P('row'), may hold values from -6 to 6
- context_features: bfloat16 [384, 512], replicated, may hold values from -6 to 6
- proj_weight: bfloat16 [512, 256], replicated, may hold values from -0.25 to 0.25
- conv_weight: bfloat16 [9, 128, 128], replicated, may hold values from -0.1875 to 0.1875
- valid_bins: int32 [576], replicated, may hold values 0 or 1
- cotangent: bfloat16 [192, 384, 128], P('row', 'col'), may hold values from -6 to 6
Outputs:
- pair_output: bfloat16 [192, 384, 128], P('row', 'col')
- pair_grad: bfloat16 [192, 384, 128], P('row', 'col')
- feature_grad: bfloat16 [192, 512], P('row')
- proj_grad: float32 [512, 256], replicated
- conv_grad: float32 [9, 128, 128], replicated
The draws below stay inside these ranges and needn't reach their ends.
All inputs are finite; a program needn't handle non-finite values.
Results may differ from the reference program's by a relative error of at most 0.0065.
Values may be sent and summed in bfloat16 or wider, within the bound.
No kernel may reach another device: no remote copies, remote signals or barrier semaphores. Data moves between devices by JAX's collectives and lax.ppermute only.
A program may use at most 64 MiB of HBM per device.

```python
import jax
import jax.numpy as jnp
from jax import lax

CP = 128
F = 512
BINS = 192
BAND = 384


def with_ends(drawn, own_key, low, high):
    index_at = [jax.random.randint(jax.random.fold_in(own_key, axis), (), 0, length) for axis, length in enumerate(drawn.shape)]
    widest = drawn.shape.index(max(drawn.shape))
    next_to = index_at[:widest] + [(index_at[widest] + 1) % drawn.shape[widest]] + index_at[widest + 1:]
    return drawn.at[tuple(index_at)].set(low).at[tuple(next_to)].set(high)


def steps_of(rng, extent, shards, low, top_value):
    def one(position, parts):
        draws = jax.random.uniform(jax.random.fold_in(jax.random.fold_in(rng, 6), position), (parts,), jnp.float32, low / len(shards), top_value / len(shards))
        return jnp.repeat(jnp.exp(draws), extent[position] // parts).reshape((-1,) + (1,) * (len(extent) - position - 1))

    loudness = one(*shards[0])
    for cut in shards[1:]:
        loudness = loudness * one(*cut)
    return loudness


def normal_values(stream_key, dims, scale, bound, pieces=(), held_as=jnp.bfloat16):
    factor_of = steps_of(stream_key, dims, pieces, -0.22, 0.18) if pieces else 1.0
    drawn = jax.random.normal(stream_key, dims, jnp.float32) * scale * factor_of
    return jnp.minimum(jnp.maximum(drawn, -bound), bound).astype(held_as)


def setup_inputs(seed: int = 0) -> dict:
    key_list = jax.random.split(jax.random.key(seed), 8)
    pair_input = normal_values(key_list[0], (BINS, BAND, CP), 1.0, 6.0, ((0, 4), (1, 8)))
    bin_features = normal_values(key_list[1], (BINS, F), 1.0, 6.0, ((0, 4),))
    context_features = normal_values(key_list[2], (BAND, F), 1.0, 6.0)
    proj_weight = normal_values(key_list[3], (F, 2 * CP), F ** -0.5, 0.25)
    conv_weight = normal_values(key_list[4], (9, CP, CP), (9 * CP) ** -0.5, 0.1875)
    valid_bins = with_ends((jax.random.randint(key_list[5], (BINS + BAND,), 0, 8) < 7).astype(jnp.int32), jax.random.fold_in(key_list[5], 1), 0, 1)
    cotangent = normal_values(key_list[6], (BINS, BAND, CP), 1.0, 6.0, ((0, 4), (1, 8)))
    return dict(pair_input=pair_input, bin_features=bin_features, context_features=context_features, proj_weight=proj_weight, conv_weight=conv_weight, valid_bins=valid_bins, cotangent=cotangent)


def silu_parts(values):
    sigma = jax.nn.sigmoid(values)
    return values * sigma, sigma * (1.0 + values * (1.0 - sigma))


def reference(pair_input, bin_features, context_features, proj_weight, conv_weight, valid_bins, cotangent):
    proj = jnp.dot(bin_features, proj_weight, preferred_element_type=jnp.float32).astype(jnp.bfloat16)
    query_part = proj[:, :CP].astype(jnp.float32)
    context_key = jnp.dot(context_features, proj_weight[:, CP:], preferred_element_type=jnp.float32).astype(jnp.bfloat16)
    key_part = jnp.concatenate([proj[:, CP:], context_key], axis=0)
    valid_float = valid_bins.astype(jnp.float32)
    column_index = jnp.arange(BINS, dtype=jnp.int32)[:, None] + jnp.arange(BAND, dtype=jnp.int32)[None, :]
    key_skew = key_part[column_index].astype(jnp.float32)
    mask = (valid_float[:BINS][:, None] * valid_float[column_index])[:, :, None]
    mixed = (mask * (pair_input.astype(jnp.float32) + query_part[:, None, :] + key_skew)).astype(jnp.bfloat16)
    padded = jnp.pad(mixed, ((1, 1), (1, 1), (0, 0))).astype(jnp.float32)
    weights = conv_weight.astype(jnp.float32)
    conv = jnp.zeros((BINS, BAND, CP), jnp.float32)
    for offset_index in range(9):
        row_step = offset_index // 3 - 1
        band_step = offset_index % 3 - 1
        shifted = padded[1 + row_step:1 + row_step + BINS, 1 + band_step:1 + band_step + BAND]
        conv = conv + jnp.einsum("abc,cd->abd", shifted, weights[offset_index])
    activated, slope = silu_parts(conv)
    pair_output = (pair_input.astype(jnp.float32) + mask * activated).astype(jnp.bfloat16)
    conv_cot = (mask * cotangent.astype(jnp.float32) * slope).astype(jnp.bfloat16)
    cot_float = conv_cot.astype(jnp.float32)
    cot_pad = jnp.pad(cot_float, ((1, 1), (1, 1), (0, 0)))
    back = jnp.zeros((BINS, BAND, CP), jnp.float32)
    tap_grads = []
    for offset_index in range(9):
        row_step = offset_index // 3 - 1
        band_step = offset_index % 3 - 1
        moved = cot_pad[1 - row_step:1 - row_step + BINS, 1 - band_step:1 - band_step + BAND]
        back = back + jnp.einsum("abd,cd->abc", moved, weights[offset_index])
        shifted = padded[1 + row_step:1 + row_step + BINS, 1 + band_step:1 + band_step + BAND]
        tap_grads.append(jnp.einsum("abc,abd->cd", shifted, cot_float))
    conv_grad = jnp.stack(tap_grads)
    pair_grad = (cotangent.astype(jnp.float32) + mask * back).astype(jnp.bfloat16)
    masked = mask * back
    query_grad = jnp.sum(masked, axis=1)
    key_grad = jax.ops.segment_sum(masked.reshape(BINS * BAND, CP), column_index.reshape(-1), num_segments=BINS + BAND)
    bin_grad = jnp.concatenate([query_grad, key_grad[:BINS]], axis=1)
    proj_grad = jnp.dot(bin_features.astype(jnp.float32).T, bin_grad, precision=lax.Precision.HIGHEST)
    context_grad = jnp.dot(context_features.astype(jnp.float32).T, key_grad[BINS:], precision=lax.Precision.HIGHEST)
    proj_grad = proj_grad + jnp.pad(context_grad, ((0, 0), (CP, 0)))
    feature_grad = jnp.dot(bin_grad.astype(jnp.bfloat16), proj_weight.T, preferred_element_type=jnp.float32).astype(jnp.bfloat16)
    return pair_output, pair_grad, feature_grad, proj_grad, conv_grad
```

```python
import functools

import jax
import jax.numpy as jnp
from jax import lax
from jax.experimental import pallas as pl
from jax.experimental.pallas import tpu as pltpu
from jax.sharding import Mesh, PartitionSpec as P

ROW = ("rx", "core")
CHIPS = ("rx", "col")
BF16 = jnp.bfloat16
F32 = jnp.float32
HALO = 2
SIDE = 16
MARGIN = 16
PARAMS = pltpu.CompilerParams(vmem_limit_bytes=56 * 1024 * 1024)


def halo_row(tile, edges, index, above, below, first, last):
    if index < 0:
        return edges[above, last + 1 + index]
    if index >= tile.shape[0]:
        return edges[below, first + index - tile.shape[0]]
    return tile[index]


def neighbours(edges):
    row = lax.axis_index(ROW)
    return jnp.maximum(row - 1, 0), jnp.minimum(row + 1, edges.shape[0] - 1)


def column_kernel(pair_low, pair_high, cot_low, cot_high, edges, to_low, to_high, work):
    tile_rows = pair_low.shape[0]
    band_cols = edges.shape[2]
    above, below = neighbours(edges)
    rows = tile_rows + 2 * HALO
    taken = work.shape[0] // SIDE
    work[rows * SIDE :, :] = jnp.zeros((work.shape[0] - rows * SIDE, work.shape[1]), F32)
    for out, pair, cot, start, picks in (
        (to_low, pair_low, cot_low, 0, (0, 1)),
        (to_high, pair_high, cot_high, band_cols - SIDE, (SIDE - 2, SIDE - 1)),
    ):
        out[:, taken:, :] = jnp.zeros((3, out.shape[1] - taken, out.shape[2]), out.dtype)
        for tile, first, last, columns, slot in (
            (pair, 0, 3, picks, 0),
            (cot, 4, 5, (picks[0] if start == 0 else picks[1],), 2),
        ):
            depth = HALO if slot == 0 else 1
            for index in range(-HALO, tile_rows + HALO):
                if index < -depth or index >= tile_rows + depth:
                    values = jnp.zeros((SIDE, work.shape[1]), F32)
                elif 0 <= index < tile_rows:
                    values = tile[index].astype(F32)
                elif index < 0:
                    values = edges[above, last + 1 + index, start : start + SIDE].astype(F32)
                else:
                    values = edges[below, first + index - tile_rows, start : start + SIDE].astype(F32)
                work[(index + HALO) * SIDE : (index + HALO + 1) * SIDE, :] = values
            for place, column in enumerate(columns):
                out[slot + place, :taken, :] = work[pl.ds(column, taken, stride=SIDE), :].astype(out.dtype)


def tile_kernel(
    valid, pair, cot, low, high, edges, features, context, proj_weight, conv_weight,
    pair_output, pair_grad, keep, send,
    bins, query, key, window, rows_valid, mixed, carry, mixed3, carry3, own, skew, totals,
):
    tile_rows, band_cols, channels = pair.shape
    pitch = 64
    pad = 8
    row, col = lax.axis_index(ROW), lax.axis_index("col")
    core = lax.axis_index("core")
    above, below = neighbours(edges)
    all_bins = features.shape[0]
    tail = context.shape[0]
    row_start = row * tile_rows
    col_start = row_start + col * band_cols
    total_rows = tile_rows + 2 * HALO

    def place(index, column):
        return (index + HALO) * pitch + pad + column

    bins[:MARGIN, :] = jnp.zeros((MARGIN, bins.shape[1]), bins.dtype)
    bins[MARGIN : MARGIN + all_bins, :] = features[...]
    bins[MARGIN + all_bins : MARGIN + all_bins + tail, :] = context[...]
    bins[MARGIN + all_bins + tail :, :] = jnp.zeros((bins.shape[0] - MARGIN - all_bins - tail, bins.shape[1]), bins.dtype)
    row_bins = bins[pl.ds(pl.multiple_of(row_start, 16), query.shape[0]), :]
    query[...] = jnp.dot(row_bins, proj_weight[:, :channels], preferred_element_type=F32).astype(BF16).astype(F32)
    col_bins = bins[pl.ds(pl.multiple_of(col_start, 16), key.shape[0]), :]
    key[...] = jnp.dot(col_bins, proj_weight[:, channels:], preferred_element_type=F32).astype(BF16).astype(F32)

    row_scalars = []
    for index in range(-HALO, tile_rows + HALO):
        bin_index = row_start + index
        inside = jnp.logical_and(bin_index >= 0, bin_index < all_bins)
        scalar = jnp.where(inside, valid[jnp.clip(bin_index, 0, all_bins - 1)], 0).astype(F32)
        row_scalars.append(scalar)
        rows_valid[index + HALO : index + HALO + 1, :] = jnp.full((1, channels), scalar, F32)
    rows_valid[total_rows:, :] = jnp.zeros((rows_valid.shape[0] - total_rows, channels), F32)
    for index in range(-2 * HALO, tile_rows + band_cols + 2 * HALO):
        bin_index = col_start + index
        inside = jnp.logical_and(bin_index >= 0, bin_index < all_bins + tail)
        scalar = jnp.where(inside, valid[jnp.clip(bin_index, 0, all_bins + tail - 1)], 0).astype(F32)
        window[MARGIN + index : MARGIN + index + 1, :] = jnp.full((1, channels), scalar, F32)

    def mask_of(index):
        return window[pl.ds(MARGIN + index, band_cols), :] * row_scalars[index + HALO]

    mixed[...] = jnp.zeros(mixed.shape, F32)
    carry[...] = jnp.zeros(carry.shape, F32)
    for index in range(-HALO, tile_rows + HALO):
        mask = mask_of(index)
        source = halo_row(pair, edges, index, above, below, 0, 3).astype(F32)
        value = mask * (source + query[pl.ds(MARGIN + index, 1), :] + key[pl.ds(MARGIN + index, band_cols), :])
        mixed[pl.ds(pad + place(index, 0), band_cols), :] = value
        if -1 <= index <= tile_rows:
            source = halo_row(cot, edges, index, above, below, 4, 5).astype(F32)
            carry[pl.ds(pad + place(index, 0), band_cols), :] = mask * source
    strided = rows_valid.shape[0]
    has_low = (col > 0).astype(F32)
    has_high = (col < lax.axis_size("col") - 1).astype(F32)
    for column, source, slot, has in (
        (-2, low, 0, has_low), (-1, low, 1, has_low), (band_cols, high, 0, has_high), (band_cols + 1, high, 1, has_high),
    ):
        begin = MARGIN + column - HALO
        mask = rows_valid[...] * window[pl.ds(begin, strided), :] * has
        value = source[slot, :strided].astype(F32) + query[pl.ds(MARGIN - HALO, strided), :] + key[pl.ds(begin, strided), :]
        mixed[pl.ds(pad + place(-HALO, column), strided, stride=pitch), :] = jnp.where(mask > 0.0, value, 0.0)
        if column in (-1, band_cols):
            value = jnp.where(mask > 0.0, source[2, :strided].astype(F32), 0.0)
            carry[pl.ds(pad + place(-HALO, column), strided, stride=pitch), :] = value

    span = total_rows * pitch
    block = 4 * pitch
    for start in range(0, span, block):
        for step in range(3):
            mixed3[start : start + block, step * channels : (step + 1) * channels] = mixed[
                pl.ds(pad + start + step - 1, block), :
            ].astype(BF16)

    weights = conv_weight[...].reshape(9 * channels, channels)
    per = 5
    for first in range(-1, tile_rows + 1, per):
        begin = (first + HALO) * pitch
        around = jnp.concatenate(
            [mixed3[begin + step * pitch : begin + (step + per) * pitch, :] for step in (-1, 0, 1)], axis=1
        )
        conv = jnp.dot(around, weights, preferred_element_type=F32)
        sigma = jax.nn.sigmoid(conv)
        activated = conv * sigma
        slope = sigma * (1.0 + conv * (1.0 - sigma))
        here = pl.ds(pad + begin, per * pitch)
        carry[here, :] = carry[here, :] * slope
        for index in range(max(first, 0), min(first + per, tile_rows)):
            at = (index - first) * pitch + pad
            pair_output[index] = (
                pair[index].astype(F32) + mask_of(index) * activated[at : at + band_cols, :]
            ).astype(BF16)

    for start in range(0, span, block):
        for step in range(3):
            carry3[start : start + block, step * channels : (step + 1) * channels] = carry[
                pl.ds(pad + start + 1 - step, block), :
            ].astype(BF16)
    spot = lax.broadcasted_iota(jnp.int32, (pitch, channels), 0)
    inner = jnp.logical_and(spot >= pad, spot < pad + band_cols)
    for index in range(tile_rows):
        begin = (index + HALO) * pitch
        own[index * pitch : (index + 1) * pitch, :] = jnp.where(inner, carry[pl.ds(pad + begin, pitch), :], 0.0).astype(BF16)

    totals[...] = jnp.zeros(totals.shape, F32)
    skew[...] = jnp.zeros(skew.shape, F32)
    turned = jnp.concatenate([conv_weight[tap] for tap in range(9)], axis=1)
    per = 6
    query_at = 9 * channels + all_bins + tail
    query_rows = []
    for first in range(0, tile_rows, per):
        begin = (first + HALO) * pitch
        around = jnp.concatenate(
            [carry3[begin - step * pitch : begin + (per - step) * pitch, :] for step in (-1, 0, 1)], axis=1
        )
        back = lax.dot_general(around, turned, (((1,), (1,)), ((), ())), preferred_element_type=F32)
        for index in range(first, first + per):
            at = (index - first) * pitch + pad
            masked = mask_of(index) * back[at : at + band_cols, :]
            pair_grad[index] = (cot[index].astype(F32) + masked).astype(BF16)
            query_rows.append(jnp.sum(masked, axis=0, keepdims=True))
            skew[index % 8, index - index % 8 : index - index % 8 + band_cols, :] += masked
    query_sum = jnp.concatenate(query_rows, axis=0)
    totals[pl.ds(pl.multiple_of(query_at + row_start, 16), tile_rows), :] = query_sum
    span_bins = tile_rows + band_cols
    for step in range(8):
        key_at = 9 * channels + col_start + step
        reach = span_bins - 8
        totals[pl.ds(key_at, reach), :] += skew[step, :reach, :]

    per = 12
    grads = jnp.zeros((channels, 9 * channels), F32)
    for first in range(0, tile_rows, per):
        begin = (first + HALO) * pitch
        around = jnp.concatenate(
            [mixed3[begin + step * pitch : begin + (per + step) * pitch, :] for step in (-1, 0, 1)], axis=1
        )
        grads = grads + lax.dot_general(
            own[first * pitch : (first + per) * pitch, :], around, (((0,), (0,)), ((), ())), preferred_element_type=F32
        )
    for tap in range(9):
        totals[tap * channels : (tap + 1) * channels, :] = grads[:, tap * channels : (tap + 1) * channels]
    half = keep.shape[0]
    keep[...] = totals[pl.ds(pl.multiple_of(core * half, half), half), :]
    send[...] = totals[pl.ds(pl.multiple_of((1 - core) * half, half), half), :].astype(BF16)


def finish_kernel(mine, theirs, features, context, proj_weight, feature_grad, proj_grad, conv_grad, whole):
    core = lax.axis_index("core")
    row = lax.axis_index(ROW)
    half = mine.shape[0]
    channels = mine.shape[1]
    all_bins, tail = features.shape[0], context.shape[0]
    tile_rows = feature_grad.shape[0]
    whole[pl.ds(pl.multiple_of(core * half, half), half), :] = mine[...]
    whole[pl.ds(pl.multiple_of((1 - core) * half, half), half), :] = theirs[...]
    for tap in range(9):
        conv_grad[tap] = whole[tap * channels : (tap + 1) * channels, :].astype(F32).T
    key_at = 9 * channels
    query_at = key_at + all_bins + tail
    flip = (((0,), (0,)), ((), ()))
    own = features[...]
    proj_grad[:, :channels] = lax.dot_general(own, whole[query_at : query_at + all_bins, :], flip, preferred_element_type=F32)
    proj_grad[:, channels:] = lax.dot_general(
        own, whole[key_at : key_at + all_bins, :], flip, preferred_element_type=F32
    ) + lax.dot_general(
        context[...], whole[key_at + all_bins : query_at, :], flip, preferred_element_type=F32
    )
    start = pl.multiple_of(row * tile_rows, 16)
    both = jnp.concatenate(
        [whole[pl.ds(query_at + start, tile_rows), :], whole[pl.ds(key_at + start, tile_rows), :]], axis=1
    )
    feature_grad[...] = lax.dot_general(
        both, proj_weight[...], (((1,), (1,)), ((), ())), preferred_element_type=F32
    ).astype(BF16)


def body(
    pair_input, bin_features, context_features, proj_weight, conv_weight, valid_bins, cotangent
):
    tile_rows, band_cols, channels = pair_input.shape
    row_count = lax.axis_size(ROW)
    col_count = lax.axis_size("col")
    all_bins = tile_rows * row_count
    tail = context_features.shape[0]
    chips = row_count * col_count // 2
    side_rows = -(-(tile_rows + 2 * HALO) // 16) * 16
    taken = -(-(tile_rows + 2 * HALO) // 8) * 8

    edges = jnp.concatenate(
        [pair_input[:2], pair_input[-2:], cotangent[:1], cotangent[-1:]], axis=0
    )
    edges, features = lax.all_gather((edges, bin_features), ROW, axis=0)
    features = features.reshape(all_bins, bin_features.shape[1])

    vmem = pl.BlockSpec(memory_space=pltpu.VMEM)
    low_side = pl.BlockSpec((tile_rows, SIDE, channels), lambda step: (0, 0, 0))
    high_side = pl.BlockSpec((tile_rows, SIDE, channels), lambda step: (0, band_cols // SIDE - 1, 0))
    side = jax.ShapeDtypeStruct((3, side_rows, channels), BF16)
    to_low, to_high = pl.pallas_call(
        column_kernel,
        grid=(1,),
        out_shape=(side, side),
        in_specs=[low_side, high_side, low_side, high_side, vmem],
        out_specs=(vmem, vmem),
        scratch_shapes=[pltpu.VMEM((taken * SIDE, channels), F32)],
        compiler_params=PARAMS,
        name="columns",
    )(pair_input, pair_input, cotangent, cotangent, edges)
    up = [(i, i + 1) for i in range(col_count - 1)]
    from_low = lax.ppermute(to_high, "col", up)
    from_high = lax.ppermute(to_low, "col", [(target, source) for source, target in up])

    piece = -(-(9 * channels + 2 * all_bins + tail) // (32 * chips)) * 16
    half = piece * chips
    span = (tile_rows + 2 * HALO) * 64
    near = tile_rows + band_cols + 2 * MARGIN
    pair_output, pair_grad, keep, send = pl.pallas_call(
        tile_kernel,
        out_shape=(
            jax.ShapeDtypeStruct(pair_input.shape, BF16),
            jax.ShapeDtypeStruct(pair_input.shape, BF16),
            jax.ShapeDtypeStruct((half, channels), F32),
            jax.ShapeDtypeStruct((half, channels), BF16),
        ),
        in_specs=[pl.BlockSpec(memory_space=pltpu.SMEM)] + [vmem] * 9,
        out_specs=(vmem,) * 4,
        scratch_shapes=[
            pltpu.VMEM((MARGIN + all_bins + tail + MARGIN, bin_features.shape[1]), BF16),
            pltpu.VMEM((tile_rows + 2 * MARGIN, channels), F32),
            pltpu.VMEM((near, channels), F32),
            pltpu.VMEM((near, channels), F32),
            pltpu.VMEM((taken, channels), F32),
            pltpu.VMEM((span + 64 * (taken - tile_rows), channels), F32),
            pltpu.VMEM((span + 64 * (taken - tile_rows), channels), F32),
            pltpu.VMEM((span, 3 * channels), BF16),
            pltpu.VMEM((span, 3 * channels), BF16),
            pltpu.VMEM((tile_rows * 64, channels), BF16),
            pltpu.VMEM((8, tile_rows + band_cols, channels), F32),
            pltpu.VMEM((2 * half, channels), F32),
        ],
        compiler_params=PARAMS,
        name="tile",
    )(
        valid_bins, pair_input, cotangent, from_low, from_high, edges, features, context_features,
        proj_weight, conv_weight,
    )

    swap = [(0, 1), (1, 0)]
    part = (keep + lax.ppermute(send, "core", swap).astype(F32)).astype(BF16)
    pieces = lax.all_to_all(part.reshape(chips, piece, channels), CHIPS, 0, 0)
    total = jnp.sum(pieces.astype(F32), axis=0).astype(BF16)
    mine = lax.all_to_all(
        jnp.broadcast_to(total, (chips, piece, channels)), CHIPS, 0, 0
    ).reshape(half, channels)
    theirs = lax.ppermute(mine, "core", swap)

    feature_grad, proj_grad, conv_grad = pl.pallas_call(
        finish_kernel,
        out_shape=(
            jax.ShapeDtypeStruct(bin_features.shape, BF16),
            jax.ShapeDtypeStruct(proj_weight.shape, F32),
            jax.ShapeDtypeStruct(conv_weight.shape, F32),
        ),
        in_specs=[vmem] * 5,
        out_specs=(vmem,) * 3,
        scratch_shapes=[pltpu.VMEM((2 * half, channels), BF16)],
        compiler_params=PARAMS,
        name="finish",
    )(mine, theirs, features, context_features, proj_weight)
    return (pair_output, pair_grad, feature_grad, proj_grad, conv_grad)


def solution(mesh):
    rows, cols = mesh.shape["row"], mesh.shape["col"]
    split = Mesh(mesh.devices.reshape(rows // 2, 2, cols), ("rx", "core", "col"))
    tile = P(ROW, "col", None)
    in_specs = (tile, P(ROW, None), P(), P(), P(), P(), tile)
    out_specs = (tile, tile, P(ROW, None), P(), P())
    return jax.shard_map(body, mesh=split, in_specs=in_specs, out_specs=out_specs, check_vma=False)
```

```python
import jax
import jax.numpy as jnp
from jax import lax
from jax.experimental import pallas as pl
from jax.experimental.pallas import tpu as pltpu
from jax.sharding import Mesh, PartitionSpec as P

ROW = ("rx", "core")
CHIPS = ("rx", "col")
BF16 = jnp.bfloat16
F32 = jnp.float32
HALO = 2
EDGES = 2 * HALO + 2
SIDE = 16
MARGIN = 16
PITCH = 64
PAD = 8
WIDE = pltpu.CompilerParams(vmem_limit_bytes=60 * 1024 * 1024)
PARAMS = pltpu.CompilerParams(vmem_limit_bytes=20 * 1024 * 1024)


def pack_kernel(pair, cot, features, packed, sems):
    tile_rows, channels = pair.shape[0], pair.shape[2]
    parts = [
        (pair.at[:HALO], packed.at[:HALO]),
        (pair.at[tile_rows - HALO :], packed.at[HALO : 2 * HALO]),
        (cot.at[:1], packed.at[2 * HALO : 2 * HALO + 1]),
        (cot.at[tile_rows - 1 :], packed.at[2 * HALO + 1 : EDGES]),
    ]
    for part in range(features.shape[1] // channels):
        parts.append((features.at[:, part * channels : (part + 1) * channels], packed.at[EDGES + part]))
    copies = [pltpu.make_async_copy(source, target, sems.at[i]) for i, (source, target) in enumerate(parts)]
    for copy in copies:
        copy.start()
    for copy in copies:
        copy.wait()


def column_kernel(one, other, pair_low, pair_high, cot_low, cot_high, near, to_even, to_odd, work, sides):
    tile_rows, _, channels = pair_low.shape
    band_cols = one.shape[1]
    odd_row = lax.rem(lax.axis_index(ROW), 2)
    near[1 - odd_row] = one[:EDGES]
    near[odd_row] = other[:EDGES]
    rows = tile_rows + 2 * HALO
    taken = work.shape[0] // SIDE
    work[rows * SIDE :, :] = jnp.zeros((work.shape[0] - rows * SIDE, channels), F32)
    for side, pair, cot, start, picks in (
        (0, pair_low, cot_low, 0, (0, 1)),
        (1, pair_high, cot_high, band_cols - SIDE, (SIDE - 2, SIDE - 1)),
    ):
        sides[side, :, taken:, :] = jnp.zeros((3, sides.shape[2] - taken, channels), BF16)
        for tile, first, last, columns, slot in (
            (pair, 0, 3, picks, 0),
            (cot, 4, 5, (picks[side],), 2),
        ):
            depth = HALO if slot == 0 else 1
            for index in range(-HALO, tile_rows + HALO):
                if index < -depth or index >= tile_rows + depth:
                    values = jnp.zeros((SIDE, channels), F32)
                elif 0 <= index < tile_rows:
                    values = tile[index].astype(F32)
                elif index < 0:
                    values = near[0, last + 1 + index, start : start + SIDE].astype(F32)
                else:
                    values = near[1, first + index - tile_rows, start : start + SIDE].astype(F32)
                work[(index + HALO) * SIDE : (index + HALO + 1) * SIDE, :] = values
            for position, column in enumerate(columns):
                sides[side, slot + position, :taken, :] = work[pl.ds(column, taken, stride=SIDE), :].astype(BF16)
    odd_col = lax.rem(lax.axis_index("col"), 2)
    to_even[...] = sides[1 - odd_col]
    to_odd[...] = sides[odd_col]


def prepare_kernel(
    valid, context, proj_weight, conv_weight, *refs
):
    sources, (features, query, key, window, rows_valid, forward, backward, bins) = refs[:-8], refs[-8:]
    channels = query.shape[1]
    all_bins, tail = features.shape[0], context.shape[0]
    row, col = lax.axis_index(ROW), lax.axis_index("col")
    if len(sources) == 1:
        blocks = [(sources[0].at[index], index) for index in range(sources[0].shape[0])]
    else:
        blocks = [(source, lax.bitwise_xor(row, step)) for source, step in zip(sources, (0, 1, 3, 2))]
    tile_rows = sources[0].shape[-2]
    row_start = row * tile_rows
    col_start = row_start + col * (key.shape[0] - 2 * MARGIN - tile_rows)
    bins[:MARGIN, :] = jnp.zeros((MARGIN, bins.shape[1]), BF16)
    for source, index in blocks:
        start = pl.multiple_of(MARGIN + index * tile_rows, 16)
        for part in range(bins.shape[1] // channels):
            bins[pl.ds(start, tile_rows), part * channels : (part + 1) * channels] = source[EDGES + part]
    bins[MARGIN + all_bins : MARGIN + all_bins + tail, :] = context[...]
    bins[MARGIN + all_bins + tail :, :] = jnp.zeros((MARGIN, bins.shape[1]), BF16)
    features[...] = bins[MARGIN : MARGIN + all_bins, :]
    row_bins = bins[pl.ds(pl.multiple_of(row_start, 16), query.shape[0]), :]
    query[...] = jnp.dot(row_bins, proj_weight[:, :channels], preferred_element_type=F32).astype(BF16).astype(F32)
    col_bins = bins[pl.ds(pl.multiple_of(col_start, 16), key.shape[0]), :]
    key[...] = jnp.dot(col_bins, proj_weight[:, channels:], preferred_element_type=F32).astype(BF16).astype(F32)

    flags = jnp.broadcast_to(valid[...].astype(F32).astype(BF16), (channels, all_bins + tail))
    flip = (((1,), (1,)), ((), ()))
    for target, begin, stop in ((window, col_start - MARGIN, all_bins + tail), (rows_valid, row_start - HALO, all_bins)):
        shape = (target.shape[0], all_bins + tail)
        bin_index = lax.broadcasted_iota(jnp.int32, shape, 1)
        chosen = jnp.logical_and(bin_index == lax.broadcasted_iota(jnp.int32, shape, 0) + begin, bin_index < stop)
        target[...] = lax.dot_general(chosen.astype(F32).astype(BF16), flags, flip, preferred_element_type=F32)

    forward[...] = jnp.zeros(forward.shape, BF16)
    backward[...] = jnp.zeros(backward.shape, BF16)
    for tap in range(9):
        row_step, step = tap // 3 - 1, tap % 3
        values = conv_weight[tap]
        turned = values.astype(F32).T.astype(BF16)
        for out in range(2):
            lanes = slice(out * channels, (out + 1) * channels)
            at = ((row_step + 1 + out) * 3 + step) * channels
            forward[at : at + channels, lanes] = values
            at = ((1 - row_step + out) * 3 + step) * channels
            backward[at : at + channels, lanes] = turned


def tile_kernel(
    pair, cot, from_even, from_odd, near, query, key, window, rows_valid, forward, backward,
    pair_output, pair_grad, keep, send,
    sides, mixed, carry, mixed3, carry3, own, skew, totals, output, grad, sems,
):
    tile_rows, band_cols, channels = pair.shape
    row, col = lax.axis_index(ROW), lax.axis_index("col")
    core = lax.axis_index("core")
    all_bins = lax.axis_size(ROW) * tile_rows
    tail = lax.axis_size("col") * band_cols
    row_start = row * tile_rows
    col_start = row_start + col * band_cols
    total_rows = tile_rows + 2 * HALO
    odd_col = lax.rem(col, 2)
    sides[1 - odd_col] = from_even[...]
    sides[odd_col] = from_odd[...]

    def place(index, column):
        return (index + HALO) * PITCH + PAD + column

    def mask_of(index):
        return window[pl.ds(MARGIN + index, band_cols), :] * rows_valid[pl.ds(index + HALO, 1), :]

    def halo_row(tile, index, first, last):
        if index < 0:
            return near[0, last + 1 + index]
        if index >= tile_rows:
            return near[1, first + index - tile_rows]
        return tile[index]

    rest = PITCH - band_cols - PAD
    gap = jnp.zeros((PAD + rest, channels), F32)
    for array in (mixed, carry):
        array[: 2 * PAD, :] = jnp.zeros((2 * PAD, channels), F32)
        for index in range(total_rows):
            begin = PAD + index * PITCH + PAD + band_cols
            array[begin : begin + PAD + rest, :] = gap
    empty = jnp.zeros((band_cols, channels), F32)
    carry[pl.ds(PAD + place(-HALO, 0), band_cols), :] = empty
    carry[pl.ds(PAD + place(tile_rows + 1, 0), band_cols), :] = empty
    for index in range(-HALO, tile_rows + HALO):
        mask = mask_of(index)
        source = halo_row(pair, index, 0, 3).astype(F32)
        value = mask * (source + query[pl.ds(MARGIN + index, 1), :] + key[pl.ds(MARGIN + index, band_cols), :])
        mixed[pl.ds(PAD + place(index, 0), band_cols), :] = value
        if -1 <= index <= tile_rows:
            source = halo_row(cot, index, 4, 5).astype(F32)
            carry[pl.ds(PAD + place(index, 0), band_cols), :] = mask * source
    strided = rows_valid.shape[0]
    has_low = (col > 0).astype(F32)
    has_high = (col < lax.axis_size("col") - 1).astype(F32)
    for column, side, slot, has in (
        (-2, 0, 0, has_low), (-1, 0, 1, has_low), (band_cols, 1, 0, has_high), (band_cols + 1, 1, 1, has_high),
    ):
        begin = MARGIN + column - HALO
        mask = rows_valid[...] * window[pl.ds(begin, strided), :] * has
        value = sides[side, slot, :strided].astype(F32) + query[pl.ds(MARGIN - HALO, strided), :] + key[pl.ds(begin, strided), :]
        mixed[pl.ds(PAD + place(-HALO, column), strided, stride=PITCH), :] = mask * value
        if column in (-1, band_cols):
            value = mask * sides[side, 2, :strided].astype(F32)
            carry[pl.ds(PAD + place(-HALO, column), strided, stride=PITCH), :] = value

    def spread(source, target, first, last, sign):
        for index in range(first, last):
            start = (index + HALO) * PITCH
            for step in range(3):
                target[start : start + PITCH, step * channels : (step + 1) * channels] = source[
                    pl.ds(PAD + start + sign * (step - 1), PITCH), :
                ].astype(BF16)

    def four_rows(source, first, pairs):
        columns = []
        for step in range(4):
            starts = [(first + 2 * index + step - 1 + HALO) * PITCH for index in range(pairs)]
            columns.append(jnp.concatenate([source[start : start + PITCH, :] for start in starts], axis=0))
        return jnp.concatenate(columns, axis=1)

    spread(mixed, mixed3, -HALO, tile_rows + HALO, 1)

    pairs = 5
    for first in range(-1, tile_rows + 1, 2 * pairs):
        conv = jnp.dot(four_rows(mixed3, first, pairs), forward[...], preferred_element_type=F32)
        sigma = jax.nn.sigmoid(conv)
        activated = conv * sigma
        slope = sigma * (1.0 + conv * (1.0 - sigma))
        for offset in range(2 * pairs):
            index = first + offset
            lanes = slice(offset % 2 * channels, (offset % 2 + 1) * channels)
            at = offset // 2 * PITCH
            here = pl.ds(PAD + (index + HALO) * PITCH, PITCH)
            carry[here, :] = carry[here, :] * slope[at : at + PITCH, lanes]
            if 0 <= index < tile_rows:
                output[index] = (
                    pair[index].astype(F32) + mask_of(index) * activated[at + PAD : at + PAD + band_cols, lanes]
                ).astype(BF16)
    write_output = pltpu.make_async_copy(output, pair_output, sems.at[0])
    write_output.start()

    spread(carry, carry3, -1, tile_rows + 1, -1)
    spot = lax.broadcasted_iota(jnp.int32, (PITCH, channels), 0)
    inner = jnp.logical_and(spot >= PAD, spot < PAD + band_cols)
    for index in range(tile_rows):
        begin = (index + HALO) * PITCH
        own[index * PITCH : (index + 1) * PITCH, :] = jnp.where(inner, carry[pl.ds(PAD + begin, PITCH), :], 0.0).astype(BF16)

    totals[...] = jnp.zeros(totals.shape, F32)
    skew[...] = jnp.zeros(skew.shape, F32)
    pairs = 4
    query_at = 9 * channels + all_bins + tail
    query_rows = []
    for first in range(0, tile_rows, 2 * pairs):
        back = jnp.dot(four_rows(carry3, first, pairs), backward[...], preferred_element_type=F32)
        for offset in range(2 * pairs):
            index = first + offset
            lanes = slice(offset % 2 * channels, (offset % 2 + 1) * channels)
            at = offset // 2 * PITCH + PAD
            masked = mask_of(index) * back[at : at + band_cols, lanes]
            grad[index] = (cot[index].astype(F32) + masked).astype(BF16)
            query_rows.append(jnp.sum(masked, axis=0, keepdims=True))
            skew[index % 8, index - index % 8 : index - index % 8 + band_cols, :] += masked
    write_grad = pltpu.make_async_copy(grad, pair_grad, sems.at[1])
    write_grad.start()
    totals[pl.ds(pl.multiple_of(query_at + row_start, 16), tile_rows), :] = jnp.concatenate(query_rows, axis=0)
    reach = tile_rows + band_cols - 8
    for step in range(8):
        totals[pl.ds(9 * channels + col_start + step, reach), :] += skew[step, :reach, :]

    per = 12
    grads = jnp.zeros((channels, 9 * channels), F32)
    for first in range(0, tile_rows, per):
        begin = (first + HALO) * PITCH
        around = jnp.concatenate(
            [mixed3[begin + step * PITCH : begin + (per + step) * PITCH, :] for step in (-1, 0, 1)], axis=1
        )
        grads = grads + lax.dot_general(
            own[first * PITCH : (first + per) * PITCH, :], around, (((0,), (0,)), ((), ())), preferred_element_type=F32
        )
    for tap in range(9):
        totals[tap * channels : (tap + 1) * channels, :] = grads[:, tap * channels : (tap + 1) * channels]
    half = keep.shape[0]
    keep[...] = totals[pl.ds(pl.multiple_of(core * half, half), half), :]
    send[...] = totals[pl.ds(pl.multiple_of((1 - core) * half, half), half), :].astype(BF16)
    write_output.wait()
    write_grad.wait()


def add_kernel(pieces, copies):
    total = pieces[0].astype(F32)
    for index in range(1, pieces.shape[0]):
        total = total + pieces[index].astype(F32)
    copies[...] = jnp.broadcast_to(total.astype(BF16), copies.shape)


def finish_kernel(mine, theirs, features, context, proj_weight, feature_grad, proj_grad, conv_grad, whole):
    core = lax.axis_index("core")
    row = lax.axis_index(ROW)
    half = mine.shape[0]
    channels = mine.shape[1]
    all_bins, tail = features.shape[0], context.shape[0]
    tile_rows = feature_grad.shape[0]
    whole[pl.ds(pl.multiple_of(core * half, half), half), :] = mine[...]
    whole[pl.ds(pl.multiple_of((1 - core) * half, half), half), :] = theirs[...]
    for tap in range(9):
        conv_grad[tap] = whole[tap * channels : (tap + 1) * channels, :].astype(F32).T
    key_at = 9 * channels
    query_at = key_at + all_bins + tail
    flip = (((0,), (0,)), ((), ()))
    own = features[...]
    proj_grad[:, :channels] = lax.dot_general(own, whole[query_at : query_at + all_bins, :], flip, preferred_element_type=F32)
    proj_grad[:, channels:] = lax.dot_general(
        own, whole[key_at : key_at + all_bins, :], flip, preferred_element_type=F32
    ) + lax.dot_general(
        context[...], whole[key_at + all_bins : query_at, :], flip, preferred_element_type=F32
    )
    start = pl.multiple_of(row * tile_rows, 16)
    both = jnp.concatenate(
        [whole[pl.ds(query_at + start, tile_rows), :], whole[pl.ds(key_at + start, tile_rows), :]], axis=1
    )
    feature_grad[...] = lax.dot_general(
        both, proj_weight[...], (((1,), (1,)), ((), ())), preferred_element_type=F32
    ).astype(BF16)


def body(
    pair_input, bin_features, context_features, proj_weight, conv_weight, valid_bins, cotangent
):
    tile_rows, band_cols, channels = pair_input.shape
    width = bin_features.shape[1]
    row_count = lax.axis_size(ROW)
    col_count = lax.axis_size("col")
    all_bins = tile_rows * row_count
    tail = context_features.shape[0]
    chips = row_count * col_count // 2
    side_rows = -(-(tile_rows + 2 * HALO) // 16) * 16
    taken = -(-(tile_rows + 2 * HALO) // 8) * 8
    vmem = pl.BlockSpec(memory_space=pltpu.VMEM)
    anywhere = pl.BlockSpec(memory_space=pl.ANY)

    def shape(*dims, dtype=BF16):
        return jax.ShapeDtypeStruct(dims, dtype)

    layers = EDGES + width // channels
    packed = pl.pallas_call(
        pack_kernel,
        out_shape=shape(layers, tile_rows, channels),
        in_specs=[anywhere] * 3,
        out_specs=vmem,
        scratch_shapes=[pltpu.SemaphoreType.DMA((layers,))],
        compiler_params=WIDE,
        name="pack",
    )(pair_input, cotangent, bin_features)
    other_core = [(0, 1), (1, 0)]
    if row_count == 4:
        one = lax.ppermute(packed, "core", other_core)
        other = lax.ppermute(packed, ROW, [(index, index ^ 3) for index in range(4)])
        sources = [packed, one, other, lax.ppermute(other, "core", other_core)]
    else:
        gathered = lax.all_gather(packed, ROW, axis=0)
        row = lax.axis_index(ROW)
        around = [
            lax.dynamic_index_in_dim(gathered, jnp.clip(index, 0, row_count - 1), 0, keepdims=False)
            for index in (row - 1, row + 1)
        ]
        odd = row % 2 == 1
        one = jnp.where(odd, around[0], around[1])
        other = jnp.where(odd, around[1], around[0])
        sources = [gathered]

    low_side = pl.BlockSpec((tile_rows, SIDE, channels), lambda step: (0, 0, 0))
    high_side = pl.BlockSpec((tile_rows, SIDE, channels), lambda step: (0, band_cols // SIDE - 1, 0))
    side = shape(3, side_rows, channels)
    near, to_even, to_odd = pl.pallas_call(
        column_kernel,
        grid=(1,),
        out_shape=(shape(2, EDGES, tile_rows, channels), side, side),
        in_specs=[vmem, vmem, low_side, high_side, low_side, high_side],
        out_specs=(vmem,) * 3,
        scratch_shapes=[pltpu.VMEM((taken * SIDE, channels), F32), pltpu.VMEM((2, 3, side_rows, channels), BF16)],
        compiler_params=PARAMS,
        name="columns",
    )(one, other, pair_input, pair_input, cotangent, cotangent)
    even_pairs = [(i, i ^ 1) for i in range(col_count) if i ^ 1 < col_count]
    odd_pairs = [(i, ((i + 1) ^ 1) - 1) for i in range(1, col_count) if ((i + 1) ^ 1) - 1 < col_count]
    from_even = lax.ppermute(to_even, "col", even_pairs)
    from_odd = lax.ppermute(to_odd, "col", odd_pairs)

    near_bins = tile_rows + band_cols + 2 * MARGIN
    features, query, key, window, rows_valid, forward, backward = pl.pallas_call(
        prepare_kernel,
        out_shape=(
            shape(all_bins, width),
            shape(tile_rows + 2 * MARGIN, channels, dtype=F32),
            shape(near_bins, channels, dtype=F32),
            shape(near_bins, channels, dtype=F32),
            shape(taken, channels, dtype=F32),
            shape(12 * channels, 2 * channels),
            shape(12 * channels, 2 * channels),
        ),
        in_specs=[vmem] * (4 + len(sources)),
        out_specs=(vmem,) * 7,
        scratch_shapes=[pltpu.VMEM((MARGIN + all_bins + tail + MARGIN, width), BF16)],
        compiler_params=PARAMS,
        name="prepare",
    )(valid_bins.reshape(1, all_bins + tail), context_features, proj_weight, conv_weight, *sources)

    piece = -(-(9 * channels + 2 * all_bins + tail) // (32 * chips)) * 16
    half = piece * chips
    span = (tile_rows + 2 * HALO) * PITCH
    loose = span + PITCH * (taken - tile_rows)
    pair_output, pair_grad, keep, send = pl.pallas_call(
        tile_kernel,
        out_shape=(
            shape(*pair_input.shape),
            shape(*pair_input.shape),
            shape(half, channels, dtype=F32),
            shape(half, channels),
        ),
        in_specs=[vmem] * 11,
        out_specs=(anywhere, anywhere, vmem, vmem),
        scratch_shapes=[
            pltpu.VMEM((2, 3, side_rows, channels), BF16),
            pltpu.VMEM((loose, channels), F32),
            pltpu.VMEM((loose, channels), F32),
            pltpu.VMEM((span, 3 * channels), BF16),
            pltpu.VMEM((span, 3 * channels), BF16),
            pltpu.VMEM((tile_rows * PITCH, channels), BF16),
            pltpu.VMEM((8, tile_rows + band_cols, channels), F32),
            pltpu.VMEM((2 * half, channels), F32),
            pltpu.VMEM(pair_input.shape, BF16),
            pltpu.VMEM(pair_input.shape, BF16),
            pltpu.SemaphoreType.DMA((2,)),
        ],
        compiler_params=PARAMS,
        name="tile",
    )(pair_input, cotangent, from_even, from_odd, near, query, key, window, rows_valid, forward, backward)

    part = (keep + lax.ppermute(send, "core", other_core).astype(F32)).astype(BF16)
    pieces = lax.all_to_all(part.reshape(chips, piece, channels), CHIPS, 0, 0)
    copies = pl.pallas_call(
        add_kernel,
        out_shape=shape(chips, piece, channels),
        in_specs=[vmem],
        out_specs=vmem,
        compiler_params=PARAMS,
        name="add",
    )(pieces)
    mine = lax.all_to_all(copies, CHIPS, 0, 0).reshape(half, channels)
    theirs = lax.ppermute(mine, "core", other_core)

    feature_grad, proj_grad, conv_grad = pl.pallas_call(
        finish_kernel,
        out_shape=(
            shape(*bin_features.shape),
            shape(*proj_weight.shape, dtype=F32),
            shape(*conv_weight.shape, dtype=F32),
        ),
        in_specs=[vmem] * 5,
        out_specs=(vmem,) * 3,
        scratch_shapes=[pltpu.VMEM((2 * half, channels), BF16)],
        compiler_params=PARAMS,
        name="finish",
    )(mine, theirs, features, context_features, proj_weight)
    return (pair_output, pair_grad, feature_grad, proj_grad, conv_grad)


def solution(mesh):
    rows, cols = mesh.shape["row"], mesh.shape["col"]
    split = Mesh(mesh.devices.reshape(rows // 2, 2, cols), ("rx", "core", "col"))
    tile = P(ROW, "col", None)
    in_specs = (tile, P(ROW, None), P(), P(), P(), P(), tile)
    out_specs = (tile, tile, P(ROW, None), P(), P())
    return jax.shard_map(body, mesh=split, in_specs=in_specs, out_specs=out_specs, check_vma=False)
```

```python
import jax
import jax.numpy as jnp
from jax import lax
from jax.experimental import pallas as pl
from jax.experimental.pallas import tpu as pltpu
from jax.sharding import Mesh, PartitionSpec as P

ROW = ("rx", "core")
CHIPS = ("rx", "col")
BF16 = jnp.bfloat16
F32 = jnp.float32
HALO = 2
EDGES = HALO + 1
SIDE = 16
MARGIN = 16
PITCH = 64
PAD = 8
PARAMS = pltpu.CompilerParams(vmem_limit_bytes=20 * 1024 * 1024)


def pack_kernel(
    pair, cot, features, to_core, to_chip, to_even, to_odd, pair_low, pair_high, cot_low, cot_high, work, sides, sems
):
    tile_rows, band_cols, channels = pair.shape
    odd_row = lax.rem(lax.axis_index(ROW), 2)
    odd_col = lax.rem(lax.axis_index("col"), 2)
    parts = []
    for target, at_end in ((to_chip, odd_row), (to_core, 1 - odd_row)):
        parts.append((pair.at[pl.ds(at_end * (tile_rows - HALO), HALO)], target.at[:HALO]))
        parts.append((cot.at[pl.ds(at_end * (tile_rows - 1), 1)], target.at[HALO:EDGES]))
        for part in range(features.shape[1] // channels):
            parts.append((features.at[:, part * channels : (part + 1) * channels], target.at[EDGES + part]))
    parts.append((pair.at[:, :SIDE], pair_low))
    parts.append((pair.at[:, band_cols - SIDE :], pair_high))
    parts.append((cot.at[:, :SIDE], cot_low))
    parts.append((cot.at[:, band_cols - SIDE :], cot_high))
    copies = [pltpu.make_async_copy(source, target, sems.at[i]) for i, (source, target) in enumerate(parts)]
    for copy in copies[-4:] + copies[:-4]:
        copy.start()
    for copy in copies[-4:]:
        copy.wait()
    for side, (chunk, kind) in enumerate(((pair_low, cot_low), (pair_high, cot_high))):
        for slot, source, column in (
            (0, chunk, side * (SIDE - 2)), (1, chunk, side * (SIDE - 2) + 1), (2, kind, side * (SIDE - 1)),
        ):
            if slot != 1:
                work[...] = source[...].astype(F32).reshape(tile_rows * SIDE, channels)
            sides[side, slot] = work[pl.ds(column, tile_rows, stride=SIDE), :].astype(BF16)
    to_even[...] = sides[1 - odd_col]
    to_odd[...] = sides[odd_col]
    for copy in copies[:-4]:
        copy.wait()


def corner_kernel(from_even, from_odd, sides, to_core, to_chip):
    tile_rows = from_even.shape[1]
    odd_row = lax.rem(lax.axis_index(ROW), 2)
    odd_col = lax.rem(lax.axis_index("col"), 2)
    sides[1 - odd_col] = from_even[...]
    sides[odd_col] = from_odd[...]
    for target, at_end in ((to_chip, odd_row), (to_core, 1 - odd_row)):
        start = pl.multiple_of(at_end * (tile_rows - SIDE), 16)
        target[...] = sides[:, :, pl.ds(start, SIDE), :]


def weights_kernel(
    valid, context, proj_weight, conv_weight,
    window, rows_valid, forward, backward, projection, context_key, context_turned,
):
    channels = window.shape[1]
    bins = valid.shape[0]
    band_total = context.shape[0]
    all_bins = bins - band_total
    tile_rows = all_bins // lax.axis_size(ROW)
    row_start = lax.axis_index(ROW) * tile_rows
    col_start = row_start + lax.axis_index("col") * (band_total // lax.axis_size("col"))
    flags = jnp.broadcast_to(valid[...].reshape(1, bins).astype(F32).astype(BF16), (channels, bins))
    flip = (((1,), (1,)), ((), ()))
    for target, begin, stop in ((window, col_start - MARGIN, bins), (rows_valid, row_start - HALO, all_bins)):
        shape = (target.shape[0], bins)
        bin_index = lax.broadcasted_iota(jnp.int32, shape, 1)
        chosen = jnp.logical_and(bin_index == lax.broadcasted_iota(jnp.int32, shape, 0) + begin, bin_index < stop)
        target[...] = lax.dot_general(chosen.astype(F32).astype(BF16), flags, flip, preferred_element_type=F32)
    forward[...] = jnp.zeros(forward.shape, BF16)
    backward[...] = jnp.zeros(backward.shape, BF16)
    for tap in range(9):
        row_step, step = tap // 3 - 1, tap % 3
        values = conv_weight[tap]
        turned = values.astype(F32).T.astype(BF16)
        for out in range(2):
            lanes = slice(out * channels, (out + 1) * channels)
            at = ((row_step + 1 + out) * 3 + step) * channels
            forward[at : at + channels, lanes] = values
            at = ((1 - row_step + out) * 3 + step) * channels
            backward[at : at + channels, lanes] = turned
    projection[...] = proj_weight[...]
    context_key[...] = jnp.dot(context[...], proj_weight[:, channels:], preferred_element_type=F32).astype(BF16)
    context_turned[...] = context[...].astype(F32).T.astype(BF16)


def prepare_kernel(projection, context_key, *refs):
    sources, (features_turned, query, key, features, query_rows, key_rows) = refs[:-6], refs[-6:]
    channels = query.shape[1]
    all_bins, tail = features.shape[0], context_key.shape[0]
    row, col = lax.axis_index(ROW), lax.axis_index("col")
    if len(sources) == 1:
        features[...] = sources[0][...]
    else:
        for source, step in zip(sources, (0, 1, 3, 2)):
            rows = source.shape[1]
            start = pl.multiple_of(lax.bitwise_xor(row, step) * rows, 16)
            for part in range(source.shape[0] - EDGES):
                features[pl.ds(start, rows), part * channels : (part + 1) * channels] = source[EDGES + part]
    tile_rows = query.shape[0] - 2 * MARGIN
    row_start = row * tile_rows
    col_start = row_start + col * (key.shape[0] - 2 * MARGIN - tile_rows)
    proj = jnp.dot(features[...], projection[...], preferred_element_type=F32).astype(BF16).astype(F32)
    margin = jnp.zeros((MARGIN, channels), F32)
    for target, size in ((query_rows, all_bins), (key_rows, all_bins + tail)):
        target[:MARGIN, :] = margin
        target[MARGIN + size :, :] = margin
    query_rows[MARGIN : MARGIN + all_bins, :] = proj[:, :channels]
    key_rows[MARGIN : MARGIN + all_bins, :] = proj[:, channels:]
    key_rows[MARGIN + all_bins : MARGIN + all_bins + tail, :] = context_key[...].astype(F32)
    query[...] = query_rows[pl.ds(pl.multiple_of(row_start, 16), query.shape[0]), :]
    key[...] = key_rows[pl.ds(pl.multiple_of(col_start, 16), key.shape[0]), :]
    features_turned[...] = features[...].astype(F32).T.astype(BF16)


def spread(source, target, first, last, base, sign):
    channels = source.shape[1]
    for index in range(first, last):
        start = (index - base) * PITCH
        for step in range(3):
            target[start : start + PITCH, step * channels : (step + 1) * channels] = source[
                pl.ds(PAD + start + sign * (step - 1), PITCH), :
            ].astype(BF16)


def rows_of(sources, index):
    for array, base, held in sources:
        if index in held:
            return array[(index - base) * PITCH : (index - base + 1) * PITCH, :]
    raise IndexError(index)


def four_rows(sources, first, pairs):
    columns = []
    for step in range(4):
        parts = [rows_of(sources, first + 2 * index + step - 1) for index in range(pairs)]
        columns.append(jnp.concatenate(parts, axis=0))
    return jnp.concatenate(columns, axis=1)


def silu_parts(conv):
    sigma = jax.nn.sigmoid(conv)
    return conv * sigma, sigma * (1.0 + conv * (1.0 - sigma))


def has_sides():
    col = lax.axis_index("col")
    return (col > 0).astype(F32), (col < lax.axis_size("col") - 1).astype(F32)


def keep_inner(values, band_cols):
    spot = lax.broadcasted_iota(jnp.int32, values.shape, 0)
    inner = jnp.logical_and(spot >= PAD, spot < PAD + band_cols)
    return jnp.where(inner, values, 0.0).astype(BF16)


def inner_kernel(
    pair, cot, sides, query, key, window, rows_valid, forward,
    mixed3, carry3, own, output,
    mixed, carry,
):
    tile_rows, band_cols, channels = pair.shape

    def place(index, column):
        return PAD + index * PITCH + PAD + column

    def mask_of(index):
        return window[pl.ds(MARGIN + index, band_cols), :] * rows_valid[pl.ds(index + HALO, 1), :]

    gap = jnp.zeros((PITCH - band_cols, channels), F32)
    mixed[:PAD, :] = jnp.zeros((PAD, channels), F32)
    mixed[PAD : 2 * PAD, :] = jnp.zeros((PAD, channels), F32)
    for index in range(tile_rows):
        mixed[pl.ds(place(index, band_cols), PITCH - band_cols), :] = gap
        carry[pl.ds(place(index, band_cols), PITCH - band_cols), :] = gap
    for index in range(tile_rows):
        mask = mask_of(index)
        value = mask * (
            pair[index].astype(F32) + query[pl.ds(MARGIN + index, 1), :] + key[pl.ds(MARGIN + index, band_cols), :]
        )
        mixed[pl.ds(place(index, 0), band_cols), :] = value
        carry[pl.ds(place(index, 0), band_cols), :] = mask * cot[index].astype(F32)
    has_low, has_high = has_sides()
    for column, side, slot, has in (
        (-2, 0, 0, has_low), (-1, 0, 1, has_low), (band_cols, 1, 0, has_high), (band_cols + 1, 1, 1, has_high),
    ):
        begin = MARGIN + column
        mask = rows_valid[pl.ds(HALO, tile_rows), :] * window[pl.ds(begin, tile_rows), :] * has
        value = sides[side, slot].astype(F32) + query[pl.ds(MARGIN, tile_rows), :] + key[pl.ds(begin, tile_rows), :]
        mixed[pl.ds(place(0, column), tile_rows, stride=PITCH), :] = mask * value
        if column in (-1, band_cols):
            carry[pl.ds(place(0, column), tile_rows, stride=PITCH), :] = mask * sides[side, HALO].astype(F32)
    spread(mixed, mixed3, 0, tile_rows, 0, 1)

    first, last = 1, tile_rows - 1
    sources = [(mixed3, 0, range(tile_rows))]
    while first < last:
        pairs = min(5, (last - first) // 2)
        conv = jnp.dot(four_rows(sources, first, pairs), forward[...], preferred_element_type=F32)
        activated, slope = silu_parts(conv)
        for offset in range(2 * pairs):
            index = first + offset
            lanes = slice(offset % 2 * channels, (offset % 2 + 1) * channels)
            at = offset // 2 * PITCH
            here = pl.ds(PAD + index * PITCH, PITCH)
            values = carry[here, :] * slope[at : at + PITCH, lanes]
            carry[here, :] = values
            own[index * PITCH : (index + 1) * PITCH, :] = keep_inner(values, band_cols)
            output[index] = (
                pair[index].astype(F32) + mask_of(index) * activated[at + PAD : at + PAD + band_cols, lanes]
            ).astype(BF16)
        first += 2 * pairs
    spread(carry, carry3, 1, tile_rows - 1, 0, -1)


def outer_kernel(
    pair, cot, from_core, from_chip, sides, corner_core, corner_chip, query, key, window, rows_valid, forward, backward,
    mixed3, carry3, own, output,
    pair_output, pair_grad, keep, send,
    near, corners, mixed, carry, mixed3_ends, carry3_ends, own_ends, output_ends, skew, totals, grad, sems,
):
    tile_rows, band_cols, channels = pair.shape
    row, col = lax.axis_index(ROW), lax.axis_index("col")
    core = lax.axis_index("core")
    all_bins = lax.axis_size(ROW) * tile_rows
    tail = lax.axis_size("col") * band_cols
    row_start = row * tile_rows
    col_start = row_start + col * band_cols
    odd_row = lax.rem(row, 2)
    last = tile_rows - 1
    write_output = pltpu.make_async_copy(output.at[1:last], pair_output.at[1:last], sems.at[0])
    write_output.start()
    near[1 - odd_row] = from_core[:EDGES]
    near[odd_row] = from_chip[:EDGES]
    corners[1 - odd_row] = corner_core[...]
    corners[odd_row] = corner_chip[...]

    def place(position, column):
        return PAD + position * PITCH + PAD + column

    def mask_of(index):
        return window[pl.ds(MARGIN + index, band_cols), :] * rows_valid[pl.ds(index + HALO, 1), :]

    has = has_sides()
    mixed_rows = (-2, -1, tile_rows, tile_rows + 1)
    carry_rows = (-1, 0, last, tile_rows)
    gap = jnp.zeros((PITCH - band_cols, channels), F32)
    for array in (mixed, carry):
        array[: 2 * PAD, :] = jnp.zeros((2 * PAD, channels), F32)
        for position in range(4):
            array[pl.ds(place(position, band_cols), PITCH - band_cols), :] = gap

    def corner_of(index, side, slot):
        if index < 0:
            return corners[0, side, slot].astype(F32)[SIDE + index : SIDE + index + 1, :]
        return corners[1, side, slot].astype(F32)[index - tile_rows : index - tile_rows + 1, :]

    def pixel_mask(index, column, side):
        return rows_valid[pl.ds(index + HALO, 1), :] * window[pl.ds(MARGIN + index + column, 1), :] * has[side]

    for position, index in enumerate(mixed_rows):
        source = near[0, HALO + index] if index < 0 else near[1, index - tile_rows]
        row_query = query[pl.ds(MARGIN + index, 1), :]
        mixed[pl.ds(place(position, 0), band_cols), :] = mask_of(index) * (
            source.astype(F32) + row_query + key[pl.ds(MARGIN + index, band_cols), :]
        )
        for column, side, slot in ((-2, 0, 0), (-1, 0, 1), (band_cols, 1, 0), (band_cols + 1, 1, 1)):
            value = corner_of(index, side, slot) + row_query + key[pl.ds(MARGIN + index + column, 1), :]
            mixed[pl.ds(place(position, column), 1), :] = pixel_mask(index, column, side) * value
    for position, index in enumerate(carry_rows):
        source = near[0, HALO] if index < 0 else near[1, HALO] if index > last else cot[index]
        carry[pl.ds(place(position, 0), band_cols), :] = mask_of(index) * source.astype(F32)
        for column, side in ((-1, 0), (band_cols, 1)):
            if 0 <= index <= last:
                chunk = index // SIDE * SIDE
                value = sides[side, HALO, chunk : chunk + SIDE].astype(F32)[index - chunk : index - chunk + 1, :]
            else:
                value = corner_of(index, side, HALO)
            carry[pl.ds(place(position, column), 1), :] = pixel_mask(index, column, side) * value
    spread(mixed, mixed3_ends, 0, 4, 0, 1)
    mixed_sources = [
        (mixed3, 0, range(tile_rows)), (mixed3_ends, -2, (-2, -1)), (mixed3_ends, tile_rows - 2, (tile_rows, tile_rows + 1)),
    ]
    ends = jnp.concatenate([four_rows(mixed_sources, -1, 1), four_rows(mixed_sources, last, 1)], axis=0)
    activated, slope = silu_parts(jnp.dot(ends, forward[...], preferred_element_type=F32))
    for position, index in enumerate(carry_rows):
        lanes = slice(position % 2 * channels, (position % 2 + 1) * channels)
        at = position // 2 * PITCH
        here = pl.ds(PAD + position * PITCH, PITCH)
        values = carry[here, :] * slope[at : at + PITCH, lanes]
        carry[here, :] = values
        if 0 <= index <= last:
            half = position // 2
            own_ends[half * PITCH : (half + 1) * PITCH, :] = keep_inner(values, band_cols)
            output_ends[half] = (
                pair[index].astype(F32) + mask_of(index) * activated[at + PAD : at + PAD + band_cols, lanes]
            ).astype(BF16)
    spread(carry, carry3_ends, 0, 4, 0, -1)
    write_first = pltpu.make_async_copy(output_ends.at[0], pair_output.at[0], sems.at[1])
    write_last = pltpu.make_async_copy(output_ends.at[1], pair_output.at[last], sems.at[2])
    write_first.start()
    write_last.start()
    carry_sources = [
        (carry3, 0, range(1, last)), (carry3_ends, -1, (-1, 0)), (carry3_ends, tile_rows - 3, (last, tile_rows)),
    ]
    own_sources = [(own, 0, range(1, last)), (own_ends, 0, (0,)), (own_ends, tile_rows - 2, (last,))]

    totals[...] = jnp.zeros(totals.shape, F32)
    skew[...] = jnp.zeros(skew.shape, F32)
    pairs = 4
    query_at = 9 * channels + all_bins + tail
    query_rows = []
    for first in range(0, tile_rows, 2 * pairs):
        back = jnp.dot(four_rows(carry_sources, first, pairs), backward[...], preferred_element_type=F32)
        for offset in range(2 * pairs):
            index = first + offset
            lanes = slice(offset % 2 * channels, (offset % 2 + 1) * channels)
            at = offset // 2 * PITCH + PAD
            masked = mask_of(index) * back[at : at + band_cols, lanes]
            grad[index] = (cot[index].astype(F32) + masked).astype(BF16)
            query_rows.append(jnp.sum(masked, axis=0, keepdims=True))
            skew[index % 8, index - index % 8 : index - index % 8 + band_cols, :] += masked
    write_grad = pltpu.make_async_copy(grad, pair_grad, sems.at[3])
    write_grad.start()
    totals[pl.ds(pl.multiple_of(query_at + row_start, 16), tile_rows), :] = jnp.concatenate(query_rows, axis=0)
    reach = tile_rows + band_cols - 8
    for step in range(8):
        totals[pl.ds(9 * channels + col_start + step, reach), :] += skew[step, :reach, :]

    per = 12
    grads = jnp.zeros((channels, 9 * channels), F32)
    for first in range(0, tile_rows, per):
        around = jnp.concatenate(
            [
                jnp.concatenate([rows_of(mixed_sources, index + step) for index in range(first, first + per)], axis=0)
                for step in (-1, 0, 1)
            ],
            axis=1,
        )
        cots = jnp.concatenate([rows_of(own_sources, index) for index in range(first, first + per)], axis=0)
        grads = grads + lax.dot_general(cots, around, (((0,), (0,)), ((), ())), preferred_element_type=F32)
    for tap in range(9):
        totals[tap * channels : (tap + 1) * channels, :] = grads[:, tap * channels : (tap + 1) * channels]
    half = keep.shape[0]
    keep[...] = totals[pl.ds(pl.multiple_of(core * half, half), half), :]
    send[...] = totals[pl.ds(pl.multiple_of((1 - core) * half, half), half), :].astype(BF16)
    for copy in (write_output, write_first, write_last, write_grad):
        copy.wait()


def add_kernel(pieces, copies):
    total = pieces[0].astype(F32)
    for index in range(1, pieces.shape[0]):
        total = total + pieces[index].astype(F32)
    copies[...] = jnp.broadcast_to(total.astype(BF16), copies.shape)


def finish_kernel(
    mine, theirs, features_turned, context_turned, projection, feature_grad, proj_grad, conv_grad,
    whole, feature_out, proj_out, conv_out, sems,
):
    core = lax.axis_index("core")
    row = lax.axis_index(ROW)
    half, channels = mine.shape
    all_bins, tail = features_turned.shape[1], context_turned.shape[1]
    tile_rows = feature_grad.shape[0]
    whole[pl.ds(pl.multiple_of(core * half, half), half), :] = mine[...]
    whole[pl.ds(pl.multiple_of((1 - core) * half, half), half), :] = theirs[...]
    copies = [
        pltpu.make_async_copy(source, target, sems.at[index])
        for index, (source, target) in enumerate(((conv_out, conv_grad), (proj_out, proj_grad), (feature_out, feature_grad)))
    ]
    for tap in range(9):
        conv_out[tap] = whole[tap * channels : (tap + 1) * channels, :].astype(F32).T
    copies[0].start()
    key_at = 9 * channels
    query_at = key_at + all_bins + tail
    own = features_turned[...]
    proj_out[:, :channels] = jnp.dot(own, whole[query_at : query_at + all_bins, :], preferred_element_type=F32)
    proj_out[:, channels:] = jnp.dot(
        own, whole[key_at : key_at + all_bins, :], preferred_element_type=F32
    ) + jnp.dot(context_turned[...], whole[key_at + all_bins : query_at, :], preferred_element_type=F32)
    copies[1].start()
    start = pl.multiple_of(row * tile_rows, 16)
    both = jnp.concatenate(
        [whole[pl.ds(query_at + start, tile_rows), :], whole[pl.ds(key_at + start, tile_rows), :]], axis=1
    )
    feature_out[...] = lax.dot_general(
        both, projection[...], (((1,), (1,)), ((), ())), preferred_element_type=F32
    ).astype(BF16)
    copies[2].start()
    for copy in copies:
        copy.wait()


def in_hbm(*arrays):
    return [pltpu.with_memory_space_constraint(array, pltpu.HBM) for array in arrays]


def body(
    pair_input, bin_features, context_features, proj_weight, conv_weight, valid_bins, cotangent
):
    tile_rows, band_cols, channels = pair_input.shape
    width = bin_features.shape[1]
    row_count = lax.axis_size(ROW)
    col_count = lax.axis_size("col")
    all_bins = tile_rows * row_count
    tail = context_features.shape[0]
    chips = row_count * col_count // 2
    taken = -(-(tile_rows + 2 * HALO) // 8) * 8
    vmem = pl.BlockSpec(memory_space=pltpu.VMEM)
    anywhere = pl.BlockSpec(memory_space=pl.ANY)

    def shape(*dims, dtype=BF16):
        return jax.ShapeDtypeStruct(dims, dtype)

    layers = EDGES + width // channels
    chunk = pltpu.VMEM((tile_rows, SIDE, channels), BF16)
    to_core, to_chip, to_even, to_odd = pl.pallas_call(
        pack_kernel,
        out_shape=(
            shape(layers, tile_rows, channels),
            shape(layers, tile_rows, channels),
            shape(EDGES, tile_rows, channels),
            shape(EDGES, tile_rows, channels),
        ),
        in_specs=[anywhere] * 3,
        out_specs=(vmem,) * 4,
        scratch_shapes=[
            chunk, chunk, chunk, chunk,
            pltpu.VMEM((tile_rows * SIDE, channels), F32),
            pltpu.VMEM((2, EDGES, tile_rows, channels), BF16),
            pltpu.SemaphoreType.DMA((2 * layers + 4,)),
        ],
        compiler_params=PARAMS,
        name="pack",
    )(*in_hbm(pair_input, cotangent, bin_features))
    other_core = [(0, 1), (1, 0)]
    even_cols = [(i, i ^ 1) for i in range(col_count) if i ^ 1 < col_count]
    odd_cols = []
    for row in range(row_count):
        for column in range(col_count):
            partner = ((column + 1) ^ 1) - 1
            if 0 <= partner < col_count:
                odd_cols.append((row * col_count + column, row * col_count + partner))
            else:
                odd_cols.append((row * col_count + column, (row ^ 1) * col_count + column))
    odd_rows = [(i, ((i + 1) ^ 1) - 1) for i in range(1, row_count - 1)]
    ends = [(0, 3), (3, 0)] if row_count == 4 else []
    from_chip = lax.ppermute(to_chip, ROW, odd_rows + ends)
    from_odd = lax.ppermute(to_odd, ROW + ("col",), odd_cols)
    from_even = lax.ppermute(to_even, "col", even_cols)
    from_core = lax.ppermute(to_core, "core", other_core)
    near_bins = tile_rows + band_cols + 2 * MARGIN
    valid_bins, from_chip = lax.optimization_barrier((valid_bins, from_chip))
    window, rows_valid, forward, backward, projection, context_key, context_turned = pl.pallas_call(
        weights_kernel,
        out_shape=(
            shape(near_bins, channels, dtype=F32),
            shape(taken, channels, dtype=F32),
            shape(12 * channels, 2 * channels),
            shape(12 * channels, 2 * channels),
            shape(*proj_weight.shape),
            shape(tail, channels),
            shape(width, tail),
        ),
        in_specs=[vmem] * 4,
        out_specs=(vmem,) * 7,
        compiler_params=PARAMS,
        cost_estimate=pl.CostEstimate(flops=1 << 30, bytes_accessed=1 << 21, transcendentals=0),
        name="weights",
    )(*in_hbm(valid_bins, context_features, proj_weight, conv_weight))
    if row_count == 4:
        sources = [to_core, from_core, from_chip, lax.ppermute(from_chip, "core", other_core)]
    else:
        sources = [lax.all_gather(bin_features, ROW, axis=0, tiled=True)]

    features_turned, query, key = pl.pallas_call(
        prepare_kernel,
        out_shape=(
            shape(width, all_bins),
            shape(tile_rows + 2 * MARGIN, channels, dtype=F32),
            shape(near_bins, channels, dtype=F32),
        ),
        in_specs=[vmem] * (2 + len(sources)),
        out_specs=(vmem,) * 3,
        scratch_shapes=[
            pltpu.VMEM((all_bins, width), BF16),
            pltpu.VMEM((all_bins + 2 * MARGIN, channels), F32),
            pltpu.VMEM((all_bins + tail + 2 * MARGIN, channels), F32),
        ],
        compiler_params=PARAMS,
        name="prepare",
    )(projection, context_key, *sources)
    from_even, from_odd, key = lax.optimization_barrier((from_even, from_odd, key))
    corner = shape(2, EDGES, SIDE, channels)
    sides, corner_to_core, corner_to_chip = pl.pallas_call(
        corner_kernel,
        out_shape=(shape(2, EDGES, tile_rows, channels), corner, corner),
        in_specs=[vmem] * 2,
        out_specs=(vmem,) * 3,
        compiler_params=PARAMS,
        name="corners",
    )(from_even, from_odd)
    corner_chip = lax.ppermute(corner_to_chip, ROW, odd_rows + ends)
    corner_core = lax.ppermute(corner_to_core, "core", other_core)


    piece = -(-(9 * channels + 2 * all_bins + tail) // (32 * chips)) * 16
    half = piece * chips
    span = tile_rows * PITCH
    inner = pl.pallas_call(
        inner_kernel,
        out_shape=(
            shape(span, 3 * channels), shape(span, 3 * channels), shape(span, channels), shape(*pair_input.shape),
        ),
        in_specs=[vmem] * 8,
        out_specs=(vmem,) * 4,
        scratch_shapes=[pltpu.VMEM((span + 4 * PAD, channels), F32)] * 2,
        compiler_params=PARAMS,
        name="inner",
    )(pair_input, cotangent, sides, query, key, window, rows_valid, forward)
    pair_output, pair_grad, keep, send = pl.pallas_call(
        outer_kernel,
        out_shape=(
            shape(*pair_input.shape),
            shape(*pair_input.shape),
            shape(half, channels, dtype=F32),
            shape(half, channels),
        ),
        in_specs=[vmem] * 17,
        out_specs=(anywhere, anywhere, vmem, vmem),
        scratch_shapes=[
            pltpu.VMEM((2, EDGES, tile_rows, channels), BF16),
            pltpu.VMEM((2, 2, EDGES, SIDE, channels), BF16),
            pltpu.VMEM((4 * PITCH + 4 * PAD, channels), F32),
            pltpu.VMEM((4 * PITCH + 4 * PAD, channels), F32),
            pltpu.VMEM((4 * PITCH, 3 * channels), BF16),
            pltpu.VMEM((4 * PITCH, 3 * channels), BF16),
            pltpu.VMEM((2 * PITCH, channels), BF16),
            pltpu.VMEM((2, band_cols, channels), BF16),
            pltpu.VMEM((8, tile_rows + band_cols, channels), F32),
            pltpu.VMEM((2 * half, channels), F32),
            pltpu.VMEM(pair_input.shape, BF16),
            pltpu.SemaphoreType.DMA((4,)),
        ],
        compiler_params=PARAMS,
        name="outer",
    )(
        pair_input, cotangent, from_core, from_chip, sides, corner_core, corner_chip, query, key, window, rows_valid,
        forward, backward, *inner,
    )

    part = (keep + lax.ppermute(send, "core", other_core).astype(F32)).astype(BF16)
    pieces = lax.all_to_all(part.reshape(chips, piece, channels), CHIPS, 0, 0)
    copies = pl.pallas_call(
        add_kernel,
        out_shape=shape(chips, piece, channels),
        in_specs=[vmem],
        out_specs=vmem,
        compiler_params=PARAMS,
        name="add",
    )(pieces)
    mine = lax.all_to_all(copies, CHIPS, 0, 0).reshape(half, channels)
    theirs = lax.ppermute(mine, "core", other_core)

    feature_grad, proj_grad, conv_grad = pl.pallas_call(
        finish_kernel,
        out_shape=(
            shape(*bin_features.shape),
            shape(*proj_weight.shape, dtype=F32),
            shape(*conv_weight.shape, dtype=F32),
        ),
        in_specs=[vmem] * 5,
        out_specs=(anywhere,) * 3,
        scratch_shapes=[
            pltpu.VMEM((2 * half, channels), BF16),
            pltpu.VMEM(bin_features.shape, BF16),
            pltpu.VMEM(proj_weight.shape, F32),
            pltpu.VMEM(conv_weight.shape, F32),
            pltpu.SemaphoreType.DMA((3,)),
        ],
        compiler_params=PARAMS,
        name="finish",
    )(mine, theirs, features_turned, context_turned, projection)
    return (pair_output, pair_grad, feature_grad, proj_grad, conv_grad)


def solution(mesh):
    rows, cols = mesh.shape["row"], mesh.shape["col"]
    split = Mesh(mesh.devices.reshape(rows // 2, 2, cols), ("rx", "core", "col"))
    tile = P(ROW, "col", None)
    in_specs = (tile, P(ROW, None), P(), P(), P(), P(), tile)
    out_specs = (tile, tile, P(ROW, None), P(), P())
    return jax.shard_map(body, mesh=split, in_specs=in_specs, out_specs=out_specs, check_vma=False)
```

```python
import jax
import jax.numpy as jnp
from jax import lax
from jax.experimental import pallas as pl
from jax.experimental.pallas import tpu as pltpu
from jax.sharding import Mesh, PartitionSpec as P

ROW = ("rx", "core")
CHIPS = ("rx", "col")
BF16 = jnp.bfloat16
F32 = jnp.float32
HALO = 2
EDGES = HALO + 1
SIDE = 16
MARGIN = 16
PITCH = 64
PAD = 8
PARAMS = pltpu.CompilerParams(vmem_limit_bytes=20 * 1024 * 1024)


def pack_kernel(
    pair, cot, features, to_core, to_chip, to_even, to_odd, pair_low, pair_high, cot_low, cot_high, work, sides, sems
):
    tile_rows, band_cols, channels = pair.shape
    odd_row = lax.rem(lax.axis_index(ROW), 2)
    odd_col = lax.rem(lax.axis_index("col"), 2)
    parts = []
    for target, at_end in ((to_chip, odd_row), (to_core, 1 - odd_row)):
        parts.append((pair.at[pl.ds(at_end * (tile_rows - HALO), HALO)], target.at[:HALO]))
        parts.append((cot.at[pl.ds(at_end * (tile_rows - 1), 1)], target.at[HALO:EDGES]))
        for part in range(features.shape[1] // channels):
            parts.append((features.at[:, part * channels : (part + 1) * channels], target.at[EDGES + part]))
    parts.append((pair.at[:, :SIDE], pair_low))
    parts.append((pair.at[:, band_cols - SIDE :], pair_high))
    parts.append((cot.at[:, :SIDE], cot_low))
    parts.append((cot.at[:, band_cols - SIDE :], cot_high))
    copies = [pltpu.make_async_copy(source, target, sems.at[i]) for i, (source, target) in enumerate(parts)]
    for copy in copies[-4:] + copies[:-4]:
        copy.start()
    for copy in copies[-4:]:
        copy.wait()
    for side, (chunk, kind) in enumerate(((pair_low, cot_low), (pair_high, cot_high))):
        for slot, source, column in (
            (0, chunk, side * (SIDE - 2)), (1, chunk, side * (SIDE - 2) + 1), (2, kind, side * (SIDE - 1)),
        ):
            if slot != 1:
                work[...] = source[...].astype(F32).reshape(tile_rows * SIDE, channels)
            sides[side, slot] = work[pl.ds(column, tile_rows, stride=SIDE), :].astype(BF16)
    to_even[...] = sides[1 - odd_col]
    to_odd[...] = sides[odd_col]
    for copy in copies[:-4]:
        copy.wait()


def corner_kernel(from_even, from_odd, sides, to_core, to_chip):
    tile_rows = from_even.shape[1]
    odd_row = lax.rem(lax.axis_index(ROW), 2)
    odd_col = lax.rem(lax.axis_index("col"), 2)
    sides[1 - odd_col] = from_even[...]
    sides[odd_col] = from_odd[...]
    for target, at_end in ((to_chip, odd_row), (to_core, 1 - odd_row)):
        start = pl.multiple_of(at_end * (tile_rows - SIDE), 16)
        target[...] = sides[:, :, pl.ds(start, SIDE), :]


def weights_kernel(
    valid, context, proj_weight, conv_weight,
    window, rows_valid, forward, backward, projection, context_key, context_turned,
):
    channels = window.shape[1]
    bins = valid.shape[0]
    band_total = context.shape[0]
    all_bins = bins - band_total
    tile_rows = all_bins // lax.axis_size(ROW)
    row_start = lax.axis_index(ROW) * tile_rows
    col_start = row_start + lax.axis_index("col") * (band_total // lax.axis_size("col"))
    flags = jnp.broadcast_to(valid[...].reshape(1, bins).astype(F32).astype(BF16), (channels, bins))
    flip = (((1,), (1,)), ((), ()))
    for target, begin, stop in ((window, col_start - MARGIN, bins), (rows_valid, row_start - HALO, all_bins)):
        shape = (target.shape[0], bins)
        bin_index = lax.broadcasted_iota(jnp.int32, shape, 1)
        chosen = jnp.logical_and(bin_index == lax.broadcasted_iota(jnp.int32, shape, 0) + begin, bin_index < stop)
        target[...] = lax.dot_general(chosen.astype(F32).astype(BF16), flags, flip, preferred_element_type=F32)
    forward[...] = jnp.zeros(forward.shape, BF16)
    backward[...] = jnp.zeros(backward.shape, BF16)
    for tap in range(9):
        row_step, step = tap // 3 - 1, tap % 3
        values = conv_weight[tap]
        turned = values.astype(F32).T.astype(BF16)
        for out in range(2):
            lanes = slice(out * channels, (out + 1) * channels)
            at = ((row_step + 1 + out) * 3 + step) * channels
            forward[at : at + channels, lanes] = values
            at = ((1 - row_step + out) * 3 + step) * channels
            backward[at : at + channels, lanes] = turned
    projection[...] = proj_weight[...]
    context_key[...] = jnp.dot(context[...], proj_weight[:, channels:], preferred_element_type=F32).astype(BF16)
    context_turned[...] = context[...].astype(F32).T.astype(BF16)


def prepare_kernel(projection, context_key, *refs):
    sources, (features_turned, query, key, features, query_rows, key_rows) = refs[:-6], refs[-6:]
    channels = query.shape[1]
    all_bins, tail = features.shape[0], context_key.shape[0]
    row, col = lax.axis_index(ROW), lax.axis_index("col")
    if len(sources) == 1:
        features[...] = sources[0][...]
    else:
        for source, step in zip(sources, (0, 1, 3, 2)):
            rows = source.shape[1]
            start = pl.multiple_of(lax.bitwise_xor(row, step) * rows, 16)
            for part in range(source.shape[0] - EDGES):
                features[pl.ds(start, rows), part * channels : (part + 1) * channels] = source[EDGES + part]
    tile_rows = query.shape[0] - 2 * MARGIN
    row_start = row * tile_rows
    col_start = row_start + col * (key.shape[0] - 2 * MARGIN - tile_rows)
    proj = jnp.dot(features[...], projection[...], preferred_element_type=F32).astype(BF16).astype(F32)
    margin = jnp.zeros((MARGIN, channels), F32)
    for target, size in ((query_rows, all_bins), (key_rows, all_bins + tail)):
        target[:MARGIN, :] = margin
        target[MARGIN + size :, :] = margin
    query_rows[MARGIN : MARGIN + all_bins, :] = proj[:, :channels]
    key_rows[MARGIN : MARGIN + all_bins, :] = proj[:, channels:]
    key_rows[MARGIN + all_bins : MARGIN + all_bins + tail, :] = context_key[...].astype(F32)
    query[...] = query_rows[pl.ds(pl.multiple_of(row_start, 16), query.shape[0]), :]
    key[...] = key_rows[pl.ds(pl.multiple_of(col_start, 16), key.shape[0]), :]
    features_turned[...] = features[...].astype(F32).T.astype(BF16)


def quarter_of(parts):
    if parts == 1:
        return 0
    return 2 * lax.axis_index("rx") + lax.rem(lax.axis_index("col"), 2)


def spread(source, target, first, last, base, sign):
    channels = source.shape[1]
    for index in range(first, last):
        start = (index - base) * PITCH
        for step in range(3):
            target[start : start + PITCH, step * channels : (step + 1) * channels] = source[
                pl.ds(PAD + start + sign * (step - 1), PITCH), :
            ].astype(BF16)


def rows_of(sources, index):
    for array, base, held in sources:
        if index in held:
            return array[(index - base) * PITCH : (index - base + 1) * PITCH, :]
    raise IndexError(index)


def four_rows(sources, first, pairs):
    columns = []
    for step in range(4):
        parts = [rows_of(sources, first + 2 * index + step - 1) for index in range(pairs)]
        columns.append(jnp.concatenate(parts, axis=0))
    return jnp.concatenate(columns, axis=1)


def silu_parts(conv):
    sigma = jax.nn.sigmoid(conv)
    return conv * sigma, sigma * (1.0 + conv * (1.0 - sigma))


def has_sides():
    col = lax.axis_index("col")
    return (col > 0).astype(F32), (col < lax.axis_size("col") - 1).astype(F32)


def keep_inner(values, band_cols):
    spot = lax.broadcasted_iota(jnp.int32, values.shape, 0)
    inner = jnp.logical_and(spot >= PAD, spot < PAD + band_cols)
    return jnp.where(inner, values, 0.0).astype(BF16)


def inner_kernel(
    pair, cot, sides, query, key, window, rows_valid, forward,
    mixed3, carry3, own, output,
    mixed, carry,
):
    tile_rows, band_cols, channels = pair.shape

    def place(index, column):
        return PAD + index * PITCH + PAD + column

    def mask_of(index):
        return window[pl.ds(MARGIN + index, band_cols), :] * rows_valid[pl.ds(index + HALO, 1), :]

    gap = jnp.zeros((PITCH - band_cols, channels), F32)
    mixed[:PAD, :] = jnp.zeros((PAD, channels), F32)
    mixed[PAD : 2 * PAD, :] = jnp.zeros((PAD, channels), F32)
    for index in range(tile_rows):
        mixed[pl.ds(place(index, band_cols), PITCH - band_cols), :] = gap
        carry[pl.ds(place(index, band_cols), PITCH - band_cols), :] = gap
    for index in range(tile_rows):
        mask = mask_of(index)
        value = mask * (
            pair[index].astype(F32) + query[pl.ds(MARGIN + index, 1), :] + key[pl.ds(MARGIN + index, band_cols), :]
        )
        mixed[pl.ds(place(index, 0), band_cols), :] = value
        carry[pl.ds(place(index, 0), band_cols), :] = mask * cot[index].astype(F32)
    has_low, has_high = has_sides()
    for column, side, slot, has in (
        (-2, 0, 0, has_low), (-1, 0, 1, has_low), (band_cols, 1, 0, has_high), (band_cols + 1, 1, 1, has_high),
    ):
        begin = MARGIN + column
        mask = rows_valid[pl.ds(HALO, tile_rows), :] * window[pl.ds(begin, tile_rows), :] * has
        value = sides[side, slot].astype(F32) + query[pl.ds(MARGIN, tile_rows), :] + key[pl.ds(begin, tile_rows), :]
        mixed[pl.ds(place(0, column), tile_rows, stride=PITCH), :] = mask * value
        if column in (-1, band_cols):
            carry[pl.ds(place(0, column), tile_rows, stride=PITCH), :] = mask * sides[side, HALO].astype(F32)
    spread(mixed, mixed3, 0, tile_rows, 0, 1)

    first, last = 1, tile_rows - 1
    sources = [(mixed3, 0, range(tile_rows))]
    while first < last:
        pairs = min(5, (last - first) // 2)
        conv = jnp.dot(four_rows(sources, first, pairs), forward[...], preferred_element_type=F32)
        activated, slope = silu_parts(conv)
        for offset in range(2 * pairs):
            index = first + offset
            lanes = slice(offset % 2 * channels, (offset % 2 + 1) * channels)
            at = offset // 2 * PITCH
            here = pl.ds(PAD + index * PITCH, PITCH)
            values = carry[here, :] * slope[at : at + PITCH, lanes]
            carry[here, :] = values
            own[index * PITCH : (index + 1) * PITCH, :] = keep_inner(values, band_cols)
            output[index] = (
                pair[index].astype(F32) + mask_of(index) * activated[at + PAD : at + PAD + band_cols, lanes]
            ).astype(BF16)
        first += 2 * pairs
    spread(carry, carry3, 1, tile_rows - 1, 0, -1)


def outer_kernel(
    pair, cot, from_core, from_chip, sides, corner_core, corner_chip, query, key, window, rows_valid, forward, backward,
    mixed3, carry3, own, output,
    pair_output, pair_grad, keep, send,
    near, corners, mixed, carry, mixed3_ends, carry3_ends, own_ends, output_ends, skew, totals, grad, sems,
):
    tile_rows, band_cols, channels = pair.shape
    row, col = lax.axis_index(ROW), lax.axis_index("col")
    core = lax.axis_index("core")
    all_bins = lax.axis_size(ROW) * tile_rows
    tail = lax.axis_size("col") * band_cols
    row_start = row * tile_rows
    col_start = row_start + col * band_cols
    odd_row = lax.rem(row, 2)
    last = tile_rows - 1
    write_output = pltpu.make_async_copy(output.at[1:last], pair_output.at[1:last], sems.at[0])
    write_output.start()
    near[1 - odd_row] = from_core[:EDGES]
    near[odd_row] = from_chip[:EDGES]
    corners[1 - odd_row] = corner_core[...]
    corners[odd_row] = corner_chip[...]

    def place(position, column):
        return PAD + position * PITCH + PAD + column

    def mask_of(index):
        return window[pl.ds(MARGIN + index, band_cols), :] * rows_valid[pl.ds(index + HALO, 1), :]

    has = has_sides()
    mixed_rows = (-2, -1, tile_rows, tile_rows + 1)
    carry_rows = (-1, 0, last, tile_rows)
    gap = jnp.zeros((PITCH - band_cols, channels), F32)
    for array in (mixed, carry):
        array[: 2 * PAD, :] = jnp.zeros((2 * PAD, channels), F32)
        for position in range(4):
            array[pl.ds(place(position, band_cols), PITCH - band_cols), :] = gap

    def corner_of(index, side, slot):
        if index < 0:
            return corners[0, side, slot].astype(F32)[SIDE + index : SIDE + index + 1, :]
        return corners[1, side, slot].astype(F32)[index - tile_rows : index - tile_rows + 1, :]

    def pixel_mask(index, column, side):
        return rows_valid[pl.ds(index + HALO, 1), :] * window[pl.ds(MARGIN + index + column, 1), :] * has[side]

    for position, index in enumerate(mixed_rows):
        source = near[0, HALO + index] if index < 0 else near[1, index - tile_rows]
        row_query = query[pl.ds(MARGIN + index, 1), :]
        mixed[pl.ds(place(position, 0), band_cols), :] = mask_of(index) * (
            source.astype(F32) + row_query + key[pl.ds(MARGIN + index, band_cols), :]
        )
        for column, side, slot in ((-2, 0, 0), (-1, 0, 1), (band_cols, 1, 0), (band_cols + 1, 1, 1)):
            value = corner_of(index, side, slot) + row_query + key[pl.ds(MARGIN + index + column, 1), :]
            mixed[pl.ds(place(position, column), 1), :] = pixel_mask(index, column, side) * value
    for position, index in enumerate(carry_rows):
        source = near[0, HALO] if index < 0 else near[1, HALO] if index > last else cot[index]
        carry[pl.ds(place(position, 0), band_cols), :] = mask_of(index) * source.astype(F32)
        for column, side in ((-1, 0), (band_cols, 1)):
            if 0 <= index <= last:
                chunk = index // SIDE * SIDE
                value = sides[side, HALO, chunk : chunk + SIDE].astype(F32)[index - chunk : index - chunk + 1, :]
            else:
                value = corner_of(index, side, HALO)
            carry[pl.ds(place(position, column), 1), :] = pixel_mask(index, column, side) * value
    spread(mixed, mixed3_ends, 0, 4, 0, 1)
    mixed_sources = [
        (mixed3, 0, range(tile_rows)), (mixed3_ends, -2, (-2, -1)), (mixed3_ends, tile_rows - 2, (tile_rows, tile_rows + 1)),
    ]
    ends = jnp.concatenate([four_rows(mixed_sources, -1, 1), four_rows(mixed_sources, last, 1)], axis=0)
    activated, slope = silu_parts(jnp.dot(ends, forward[...], preferred_element_type=F32))
    for position, index in enumerate(carry_rows):
        lanes = slice(position % 2 * channels, (position % 2 + 1) * channels)
        at = position // 2 * PITCH
        here = pl.ds(PAD + position * PITCH, PITCH)
        values = carry[here, :] * slope[at : at + PITCH, lanes]
        carry[here, :] = values
        if 0 <= index <= last:
            half = position // 2
            own_ends[half * PITCH : (half + 1) * PITCH, :] = keep_inner(values, band_cols)
            output_ends[half] = (
                pair[index].astype(F32) + mask_of(index) * activated[at + PAD : at + PAD + band_cols, lanes]
            ).astype(BF16)
    spread(carry, carry3_ends, 0, 4, 0, -1)
    write_first = pltpu.make_async_copy(output_ends.at[0], pair_output.at[0], sems.at[1])
    write_last = pltpu.make_async_copy(output_ends.at[1], pair_output.at[last], sems.at[2])
    write_first.start()
    write_last.start()
    carry_sources = [
        (carry3, 0, range(1, last)), (carry3_ends, -1, (-1, 0)), (carry3_ends, tile_rows - 3, (last, tile_rows)),
    ]
    own_sources = [(own, 0, range(1, last)), (own_ends, 0, (0,)), (own_ends, tile_rows - 2, (last,))]

    totals[...] = jnp.zeros(totals.shape, F32)
    skew[...] = jnp.zeros(skew.shape, F32)
    pairs = 4
    query_at = 9 * channels + all_bins + tail
    query_rows = []
    for first in range(0, tile_rows, 2 * pairs):
        back = jnp.dot(four_rows(carry_sources, first, pairs), backward[...], preferred_element_type=F32)
        for offset in range(2 * pairs):
            index = first + offset
            lanes = slice(offset % 2 * channels, (offset % 2 + 1) * channels)
            at = offset // 2 * PITCH + PAD
            masked = mask_of(index) * back[at : at + band_cols, lanes]
            grad[index] = (cot[index].astype(F32) + masked).astype(BF16)
            query_rows.append(jnp.sum(masked, axis=0, keepdims=True))
            skew[index % 8, index - index % 8 : index - index % 8 + band_cols, :] += masked
    write_grad = pltpu.make_async_copy(grad, pair_grad, sems.at[3])
    write_grad.start()
    totals[pl.ds(pl.multiple_of(query_at + row_start, 16), tile_rows), :] = jnp.concatenate(query_rows, axis=0)
    reach = tile_rows + band_cols - 8
    for step in range(8):
        totals[pl.ds(9 * channels + col_start + step, reach), :] += skew[step, :reach, :]

    per = 12
    grads = jnp.zeros((channels, 9 * channels), F32)
    for first in range(0, tile_rows, per):
        around = jnp.concatenate(
            [
                jnp.concatenate([rows_of(mixed_sources, index + step) for index in range(first, first + per)], axis=0)
                for step in (-1, 0, 1)
            ],
            axis=1,
        )
        cots = jnp.concatenate([rows_of(own_sources, index) for index in range(first, first + per)], axis=0)
        grads = grads + lax.dot_general(cots, around, (((0,), (0,)), ((), ())), preferred_element_type=F32)
    for tap in range(9):
        totals[tap * channels : (tap + 1) * channels, :] = grads[:, tap * channels : (tap + 1) * channels]
    parts, size = keep.shape[:2]
    for part in range(parts):
        place = lax.bitwise_xor(quarter_of(parts), part)
        keep[part] = totals[pl.ds(pl.multiple_of((core * parts + place) * size, 16), size), :]
        send[part] = totals[pl.ds(pl.multiple_of(((1 - core) * parts + place) * size, 16), size), :].astype(BF16)
    for copy in (write_output, write_first, write_last, write_grad):
        copy.wait()


def add_kernel(pieces, copies):
    total = pieces[0].astype(F32)
    for index in range(1, pieces.shape[0]):
        total = total + pieces[index].astype(F32)
    copies[...] = jnp.broadcast_to(total.astype(BF16), copies.shape)


def finish_kernel(
    mine, theirs, features_turned, context_turned, projection, feature_grad, proj_grad, conv_grad,
    whole, feature_out, proj_out, conv_out, sems,
):
    core = lax.axis_index("core")
    row = lax.axis_index(ROW)
    parts, size, channels = mine.shape
    all_bins, tail = features_turned.shape[1], context_turned.shape[1]
    tile_rows = feature_grad.shape[0]
    for part in range(parts):
        place = lax.bitwise_xor(quarter_of(parts), part)
        whole[pl.ds(pl.multiple_of((core * parts + place) * size, 16), size), :] = mine[part]
        whole[pl.ds(pl.multiple_of(((1 - core) * parts + place) * size, 16), size), :] = theirs[part]
    copies = [
        pltpu.make_async_copy(source, target, sems.at[index])
        for index, (source, target) in enumerate(((conv_out, conv_grad), (proj_out, proj_grad), (feature_out, feature_grad)))
    ]
    for tap in range(9):
        conv_out[tap] = whole[tap * channels : (tap + 1) * channels, :].astype(F32).T
    copies[0].start()
    key_at = 9 * channels
    query_at = key_at + all_bins + tail
    own = features_turned[...]
    proj_out[:, :channels] = jnp.dot(own, whole[query_at : query_at + all_bins, :], preferred_element_type=F32)
    proj_out[:, channels:] = jnp.dot(
        own, whole[key_at : key_at + all_bins, :], preferred_element_type=F32
    ) + jnp.dot(context_turned[...], whole[key_at + all_bins : query_at, :], preferred_element_type=F32)
    copies[1].start()
    start = pl.multiple_of(row * tile_rows, 16)
    both = jnp.concatenate(
        [whole[pl.ds(query_at + start, tile_rows), :], whole[pl.ds(key_at + start, tile_rows), :]], axis=1
    )
    feature_out[...] = lax.dot_general(
        both, projection[...], (((1,), (1,)), ((), ())), preferred_element_type=F32
    ).astype(BF16)
    copies[2].start()
    for copy in copies:
        copy.wait()


def in_hbm(*arrays):
    return [pltpu.with_memory_space_constraint(array, pltpu.HBM) for array in arrays]


def body(
    pair_input, bin_features, context_features, proj_weight, conv_weight, valid_bins, cotangent
):
    tile_rows, band_cols, channels = pair_input.shape
    width = bin_features.shape[1]
    row_count = lax.axis_size(ROW)
    col_count = lax.axis_size("col")
    all_bins = tile_rows * row_count
    tail = context_features.shape[0]
    chips = row_count * col_count // 2
    taken = -(-(tile_rows + 2 * HALO) // 8) * 8
    vmem = pl.BlockSpec(memory_space=pltpu.VMEM)
    anywhere = pl.BlockSpec(memory_space=pl.ANY)

    def shape(*dims, dtype=BF16):
        return jax.ShapeDtypeStruct(dims, dtype)

    layers = EDGES + width // channels
    chunk = pltpu.VMEM((tile_rows, SIDE, channels), BF16)
    to_core, to_chip, to_even, to_odd = pl.pallas_call(
        pack_kernel,
        out_shape=(
            shape(layers, tile_rows, channels),
            shape(layers, tile_rows, channels),
            shape(EDGES, tile_rows, channels),
            shape(EDGES, tile_rows, channels),
        ),
        in_specs=[anywhere] * 3,
        out_specs=(vmem,) * 4,
        scratch_shapes=[
            chunk, chunk, chunk, chunk,
            pltpu.VMEM((tile_rows * SIDE, channels), F32),
            pltpu.VMEM((2, EDGES, tile_rows, channels), BF16),
            pltpu.SemaphoreType.DMA((2 * layers + 4,)),
        ],
        compiler_params=PARAMS,
        name="pack",
    )(*in_hbm(pair_input, cotangent, bin_features))
    other_core = [(0, 1), (1, 0)]
    even_cols = [(i, i ^ 1) for i in range(col_count) if i ^ 1 < col_count]
    odd_cols = []
    for row in range(row_count):
        for column in range(col_count):
            partner = ((column + 1) ^ 1) - 1
            if 0 <= partner < col_count:
                odd_cols.append((row * col_count + column, row * col_count + partner))
            else:
                odd_cols.append((row * col_count + column, (row ^ 1) * col_count + column))
    odd_rows = [(i, ((i + 1) ^ 1) - 1) for i in range(1, row_count - 1)]
    ends = [(0, 3), (3, 0)] if row_count == 4 else []
    from_chip = lax.ppermute(to_chip, ROW, odd_rows + ends)
    from_odd = lax.ppermute(to_odd, ROW + ("col",), odd_cols)
    from_even = lax.ppermute(to_even, "col", even_cols)
    from_core = lax.ppermute(to_core, "core", other_core)
    near_bins = tile_rows + band_cols + 2 * MARGIN
    valid_bins, from_chip = lax.optimization_barrier((valid_bins, from_chip))
    window, rows_valid, forward, backward, projection, context_key, context_turned = pl.pallas_call(
        weights_kernel,
        out_shape=(
            shape(near_bins, channels, dtype=F32),
            shape(taken, channels, dtype=F32),
            shape(12 * channels, 2 * channels),
            shape(12 * channels, 2 * channels),
            shape(*proj_weight.shape),
            shape(tail, channels),
            shape(width, tail),
        ),
        in_specs=[vmem] * 4,
        out_specs=(vmem,) * 7,
        compiler_params=PARAMS,
        cost_estimate=pl.CostEstimate(flops=1 << 30, bytes_accessed=1 << 21, transcendentals=0),
        name="weights",
    )(*in_hbm(valid_bins, context_features, proj_weight, conv_weight))
    if row_count == 4:
        sources = [to_core, from_core, from_chip, lax.ppermute(from_chip, "core", other_core)]
    else:
        sources = [lax.all_gather(bin_features, ROW, axis=0, tiled=True)]

    features_turned, query, key = pl.pallas_call(
        prepare_kernel,
        out_shape=(
            shape(width, all_bins),
            shape(tile_rows + 2 * MARGIN, channels, dtype=F32),
            shape(near_bins, channels, dtype=F32),
        ),
        in_specs=[vmem] * (2 + len(sources)),
        out_specs=(vmem,) * 3,
        scratch_shapes=[
            pltpu.VMEM((all_bins, width), BF16),
            pltpu.VMEM((all_bins + 2 * MARGIN, channels), F32),
            pltpu.VMEM((all_bins + tail + 2 * MARGIN, channels), F32),
        ],
        compiler_params=PARAMS,
        name="prepare",
    )(projection, context_key, *sources)
    from_even, from_odd, key = lax.optimization_barrier((from_even, from_odd, key))
    corner = shape(2, EDGES, SIDE, channels)
    sides, corner_to_core, corner_to_chip = pl.pallas_call(
        corner_kernel,
        out_shape=(shape(2, EDGES, tile_rows, channels), corner, corner),
        in_specs=[vmem] * 2,
        out_specs=(vmem,) * 3,
        compiler_params=PARAMS,
        name="corners",
    )(from_even, from_odd)
    corner_chip = lax.ppermute(corner_to_chip, ROW, odd_rows + ends)
    corner_core = lax.ppermute(corner_to_core, "core", other_core)


    total_rows = 9 * channels + 2 * all_bins + tail
    staged = (row_count, col_count) == (4, 8) and total_rows % 128 == 0
    if staged:
        parts, half = 4, total_rows // 2
    else:
        parts, half = 1, -(-total_rows // (32 * chips)) * 16 * chips
    span = tile_rows * PITCH
    inner = pl.pallas_call(
        inner_kernel,
        out_shape=(
            shape(span, 3 * channels), shape(span, 3 * channels), shape(span, channels), shape(*pair_input.shape),
        ),
        in_specs=[vmem] * 8,
        out_specs=(vmem,) * 4,
        scratch_shapes=[pltpu.VMEM((span + 4 * PAD, channels), F32)] * 2,
        compiler_params=PARAMS,
        name="inner",
    )(pair_input, cotangent, sides, query, key, window, rows_valid, forward)
    pair_output, pair_grad, keep, send = pl.pallas_call(
        outer_kernel,
        out_shape=(
            shape(*pair_input.shape),
            shape(*pair_input.shape),
            shape(parts, half // parts, channels, dtype=F32),
            shape(parts, half // parts, channels),
        ),
        in_specs=[vmem] * 17,
        out_specs=(anywhere, anywhere, vmem, vmem),
        scratch_shapes=[
            pltpu.VMEM((2, EDGES, tile_rows, channels), BF16),
            pltpu.VMEM((2, 2, EDGES, SIDE, channels), BF16),
            pltpu.VMEM((4 * PITCH + 4 * PAD, channels), F32),
            pltpu.VMEM((4 * PITCH + 4 * PAD, channels), F32),
            pltpu.VMEM((4 * PITCH, 3 * channels), BF16),
            pltpu.VMEM((4 * PITCH, 3 * channels), BF16),
            pltpu.VMEM((2 * PITCH, channels), BF16),
            pltpu.VMEM((2, band_cols, channels), BF16),
            pltpu.VMEM((8, tile_rows + band_cols, channels), F32),
            pltpu.VMEM((2 * half, channels), F32),
            pltpu.VMEM(pair_input.shape, BF16),
            pltpu.SemaphoreType.DMA((4,)),
        ],
        compiler_params=PARAMS,
        name="outer",
    )(
        pair_input, cotangent, from_core, from_chip, sides, corner_core, corner_chip, query, key, window, rows_valid,
        forward, backward, *inner,
    )

    halves = keep + lax.ppermute(send, "core", other_core).astype(F32)
    if staged:
        def across(values, bits):
            return lax.ppermute(values, ROW + ("col",), [(index, index ^ bits) for index in range(32)])

        plane = (1, 16, 17)
        got = [across(halves[part].astype(BF16), bits).astype(F32) for part, bits in enumerate(plane, 1)]
        mine = (halves[0] + got[0] + got[1] + got[2]).astype(BF16)
        near, far, opposite = [across(mine, bits).astype(F32) for bits in (2, 4, 6)]
        mine = ((mine.astype(F32) + near) + (far + opposite)).astype(BF16)
        mine = jnp.stack([mine] + [across(mine, bits) for bits in plane])
    else:
        piece = half // chips
        pieces = lax.all_to_all(halves.astype(BF16).reshape(chips, piece, channels), CHIPS, 0, 0)
        copies = pl.pallas_call(
            add_kernel,
            out_shape=shape(chips, piece, channels),
            in_specs=[vmem],
            out_specs=vmem,
            compiler_params=PARAMS,
            name="add",
        )(pieces)
        mine = lax.all_to_all(copies, CHIPS, 0, 0).reshape(1, half, channels)
    theirs = lax.ppermute(mine, "core", other_core)

    feature_grad, proj_grad, conv_grad = pl.pallas_call(
        finish_kernel,
        out_shape=(
            shape(*bin_features.shape),
            shape(*proj_weight.shape, dtype=F32),
            shape(*conv_weight.shape, dtype=F32),
        ),
        in_specs=[vmem] * 5,
        out_specs=(anywhere,) * 3,
        scratch_shapes=[
            pltpu.VMEM((2 * half, channels), BF16),
            pltpu.VMEM(bin_features.shape, BF16),
            pltpu.VMEM(proj_weight.shape, F32),
            pltpu.VMEM(conv_weight.shape, F32),
            pltpu.SemaphoreType.DMA((3,)),
        ],
        compiler_params=PARAMS,
        name="finish",
    )(mine, theirs, features_turned, context_turned, projection)
    return (pair_output, pair_grad, feature_grad, proj_grad, conv_grad)


def solution(mesh):
    rows, cols = mesh.shape["row"], mesh.shape["col"]
    split = Mesh(mesh.devices.reshape(rows // 2, 2, cols), ("rx", "core", "col"))
    tile = P(ROW, "col", None)
    in_specs = (tile, P(ROW, None), P(), P(), P(), P(), tile)
    out_specs = (tile, tile, P(ROW, None), P(), P())
    return jax.shard_map(body, mesh=split, in_specs=in_specs, out_specs=out_specs, check_vma=False)
```

```python
import jax
import jax.numpy as jnp
from jax import lax
from jax.experimental import pallas as pl
from jax.experimental.pallas import tpu as pltpu
from jax.sharding import Mesh, PartitionSpec as P

ROW = ("rx", "core")
CHIPS = ("rx", "col")
BF16 = jnp.bfloat16
F32 = jnp.float32
HALO = 2
EDGES = HALO + 1
SIDE = 16
MARGIN = 16
PITCH = 64
PAD = 8
PARAMS = pltpu.CompilerParams(vmem_limit_bytes=20 * 1024 * 1024)


def pack_kernel(
    pair, cot, features, to_core, to_chip, to_even, to_odd, pair_low, pair_high, cot_low, cot_high, own, work, sides, sems
):
    tile_rows, band_cols, channels = pair.shape
    odd_row = lax.rem(lax.axis_index(ROW), 2)
    odd_col = lax.rem(lax.axis_index("col"), 2)
    parts = [
        (pair.at[:, :SIDE], pair_low),
        (pair.at[:, band_cols - SIDE :], pair_high),
        (cot.at[:, :SIDE], cot_low),
        (cot.at[:, band_cols - SIDE :], cot_high),
        (features, own),
    ]
    for target, at_end in ((to_chip, odd_row), (to_core, 1 - odd_row)):
        parts.append((pair.at[pl.ds(at_end * (tile_rows - HALO), HALO)], target.at[:HALO]))
        parts.append((cot.at[pl.ds(at_end * (tile_rows - 1), 1)], target.at[HALO:EDGES]))
    copies = [pltpu.make_async_copy(source, target, sems.at[i]) for i, (source, target) in enumerate(parts)]
    for copy in copies:
        copy.start()
    for copy in copies[:4]:
        copy.wait()
    for side, (chunk, kind) in enumerate(((pair_low, cot_low), (pair_high, cot_high))):
        for slot, source, column in (
            (0, chunk, side * (SIDE - 2)), (1, chunk, side * (SIDE - 2) + 1), (2, kind, side * (SIDE - 1)),
        ):
            if slot != 1:
                work[...] = source[...].astype(F32).reshape(tile_rows * SIDE, channels)
            sides[side, slot] = work[pl.ds(column, tile_rows, stride=SIDE), :].astype(BF16)
    to_even[...] = sides[1 - odd_col]
    to_odd[...] = sides[odd_col]
    copies[4].wait()
    for part in range(features.shape[1] // channels):
        values = own[:, part * channels : (part + 1) * channels]
        to_chip[EDGES + part] = values
        to_core[EDGES + part] = values
    for copy in copies[5:]:
        copy.wait()


def corner_kernel(from_even, from_odd, sides, to_core, to_chip):
    tile_rows = from_even.shape[1]
    odd_row = lax.rem(lax.axis_index(ROW), 2)
    odd_col = lax.rem(lax.axis_index("col"), 2)
    sides[1 - odd_col] = from_even[...]
    sides[odd_col] = from_odd[...]
    for target, at_end in ((to_chip, odd_row), (to_core, 1 - odd_row)):
        start = pl.multiple_of(at_end * (tile_rows - SIDE), 16)
        target[...] = sides[:, :, pl.ds(start, SIDE), :]


def weights_kernel(
    valid, context, proj_weight, conv_weight,
    window, rows_valid, forward, backward, projection, context_key,
):
    channels = window.shape[1]
    bins = valid.shape[0]
    band_total = context.shape[0]
    all_bins = bins - band_total
    tile_rows = all_bins // lax.axis_size(ROW)
    row_start = lax.axis_index(ROW) * tile_rows
    col_start = row_start + lax.axis_index("col") * (band_total // lax.axis_size("col"))
    flags = jnp.broadcast_to(valid[...].reshape(1, bins).astype(F32).astype(BF16), (channels, bins))
    flip = (((1,), (1,)), ((), ()))
    for target, begin, stop in ((window, col_start - MARGIN, bins), (rows_valid, row_start - HALO, all_bins)):
        shape = (target.shape[0], bins)
        bin_index = lax.broadcasted_iota(jnp.int32, shape, 1)
        chosen = jnp.logical_and(bin_index == lax.broadcasted_iota(jnp.int32, shape, 0) + begin, bin_index < stop)
        target[...] = lax.dot_general(chosen.astype(F32).astype(BF16), flags, flip, preferred_element_type=F32)
    forward[...] = jnp.zeros(forward.shape, BF16)
    backward[...] = jnp.zeros(backward.shape, BF16)
    for tap in range(9):
        row_step, step = tap // 3 - 1, tap % 3
        values = conv_weight[tap]
        turned = values.astype(F32).T.astype(BF16)
        for out in range(2):
            lanes = slice(out * channels, (out + 1) * channels)
            at = ((row_step + 1 + out) * 3 + step) * channels
            forward[at : at + channels, lanes] = values
            at = ((1 - row_step + out) * 3 + step) * channels
            backward[at : at + channels, lanes] = turned
    projection[...] = proj_weight[...]
    context_key[...] = jnp.dot(context[...], proj_weight[:, channels:], preferred_element_type=F32).astype(BF16)


def prepare_kernel(projection, context_key, *refs):
    sources, (features, query, key, query_rows, key_rows) = refs[:-5], refs[-5:]
    channels = query.shape[1]
    all_bins, tail = features.shape[0], context_key.shape[0]
    row, col = lax.axis_index(ROW), lax.axis_index("col")
    if len(sources) == 1:
        features[...] = sources[0][...]
    else:
        for source, step in zip(sources, (0, 1, 3, 2)):
            rows = source.shape[1]
            start = pl.multiple_of(lax.bitwise_xor(row, step) * rows, 16)
            for part in range(source.shape[0] - EDGES):
                features[pl.ds(start, rows), part * channels : (part + 1) * channels] = source[EDGES + part]
    tile_rows = query.shape[0] - 2 * MARGIN
    row_start = row * tile_rows
    col_start = row_start + col * (key.shape[0] - 2 * MARGIN - tile_rows)
    proj = jnp.dot(features[...], projection[...], preferred_element_type=F32).astype(BF16).astype(F32)
    margin = jnp.zeros((MARGIN, channels), F32)
    for target, size in ((query_rows, all_bins), (key_rows, all_bins + tail)):
        target[:MARGIN, :] = margin
        target[MARGIN + size :, :] = margin
    query_rows[MARGIN : MARGIN + all_bins, :] = proj[:, :channels]
    key_rows[MARGIN : MARGIN + all_bins, :] = proj[:, channels:]
    key_rows[MARGIN + all_bins : MARGIN + all_bins + tail, :] = context_key[...].astype(F32)
    query[...] = query_rows[pl.ds(pl.multiple_of(row_start, 16), query.shape[0]), :]
    key[...] = key_rows[pl.ds(pl.multiple_of(col_start, 16), key.shape[0]), :]


def half_of(parts):
    core = lax.axis_index("core")
    if parts == 1:
        return core
    return lax.rem(core + lax.axis_index("rx") + lax.axis_index("col"), 2)


def quarter_of(parts):
    if parts == 1:
        return 0
    return 2 * lax.axis_index("rx") + lax.rem(lax.axis_index("col"), 2)


def spread(source, target, first, last, base, sign):
    channels = source.shape[1]
    for index in range(first, last):
        start = (index - base) * PITCH
        for step in range(3):
            target[start : start + PITCH, step * channels : (step + 1) * channels] = source[
                pl.ds(PAD + start + sign * (step - 1), PITCH), :
            ].astype(BF16)


def rows_of(sources, index):
    for array, base, held in sources:
        if index in held:
            return array[(index - base) * PITCH : (index - base + 1) * PITCH, :]
    raise IndexError(index)


def four_rows(sources, first, pairs):
    columns = []
    for step in range(4):
        parts = [rows_of(sources, first + 2 * index + step - 1) for index in range(pairs)]
        columns.append(jnp.concatenate(parts, axis=0))
    return jnp.concatenate(columns, axis=1)


def silu_parts(conv):
    sigma = 0.5 + 0.5 * jnp.tanh(0.5 * conv)
    return conv * sigma, sigma * (1.0 + conv * (1.0 - sigma))


def has_sides():
    col = lax.axis_index("col")
    return (col > 0).astype(F32), (col < lax.axis_size("col") - 1).astype(F32)


def keep_inner(values, band_cols):
    spot = lax.broadcasted_iota(jnp.int32, values.shape, 0)
    inner = jnp.logical_and(spot >= PAD, spot < PAD + band_cols)
    return jnp.where(inner, values, 0.0).astype(BF16)


def inner_kernel(
    pair, cot, sides, query, key, window, rows_valid, forward,
    mixed3, carry3, own, active,
    mixed, carry,
):
    tile_rows, band_cols, channels = pair.shape

    def place(index, column):
        return PAD + index * PITCH + PAD + column

    def mask_of(index):
        return window[pl.ds(MARGIN + index, band_cols), :] * rows_valid[pl.ds(index + HALO, 1), :]

    gap = jnp.zeros((PITCH - band_cols, channels), F32)
    mixed[:PAD, :] = jnp.zeros((PAD, channels), F32)
    mixed[PAD : 2 * PAD, :] = jnp.zeros((PAD, channels), F32)
    for index in range(tile_rows):
        mixed[pl.ds(place(index, band_cols), PITCH - band_cols), :] = gap
        carry[pl.ds(place(index, band_cols), PITCH - band_cols), :] = gap
    for index in range(tile_rows):
        mask = mask_of(index)
        value = mask * (
            pair[index].astype(F32) + query[pl.ds(MARGIN + index, 1), :] + key[pl.ds(MARGIN + index, band_cols), :]
        )
        mixed[pl.ds(place(index, 0), band_cols), :] = value
        carry[pl.ds(place(index, 0), band_cols), :] = mask * cot[index].astype(F32)
    has_low, has_high = has_sides()
    for column, side, slot, has in (
        (-2, 0, 0, has_low), (-1, 0, 1, has_low), (band_cols, 1, 0, has_high), (band_cols + 1, 1, 1, has_high),
    ):
        begin = MARGIN + column
        mask = rows_valid[pl.ds(HALO, tile_rows), :] * window[pl.ds(begin, tile_rows), :] * has
        value = sides[side, slot].astype(F32) + query[pl.ds(MARGIN, tile_rows), :] + key[pl.ds(begin, tile_rows), :]
        mixed[pl.ds(place(0, column), tile_rows, stride=PITCH), :] = mask * value
        if column in (-1, band_cols):
            carry[pl.ds(place(0, column), tile_rows, stride=PITCH), :] = mask * sides[side, HALO].astype(F32)
    spread(mixed, mixed3, 0, tile_rows, 0, 1)

    first, last = 1, tile_rows - 1
    sources = [(mixed3, 0, range(tile_rows))]
    while first < last:
        pairs = min(5, (last - first) // 2)
        conv = jnp.dot(four_rows(sources, first, pairs), forward[...], preferred_element_type=F32)
        activated, slope = silu_parts(conv)
        for offset in range(2 * pairs):
            index = first + offset
            lanes = slice(offset % 2 * channels, (offset % 2 + 1) * channels)
            at = offset // 2 * PITCH
            here = pl.ds(PAD + index * PITCH, PITCH)
            values = carry[here, :] * slope[at : at + PITCH, lanes]
            carry[here, :] = values
            own[index * PITCH : (index + 1) * PITCH, :] = keep_inner(values, band_cols)
            active[index] = activated[at + PAD : at + PAD + band_cols, lanes]
        first += 2 * pairs
    spread(carry, carry3, 1, tile_rows - 1, 0, -1)


def outer_kernel(
    pair, cot, from_core, from_chip, sides, corner_core, corner_chip, query, key, window, rows_valid, forward, backward,
    mixed3, carry3, own,
    active_ends, change, keep, send,
    near, corners, mixed, carry, mixed3_ends, carry3_ends, own_ends, skew, totals,
):
    tile_rows, band_cols, channels = pair.shape
    row, col = lax.axis_index(ROW), lax.axis_index("col")
    all_bins = lax.axis_size(ROW) * tile_rows
    tail = lax.axis_size("col") * band_cols
    row_start = row * tile_rows
    col_start = row_start + col * band_cols
    odd_row = lax.rem(row, 2)
    last = tile_rows - 1
    near[1 - odd_row] = from_core[:EDGES]
    near[odd_row] = from_chip[:EDGES]
    corners[1 - odd_row] = corner_core[...]
    corners[odd_row] = corner_chip[...]

    def place(position, column):
        return PAD + position * PITCH + PAD + column

    def mask_of(index):
        return window[pl.ds(MARGIN + index, band_cols), :] * rows_valid[pl.ds(index + HALO, 1), :]

    has = has_sides()
    mixed_rows = (-2, -1, tile_rows, tile_rows + 1)
    carry_rows = (-1, 0, last, tile_rows)
    gap = jnp.zeros((PITCH - band_cols, channels), F32)
    for array in (mixed, carry):
        array[: 2 * PAD, :] = jnp.zeros((2 * PAD, channels), F32)
        for position in range(4):
            array[pl.ds(place(position, band_cols), PITCH - band_cols), :] = gap

    def corner_of(index, side, slot):
        if index < 0:
            return corners[0, side, slot].astype(F32)[SIDE + index : SIDE + index + 1, :]
        return corners[1, side, slot].astype(F32)[index - tile_rows : index - tile_rows + 1, :]

    def pixel_mask(index, column, side):
        return rows_valid[pl.ds(index + HALO, 1), :] * window[pl.ds(MARGIN + index + column, 1), :] * has[side]

    for position, index in enumerate(mixed_rows):
        source = near[0, HALO + index] if index < 0 else near[1, index - tile_rows]
        row_query = query[pl.ds(MARGIN + index, 1), :]
        mixed[pl.ds(place(position, 0), band_cols), :] = mask_of(index) * (
            source.astype(F32) + row_query + key[pl.ds(MARGIN + index, band_cols), :]
        )
        for column, side, slot in ((-2, 0, 0), (-1, 0, 1), (band_cols, 1, 0), (band_cols + 1, 1, 1)):
            value = corner_of(index, side, slot) + row_query + key[pl.ds(MARGIN + index + column, 1), :]
            mixed[pl.ds(place(position, column), 1), :] = pixel_mask(index, column, side) * value
    for position, index in enumerate(carry_rows):
        source = near[0, HALO] if index < 0 else near[1, HALO] if index > last else cot[index]
        carry[pl.ds(place(position, 0), band_cols), :] = mask_of(index) * source.astype(F32)
        for column, side in ((-1, 0), (band_cols, 1)):
            if 0 <= index <= last:
                chunk = index // SIDE * SIDE
                value = sides[side, HALO, chunk : chunk + SIDE].astype(F32)[index - chunk : index - chunk + 1, :]
            else:
                value = corner_of(index, side, HALO)
            carry[pl.ds(place(position, column), 1), :] = pixel_mask(index, column, side) * value
    spread(mixed, mixed3_ends, 0, 4, 0, 1)
    mixed_sources = [
        (mixed3, 0, range(tile_rows)), (mixed3_ends, -2, (-2, -1)), (mixed3_ends, tile_rows - 2, (tile_rows, tile_rows + 1)),
    ]
    ends = jnp.concatenate([four_rows(mixed_sources, -1, 1), four_rows(mixed_sources, last, 1)], axis=0)
    activated, slope = silu_parts(jnp.dot(ends, forward[...], preferred_element_type=F32))
    for position, index in enumerate(carry_rows):
        lanes = slice(position % 2 * channels, (position % 2 + 1) * channels)
        at = position // 2 * PITCH
        here = pl.ds(PAD + position * PITCH, PITCH)
        values = carry[here, :] * slope[at : at + PITCH, lanes]
        carry[here, :] = values
        if 0 <= index <= last:
            half = position // 2
            own_ends[half * PITCH : (half + 1) * PITCH, :] = keep_inner(values, band_cols)
            active_ends[half] = activated[at + PAD : at + PAD + band_cols, lanes]
    spread(carry, carry3_ends, 0, 4, 0, -1)
    carry_sources = [
        (carry3, 0, range(1, last)), (carry3_ends, -1, (-1, 0)), (carry3_ends, tile_rows - 3, (last, tile_rows)),
    ]
    own_sources = [(own, 0, range(1, last)), (own_ends, 0, (0,)), (own_ends, tile_rows - 2, (last,))]

    totals[...] = jnp.zeros(totals.shape, F32)
    skew[...] = jnp.zeros(skew.shape, F32)
    pairs = 4
    query_at = 9 * channels + all_bins + tail
    query_rows = []
    for first in range(0, tile_rows, 2 * pairs):
        back = jnp.dot(four_rows(carry_sources, first, pairs), backward[...], preferred_element_type=F32)
        for offset in range(2 * pairs):
            index = first + offset
            lanes = slice(offset % 2 * channels, (offset % 2 + 1) * channels)
            at = offset // 2 * PITCH + PAD
            masked = mask_of(index) * back[at : at + band_cols, lanes]
            change[index] = masked
            query_rows.append(jnp.sum(masked, axis=0, keepdims=True))
            skew[index % 8, index - index % 8 : index - index % 8 + band_cols, :] += masked
    totals[pl.ds(pl.multiple_of(query_at + row_start, 16), tile_rows), :] = jnp.concatenate(query_rows, axis=0)
    reach = tile_rows + band_cols - 8
    for step in range(8):
        totals[pl.ds(9 * channels + col_start + step, reach), :] += skew[step, :reach, :]

    per = 12
    grads = jnp.zeros((channels, 9 * channels), F32)
    for first in range(0, tile_rows, per):
        around = jnp.concatenate(
            [
                jnp.concatenate([rows_of(mixed_sources, index + step) for index in range(first, first + per)], axis=0)
                for step in (-1, 0, 1)
            ],
            axis=1,
        )
        cots = jnp.concatenate([rows_of(own_sources, index) for index in range(first, first + per)], axis=0)
        grads = grads + lax.dot_general(cots, around, (((0,), (0,)), ((), ())), preferred_element_type=F32)
    for tap in range(9):
        totals[tap * channels : (tap + 1) * channels, :] = grads[:, tap * channels : (tap + 1) * channels]
    parts, size = keep.shape[:2]
    mine = half_of(parts)
    for part in range(parts):
        place = lax.bitwise_xor(quarter_of(parts), part)
        keep[part] = totals[pl.ds(pl.multiple_of((mine * parts + place) * size, 16), size), :]
        send[part] = totals[pl.ds(pl.multiple_of(((1 - mine) * parts + place) * size, 16), size), :].astype(BF16)


def late_kernel(
    pair, cot, active, active_ends, change, window, rows_valid, features, context,
    pair_output, pair_grad, features_turned, context_turned,
):
    tile_rows, band_cols, _ = pair.shape
    last = tile_rows - 1
    for index in range(tile_rows):
        mask = window[pl.ds(MARGIN + index, band_cols), :] * rows_valid[pl.ds(index + HALO, 1), :]
        values = active_ends[0] if index == 0 else active_ends[1] if index == last else active[index]
        pair_output[index] = (pair[index].astype(F32) + mask * values).astype(BF16)
        pair_grad[index] = (cot[index].astype(F32) + change[index]).astype(BF16)
    features_turned[...] = features[...].astype(F32).T.astype(BF16)
    context_turned[...] = context[...].astype(F32).T.astype(BF16)


def add_kernel(pieces, copies):
    total = pieces[0].astype(F32)
    for index in range(1, pieces.shape[0]):
        total = total + pieces[index].astype(F32)
    copies[...] = jnp.broadcast_to(total.astype(BF16), copies.shape)


def finish_kernel(
    features_turned, context_turned, projection, *refs
):
    *pieces, feature_grad, proj_grad, conv_grad, whole, feature_out, proj_out, conv_out, sems = refs
    parts = len(pieces) // 2
    mine, theirs = pieces[:parts], pieces[parts:]
    row = lax.axis_index(ROW)
    size, channels = mine[0].shape
    all_bins, tail = features_turned.shape[1], context_turned.shape[1]
    tile_rows = feature_grad.shape[0]
    half = half_of(parts)
    for part in range(parts):
        place = lax.bitwise_xor(quarter_of(parts), part)
        whole[pl.ds(pl.multiple_of((half * parts + place) * size, 16), size), :] = mine[part][...]
        whole[pl.ds(pl.multiple_of(((1 - half) * parts + place) * size, 16), size), :] = theirs[part][...]
    copies = [
        pltpu.make_async_copy(source, target, sems.at[index])
        for index, (source, target) in enumerate(((conv_out, conv_grad), (proj_out, proj_grad), (feature_out, feature_grad)))
    ]
    for tap in range(9):
        conv_out[tap] = whole[tap * channels : (tap + 1) * channels, :].astype(F32).T
    copies[0].start()
    key_at = 9 * channels
    query_at = key_at + all_bins + tail
    own = features_turned[...]
    proj_out[:, :channels] = jnp.dot(own, whole[query_at : query_at + all_bins, :], preferred_element_type=F32)
    proj_out[:, channels:] = jnp.dot(
        own, whole[key_at : key_at + all_bins, :], preferred_element_type=F32
    ) + jnp.dot(context_turned[...], whole[key_at + all_bins : query_at, :], preferred_element_type=F32)
    copies[1].start()
    start = pl.multiple_of(row * tile_rows, 16)
    both = jnp.concatenate(
        [whole[pl.ds(query_at + start, tile_rows), :], whole[pl.ds(key_at + start, tile_rows), :]], axis=1
    )
    feature_out[...] = lax.dot_general(
        both, projection[...], (((1,), (1,)), ((), ())), preferred_element_type=F32
    ).astype(BF16)
    copies[2].start()
    for copy in copies:
        copy.wait()


def in_hbm(*arrays):
    return [pltpu.with_memory_space_constraint(array, pltpu.HBM) for array in arrays]


def body(
    pair_input, bin_features, context_features, proj_weight, conv_weight, valid_bins, cotangent
):
    tile_rows, band_cols, channels = pair_input.shape
    width = bin_features.shape[1]
    row_count = lax.axis_size(ROW)
    col_count = lax.axis_size("col")
    all_bins = tile_rows * row_count
    tail = context_features.shape[0]
    chips = row_count * col_count // 2
    taken = -(-(tile_rows + 2 * HALO) // 8) * 8
    vmem = pl.BlockSpec(memory_space=pltpu.VMEM)
    anywhere = pl.BlockSpec(memory_space=pl.ANY)

    def shape(*dims, dtype=BF16):
        return jax.ShapeDtypeStruct(dims, dtype)

    layers = EDGES + width // channels
    chunk = pltpu.VMEM((tile_rows, SIDE, channels), BF16)
    to_core, to_chip, to_even, to_odd = pl.pallas_call(
        pack_kernel,
        out_shape=(
            shape(layers, tile_rows, channels),
            shape(layers, tile_rows, channels),
            shape(EDGES, tile_rows, channels),
            shape(EDGES, tile_rows, channels),
        ),
        in_specs=[anywhere] * 3,
        out_specs=(vmem,) * 4,
        scratch_shapes=[
            chunk, chunk, chunk, chunk,
            pltpu.VMEM(bin_features.shape, BF16),
            pltpu.VMEM((tile_rows * SIDE, channels), F32),
            pltpu.VMEM((2, EDGES, tile_rows, channels), BF16),
            pltpu.SemaphoreType.DMA((9,)),
        ],
        compiler_params=PARAMS,
        name="pack",
    )(*in_hbm(pair_input, cotangent, bin_features))
    other_core = [(0, 1), (1, 0)]
    even_cols = [(i, i ^ 1) for i in range(col_count) if i ^ 1 < col_count]
    odd_cols = []
    for row in range(row_count):
        for column in range(col_count):
            partner = ((column + 1) ^ 1) - 1
            if 0 <= partner < col_count:
                odd_cols.append((row * col_count + column, row * col_count + partner))
            else:
                odd_cols.append((row * col_count + column, (row ^ 1) * col_count + column))
    odd_rows = [(i, ((i + 1) ^ 1) - 1) for i in range(1, row_count - 1)]
    ends = [(0, 3), (3, 0)] if row_count == 4 else []
    from_chip = lax.ppermute(to_chip, ROW, odd_rows + ends)
    from_odd = lax.ppermute(to_odd, ROW + ("col",), odd_cols)
    from_even = lax.ppermute(to_even, "col", even_cols)
    from_core = lax.ppermute(to_core, "core", other_core)
    near_bins = tile_rows + band_cols + 2 * MARGIN
    valid_bins, from_chip = lax.optimization_barrier((valid_bins, from_chip))
    window, rows_valid, forward, backward, projection, context_key = pl.pallas_call(
        weights_kernel,
        out_shape=(
            shape(near_bins, channels, dtype=F32),
            shape(taken, channels, dtype=F32),
            shape(12 * channels, 2 * channels),
            shape(12 * channels, 2 * channels),
            shape(*proj_weight.shape),
            shape(tail, channels),
        ),
        in_specs=[vmem] * 4,
        out_specs=(vmem,) * 6,
        compiler_params=PARAMS,
        cost_estimate=pl.CostEstimate(flops=1 << 30, bytes_accessed=1 << 21, transcendentals=0),
        name="weights",
    )(*in_hbm(valid_bins, context_features, proj_weight, conv_weight))
    if row_count == 4:
        sources = [to_core, from_core, from_chip, lax.ppermute(from_chip, "core", other_core)]
    else:
        sources = [lax.all_gather(bin_features, ROW, axis=0, tiled=True)]

    features, query, key = pl.pallas_call(
        prepare_kernel,
        out_shape=(
            shape(all_bins, width),
            shape(tile_rows + 2 * MARGIN, channels, dtype=F32),
            shape(near_bins, channels, dtype=F32),
        ),
        in_specs=[vmem] * (2 + len(sources)),
        out_specs=(vmem,) * 3,
        scratch_shapes=[
            pltpu.VMEM((all_bins + 2 * MARGIN, channels), F32),
            pltpu.VMEM((all_bins + tail + 2 * MARGIN, channels), F32),
        ],
        compiler_params=PARAMS,
        name="prepare",
    )(projection, context_key, *sources)
    from_even, from_odd, key = lax.optimization_barrier((from_even, from_odd, key))
    corner = shape(2, EDGES, SIDE, channels)
    sides, corner_to_core, corner_to_chip = pl.pallas_call(
        corner_kernel,
        out_shape=(shape(2, EDGES, tile_rows, channels), corner, corner),
        in_specs=[vmem] * 2,
        out_specs=(vmem,) * 3,
        compiler_params=PARAMS,
        name="corners",
    )(from_even, from_odd)
    corner_chip = lax.ppermute(corner_to_chip, ROW, odd_rows + ends)
    corner_core = lax.ppermute(corner_to_core, "core", other_core)


    total_rows = 9 * channels + 2 * all_bins + tail
    staged = (row_count, col_count) == (4, 8) and total_rows % 128 == 0
    if staged:
        parts, half = 4, total_rows // 2
    else:
        parts, half = 1, -(-total_rows // (32 * chips)) * 16 * chips
    span = tile_rows * PITCH
    *inner, active = pl.pallas_call(
        inner_kernel,
        out_shape=(
            shape(span, 3 * channels), shape(span, 3 * channels), shape(span, channels),
            shape(*pair_input.shape, dtype=F32),
        ),
        in_specs=[vmem] * 8,
        out_specs=(vmem,) * 4,
        scratch_shapes=[pltpu.VMEM((span + 4 * PAD, channels), F32)] * 2,
        compiler_params=PARAMS,
        name="inner",
    )(pair_input, cotangent, sides, query, key, window, rows_valid, forward)
    active_ends, change, keep, send = pl.pallas_call(
        outer_kernel,
        out_shape=(
            shape(2, band_cols, channels, dtype=F32),
            shape(*pair_input.shape, dtype=F32),
            shape(parts, half // parts, channels, dtype=F32),
            shape(parts, half // parts, channels),
        ),
        in_specs=[vmem] * 16,
        out_specs=(vmem,) * 4,
        scratch_shapes=[
            pltpu.VMEM((2, EDGES, tile_rows, channels), BF16),
            pltpu.VMEM((2, 2, EDGES, SIDE, channels), BF16),
            pltpu.VMEM((4 * PITCH + 4 * PAD, channels), F32),
            pltpu.VMEM((4 * PITCH + 4 * PAD, channels), F32),
            pltpu.VMEM((4 * PITCH, 3 * channels), BF16),
            pltpu.VMEM((4 * PITCH, 3 * channels), BF16),
            pltpu.VMEM((2 * PITCH, channels), BF16),
            pltpu.VMEM((8, tile_rows + band_cols, channels), F32),
            pltpu.VMEM((2 * half, channels), F32),
        ],
        compiler_params=PARAMS,
        name="outer",
    )(
        pair_input, cotangent, from_core, from_chip, sides, corner_core, corner_chip, query, key, window, rows_valid,
        forward, backward, *inner,
    )
    pair_output, pair_grad, features_turned, context_turned = pl.pallas_call(
        late_kernel,
        out_shape=(
            shape(*pair_input.shape), shape(*pair_input.shape), shape(width, all_bins), shape(width, tail),
        ),
        in_specs=[vmem] * 9,
        out_specs=(vmem,) * 4,
        compiler_params=PARAMS,
        name="late",
    )(
        pair_input, cotangent, active, active_ends, change, window, rows_valid, features,
        *in_hbm(context_features),
    )

    halves = keep + lax.ppermute(send, "core", other_core).astype(F32)
    if staged:
        def across(values, bits):
            return lax.ppermute(values, ROW + ("col",), [(index, index ^ bits) for index in range(32)])

        plane = (1 + 8, 16 + 8, 16 + 1)
        got = [across(halves[part].astype(BF16), bits).astype(F32) for part, bits in enumerate(plane, 1)]
        mine = (halves[0] + got[0] + got[1] + got[2]).astype(BF16)
        near, far, opposite = [across(mine, bits) for bits in (2, 4, 6)]
        far, pair_output = lax.optimization_barrier((far, pair_output))
        near, far, opposite = near.astype(F32), far.astype(F32), opposite.astype(F32)
        mine = ((mine.astype(F32) + near) + (far + opposite)).astype(BF16)
        mine = [mine] + [across(mine, bits) for bits in plane]
    else:
        piece = half // chips
        pieces = lax.all_to_all(halves.astype(BF16).reshape(chips, piece, channels), CHIPS, 0, 0)
        copies = pl.pallas_call(
            add_kernel,
            out_shape=shape(chips, piece, channels),
            in_specs=[vmem],
            out_specs=vmem,
            compiler_params=PARAMS,
            name="add",
        )(pieces)
        mine = [lax.all_to_all(copies, CHIPS, 0, 0).reshape(half, channels)]
    theirs = [lax.ppermute(part, "core", other_core) for part in mine]

    feature_grad, proj_grad, conv_grad = pl.pallas_call(
        finish_kernel,
        out_shape=(
            shape(*bin_features.shape),
            shape(*proj_weight.shape, dtype=F32),
            shape(*conv_weight.shape, dtype=F32),
        ),
        in_specs=[vmem] * (3 + 2 * len(mine)),
        out_specs=(anywhere,) * 3,
        scratch_shapes=[
            pltpu.VMEM((2 * half, channels), BF16),
            pltpu.VMEM(bin_features.shape, BF16),
            pltpu.VMEM(proj_weight.shape, F32),
            pltpu.VMEM(conv_weight.shape, F32),
            pltpu.SemaphoreType.DMA((3,)),
        ],
        compiler_params=PARAMS,
        name="finish",
    )(features_turned, context_turned, projection, *mine, *theirs)
    return (pair_output, pair_grad, feature_grad, proj_grad, conv_grad)


def solution(mesh):
    rows, cols = mesh.shape["row"], mesh.shape["col"]
    split = Mesh(mesh.devices.reshape(rows // 2, 2, cols), ("rx", "core", "col"))
    tile = P(ROW, "col", None)
    in_specs = (tile, P(ROW, None), P(), P(), P(), P(), tile)
    out_specs = (tile, tile, P(ROW, None), P(), P())
    return jax.shard_map(body, mesh=split, in_specs=in_specs, out_specs=out_specs, check_vma=False)
```

```python
import jax
import jax.numpy as jnp
from jax import lax
from jax.experimental import pallas as pl
from jax.experimental.pallas import tpu as pltpu
from jax.sharding import Mesh, PartitionSpec as P

ROW = ("rx", "core")
CHIPS = ("rx", "col")
BF16 = jnp.bfloat16
F32 = jnp.float32
HALO = 2
EDGES = HALO + 1
SIDE = 16
MARGIN = 16
PITCH = 64
PAD = 8
PARAMS = pltpu.CompilerParams(vmem_limit_bytes=20 * 1024 * 1024)


def pack_kernel(
    pair, cot, features, context_in, proj_weight_in, conv_weight_in, valid_in,
    to_core, to_chip, to_even, to_odd, context, proj_weight, conv_weight, valid, pair_low, pair_high, cot_low, cot_high, own, work, sides, sems
):
    tile_rows, band_cols, channels = pair.shape
    odd_row = lax.rem(lax.axis_index(ROW), 2)
    odd_col = lax.rem(lax.axis_index("col"), 2)
    parts = [
        (pair.at[:, :SIDE], pair_low),
        (pair.at[:, band_cols - SIDE :], pair_high),
        (cot.at[:, :SIDE], cot_low),
        (cot.at[:, band_cols - SIDE :], cot_high),
        (features, own),
    ]
    for target, at_end in ((to_chip, odd_row), (to_core, 1 - odd_row)):
        parts.append((pair.at[pl.ds(at_end * (tile_rows - HALO), HALO)], target.at[:HALO]))
        parts.append((cot.at[pl.ds(at_end * (tile_rows - 1), 1)], target.at[HALO:EDGES]))
    parts += [(context_in, context), (proj_weight_in, proj_weight), (conv_weight_in, conv_weight), (valid_in, valid)]
    copies = [pltpu.make_async_copy(source, target, sems.at[i]) for i, (source, target) in enumerate(parts)]
    for copy in copies:
        copy.start()
    for copy in copies[:4]:
        copy.wait()
    for side, (chunk, kind) in enumerate(((pair_low, cot_low), (pair_high, cot_high))):
        for slot, source, column in (
            (0, chunk, side * (SIDE - 2)), (1, chunk, side * (SIDE - 2) + 1), (2, kind, side * (SIDE - 1)),
        ):
            if slot != 1:
                work[...] = source[...].astype(F32).reshape(tile_rows * SIDE, channels)
            sides[side, slot] = work[pl.ds(column, tile_rows, stride=SIDE), :].astype(BF16)
    to_even[...] = sides[1 - odd_col]
    to_odd[...] = sides[odd_col]
    copies[4].wait()
    for part in range(features.shape[1] // channels):
        values = own[:, part * channels : (part + 1) * channels]
        to_chip[EDGES + part] = values
        to_core[EDGES + part] = values
    for copy in copies[5:]:
        copy.wait()


def corner_kernel(from_even, from_odd, sides, to_core, to_chip):
    tile_rows = from_even.shape[1]
    odd_row = lax.rem(lax.axis_index(ROW), 2)
    odd_col = lax.rem(lax.axis_index("col"), 2)
    sides[1 - odd_col] = from_even[...]
    sides[odd_col] = from_odd[...]
    for target, at_end in ((to_chip, odd_row), (to_core, 1 - odd_row)):
        start = pl.multiple_of(at_end * (tile_rows - SIDE), 16)
        target[...] = sides[:, :, pl.ds(start, SIDE), :]


def weights_kernel(
    valid, context, proj_weight, conv_weight,
    window, rows_valid, forward, backward, context_key,
):
    channels = window.shape[1]
    bins = valid.shape[0]
    band_total = context.shape[0]
    all_bins = bins - band_total
    tile_rows = all_bins // lax.axis_size(ROW)
    row_start = lax.axis_index(ROW) * tile_rows
    col_start = row_start + lax.axis_index("col") * (band_total // lax.axis_size("col"))
    flags = jnp.broadcast_to(valid[...].reshape(1, bins).astype(F32).astype(BF16), (channels, bins))
    flip = (((1,), (1,)), ((), ()))
    for target, begin, stop in ((window, col_start - MARGIN, bins), (rows_valid, row_start - HALO, all_bins)):
        shape = (target.shape[0], bins)
        bin_index = lax.broadcasted_iota(jnp.int32, shape, 1)
        chosen = jnp.logical_and(bin_index == lax.broadcasted_iota(jnp.int32, shape, 0) + begin, bin_index < stop)
        target[...] = lax.dot_general(chosen.astype(F32).astype(BF16), flags, flip, preferred_element_type=F32)
    forward[...] = jnp.zeros(forward.shape, BF16)
    backward[...] = jnp.zeros(backward.shape, BF16)
    for tap in range(9):
        row_step, step = tap // 3 - 1, tap % 3
        values = conv_weight[tap]
        turned = values.astype(F32).T.astype(BF16)
        for out in range(2):
            lanes = slice(out * channels, (out + 1) * channels)
            at = ((row_step + 1 + out) * 3 + step) * channels
            forward[at : at + channels, lanes] = values
            at = ((1 - row_step + out) * 3 + step) * channels
            backward[at : at + channels, lanes] = turned
    context_key[...] = jnp.dot(context[...], proj_weight[:, channels:], preferred_element_type=F32).astype(BF16)


def prepare_kernel(projection, context_key, *refs):
    sources, (features, query, key, query_rows, key_rows) = refs[:-5], refs[-5:]
    channels = query.shape[1]
    all_bins, tail = features.shape[0], context_key.shape[0]
    row, col = lax.axis_index(ROW), lax.axis_index("col")
    if len(sources) == 1:
        features[...] = sources[0][...]
    else:
        for source, step in zip(sources, (0, 1, 3, 2)):
            rows = source.shape[1]
            start = pl.multiple_of(lax.bitwise_xor(row, step) * rows, 16)
            for part in range(source.shape[0] - EDGES):
                features[pl.ds(start, rows), part * channels : (part + 1) * channels] = source[EDGES + part]
    tile_rows = query.shape[0] - 2 * MARGIN
    row_start = row * tile_rows
    col_start = row_start + col * (key.shape[0] - 2 * MARGIN - tile_rows)
    proj = jnp.dot(features[...], projection[...], preferred_element_type=F32).astype(BF16).astype(F32)
    margin = jnp.zeros((MARGIN, channels), F32)
    for target, size in ((query_rows, all_bins), (key_rows, all_bins + tail)):
        target[:MARGIN, :] = margin
        target[MARGIN + size :, :] = margin
    query_rows[MARGIN : MARGIN + all_bins, :] = proj[:, :channels]
    key_rows[MARGIN : MARGIN + all_bins, :] = proj[:, channels:]
    key_rows[MARGIN + all_bins : MARGIN + all_bins + tail, :] = context_key[...].astype(F32)
    query[...] = query_rows[pl.ds(pl.multiple_of(row_start, 16), query.shape[0]), :]
    key[...] = key_rows[pl.ds(pl.multiple_of(col_start, 16), key.shape[0]), :]


def half_of(parts):
    core = lax.axis_index("core")
    if parts == 1:
        return core
    return lax.rem(core + lax.axis_index("rx") + lax.axis_index("col"), 2)


def quarter_of(parts):
    if parts == 1:
        return 0
    return 2 * lax.axis_index("rx") + lax.rem(lax.axis_index("col"), 2)


def spread(source, target, first, last, base, sign):
    channels = source.shape[1]
    for index in range(first, last):
        start = (index - base) * PITCH
        for step in range(3):
            target[start : start + PITCH, step * channels : (step + 1) * channels] = source[
                pl.ds(PAD + start + sign * (step - 1), PITCH), :
            ].astype(BF16)


def rows_of(sources, index):
    for array, base, held in sources:
        if index in held:
            return array[(index - base) * PITCH : (index - base + 1) * PITCH, :]
    raise IndexError(index)


def four_rows(sources, first, pairs):
    columns = []
    for step in range(4):
        parts = [rows_of(sources, first + 2 * index + step - 1) for index in range(pairs)]
        columns.append(jnp.concatenate(parts, axis=0))
    return jnp.concatenate(columns, axis=1)


def silu_parts(conv):
    sigma = 0.5 + 0.5 * jnp.tanh(0.5 * conv)
    return conv * sigma, sigma * (1.0 + conv * (1.0 - sigma))


def has_sides():
    col = lax.axis_index("col")
    return (col > 0).astype(F32), (col < lax.axis_size("col") - 1).astype(F32)


def keep_inner(values, band_cols):
    spot = lax.broadcasted_iota(jnp.int32, values.shape, 0)
    inner = jnp.logical_and(spot >= PAD, spot < PAD + band_cols)
    return jnp.where(inner, values, 0.0).astype(BF16)


def inner_kernel(
    pair, cot, sides, query, key, window, rows_valid, forward,
    mixed3, carry3, own, active,
    mixed, carry,
):
    tile_rows, band_cols, channels = pair.shape

    def place(index, column):
        return PAD + index * PITCH + PAD + column

    def mask_of(index):
        return window[pl.ds(MARGIN + index, band_cols), :] * rows_valid[pl.ds(index + HALO, 1), :]

    gap = jnp.zeros((PITCH - band_cols, channels), F32)
    mixed[:PAD, :] = jnp.zeros((PAD, channels), F32)
    mixed[PAD : 2 * PAD, :] = jnp.zeros((PAD, channels), F32)
    for index in range(tile_rows):
        mixed[pl.ds(place(index, band_cols), PITCH - band_cols), :] = gap
        carry[pl.ds(place(index, band_cols), PITCH - band_cols), :] = gap
    for index in range(tile_rows):
        mask = mask_of(index)
        value = mask * (
            pair[index].astype(F32) + query[pl.ds(MARGIN + index, 1), :] + key[pl.ds(MARGIN + index, band_cols), :]
        )
        mixed[pl.ds(place(index, 0), band_cols), :] = value
        carry[pl.ds(place(index, 0), band_cols), :] = mask * cot[index].astype(F32)
    has_low, has_high = has_sides()
    for column, side, slot, has in (
        (-2, 0, 0, has_low), (-1, 0, 1, has_low), (band_cols, 1, 0, has_high), (band_cols + 1, 1, 1, has_high),
    ):
        begin = MARGIN + column
        mask = rows_valid[pl.ds(HALO, tile_rows), :] * window[pl.ds(begin, tile_rows), :] * has
        value = sides[side, slot].astype(F32) + query[pl.ds(MARGIN, tile_rows), :] + key[pl.ds(begin, tile_rows), :]
        mixed[pl.ds(place(0, column), tile_rows, stride=PITCH), :] = mask * value
        if column in (-1, band_cols):
            carry[pl.ds(place(0, column), tile_rows, stride=PITCH), :] = mask * sides[side, HALO].astype(F32)
    spread(mixed, mixed3, 0, tile_rows, 0, 1)

    first, last = 1, tile_rows - 1
    sources = [(mixed3, 0, range(tile_rows))]
    while first < last:
        pairs = min(5, (last - first) // 2)
        conv = jnp.dot(four_rows(sources, first, pairs), forward[...], preferred_element_type=F32)
        activated, slope = silu_parts(conv)
        for offset in range(2 * pairs):
            index = first + offset
            lanes = slice(offset % 2 * channels, (offset % 2 + 1) * channels)
            at = offset // 2 * PITCH
            here = pl.ds(PAD + index * PITCH, PITCH)
            values = carry[here, :] * slope[at : at + PITCH, lanes]
            carry[here, :] = values
            own[index * PITCH : (index + 1) * PITCH, :] = keep_inner(values, band_cols)
            active[index] = activated[at + PAD : at + PAD + band_cols, lanes]
        first += 2 * pairs
    spread(carry, carry3, 1, tile_rows - 1, 0, -1)


def outer_kernel(
    pair, cot, from_core, from_chip, sides, corner_core, corner_chip, query, key, window, rows_valid, forward, backward,
    mixed3, carry3, own,
    active_ends, change, keep, send,
    near, corners, mixed, carry, mixed3_ends, carry3_ends, own_ends, skew, totals,
):
    tile_rows, band_cols, channels = pair.shape
    row, col = lax.axis_index(ROW), lax.axis_index("col")
    all_bins = lax.axis_size(ROW) * tile_rows
    tail = lax.axis_size("col") * band_cols
    row_start = row * tile_rows
    col_start = row_start + col * band_cols
    odd_row = lax.rem(row, 2)
    last = tile_rows - 1
    near[1 - odd_row] = from_core[:EDGES]
    near[odd_row] = from_chip[:EDGES]
    corners[1 - odd_row] = corner_core[...]
    corners[odd_row] = corner_chip[...]

    def place(position, column):
        return PAD + position * PITCH + PAD + column

    def mask_of(index):
        return window[pl.ds(MARGIN + index, band_cols), :] * rows_valid[pl.ds(index + HALO, 1), :]

    has = has_sides()
    mixed_rows = (-2, -1, tile_rows, tile_rows + 1)
    carry_rows = (-1, 0, last, tile_rows)
    gap = jnp.zeros((PITCH - band_cols, channels), F32)
    for array in (mixed, carry):
        array[: 2 * PAD, :] = jnp.zeros((2 * PAD, channels), F32)
        for position in range(4):
            array[pl.ds(place(position, band_cols), PITCH - band_cols), :] = gap

    def corner_of(index, side, slot):
        if index < 0:
            return corners[0, side, slot].astype(F32)[SIDE + index : SIDE + index + 1, :]
        return corners[1, side, slot].astype(F32)[index - tile_rows : index - tile_rows + 1, :]

    def pixel_mask(index, column, side):
        return rows_valid[pl.ds(index + HALO, 1), :] * window[pl.ds(MARGIN + index + column, 1), :] * has[side]

    for position, index in enumerate(mixed_rows):
        source = near[0, HALO + index] if index < 0 else near[1, index - tile_rows]
        row_query = query[pl.ds(MARGIN + index, 1), :]
        mixed[pl.ds(place(position, 0), band_cols), :] = mask_of(index) * (
            source.astype(F32) + row_query + key[pl.ds(MARGIN + index, band_cols), :]
        )
        for column, side, slot in ((-2, 0, 0), (-1, 0, 1), (band_cols, 1, 0), (band_cols + 1, 1, 1)):
            value = corner_of(index, side, slot) + row_query + key[pl.ds(MARGIN + index + column, 1), :]
            mixed[pl.ds(place(position, column), 1), :] = pixel_mask(index, column, side) * value
    for position, index in enumerate(carry_rows):
        source = near[0, HALO] if index < 0 else near[1, HALO] if index > last else cot[index]
        carry[pl.ds(place(position, 0), band_cols), :] = mask_of(index) * source.astype(F32)
        for column, side in ((-1, 0), (band_cols, 1)):
            if 0 <= index <= last:
                chunk = index // SIDE * SIDE
                value = sides[side, HALO, chunk : chunk + SIDE].astype(F32)[index - chunk : index - chunk + 1, :]
            else:
                value = corner_of(index, side, HALO)
            carry[pl.ds(place(position, column), 1), :] = pixel_mask(index, column, side) * value
    spread(mixed, mixed3_ends, 0, 4, 0, 1)
    mixed_sources = [
        (mixed3, 0, range(tile_rows)), (mixed3_ends, -2, (-2, -1)), (mixed3_ends, tile_rows - 2, (tile_rows, tile_rows + 1)),
    ]
    ends = jnp.concatenate([four_rows(mixed_sources, -1, 1), four_rows(mixed_sources, last, 1)], axis=0)
    activated, slope = silu_parts(jnp.dot(ends, forward[...], preferred_element_type=F32))
    for position, index in enumerate(carry_rows):
        lanes = slice(position % 2 * channels, (position % 2 + 1) * channels)
        at = position // 2 * PITCH
        here = pl.ds(PAD + position * PITCH, PITCH)
        values = carry[here, :] * slope[at : at + PITCH, lanes]
        carry[here, :] = values
        if 0 <= index <= last:
            half = position // 2
            own_ends[half * PITCH : (half + 1) * PITCH, :] = keep_inner(values, band_cols)
            active_ends[half] = activated[at + PAD : at + PAD + band_cols, lanes]
    spread(carry, carry3_ends, 0, 4, 0, -1)
    carry_sources = [
        (carry3, 0, range(1, last)), (carry3_ends, -1, (-1, 0)), (carry3_ends, tile_rows - 3, (last, tile_rows)),
    ]
    own_sources = [(own, 0, range(1, last)), (own_ends, 0, (0,)), (own_ends, tile_rows - 2, (last,))]

    totals[...] = jnp.zeros(totals.shape, F32)
    skew[...] = jnp.zeros(skew.shape, F32)
    pairs = 4
    query_at = 9 * channels + all_bins + tail
    query_rows = {}
    order = list(range(0, tile_rows, 2 * pairs))
    order = order[1:-1] + [order[0], order[-1]]
    for first in order:
        back = jnp.dot(four_rows(carry_sources, first, pairs), backward[...], preferred_element_type=F32)
        for offset in range(2 * pairs):
            index = first + offset
            lanes = slice(offset % 2 * channels, (offset % 2 + 1) * channels)
            at = offset // 2 * PITCH + PAD
            masked = mask_of(index) * back[at : at + band_cols, lanes]
            change[index] = masked
            query_rows[index] = jnp.sum(masked, axis=0, keepdims=True)
            skew[index % 8, index - index % 8 : index - index % 8 + band_cols, :] += masked
    totals[pl.ds(pl.multiple_of(query_at + row_start, 16), tile_rows), :] = jnp.concatenate([query_rows[index] for index in range(tile_rows)], axis=0)
    reach = tile_rows + band_cols - 8
    for step in range(8):
        totals[pl.ds(9 * channels + col_start + step, reach), :] += skew[step, :reach, :]

    per = 12
    grads = jnp.zeros((channels, 9 * channels), F32)
    for first in range(0, tile_rows, per):
        around = jnp.concatenate(
            [
                jnp.concatenate([rows_of(mixed_sources, index + step) for index in range(first, first + per)], axis=0)
                for step in (-1, 0, 1)
            ],
            axis=1,
        )
        cots = jnp.concatenate([rows_of(own_sources, index) for index in range(first, first + per)], axis=0)
        grads = grads + lax.dot_general(cots, around, (((0,), (0,)), ((), ())), preferred_element_type=F32)
    for tap in range(9):
        totals[tap * channels : (tap + 1) * channels, :] = grads[:, tap * channels : (tap + 1) * channels]
    parts, size = keep.shape[:2]
    mine = half_of(parts)
    for part in range(parts):
        place = lax.bitwise_xor(quarter_of(parts), part)
        keep[part] = totals[pl.ds(pl.multiple_of((mine * parts + place) * size, 16), size), :]
        send[part] = totals[pl.ds(pl.multiple_of(((1 - mine) * parts + place) * size, 16), size), :].astype(BF16)


def late_kernel(
    pair, cot, active, active_ends, change, window, rows_valid, features, context,
    pair_output, pair_grad, features_turned, context_turned,
):
    tile_rows, band_cols, _ = pair.shape
    last = tile_rows - 1
    for index in range(tile_rows):
        mask = window[pl.ds(MARGIN + index, band_cols), :] * rows_valid[pl.ds(index + HALO, 1), :]
        values = active_ends[0] if index == 0 else active_ends[1] if index == last else active[index]
        pair_output[index] = (pair[index].astype(F32) + mask * values).astype(BF16)
        pair_grad[index] = (cot[index].astype(F32) + change[index]).astype(BF16)
    features_turned[...] = features[...].astype(F32).T.astype(BF16)
    context_turned[...] = context[...].astype(F32).T.astype(BF16)


def add_kernel(pieces, copies):
    total = pieces[0].astype(F32)
    for index in range(1, pieces.shape[0]):
        total = total + pieces[index].astype(F32)
    copies[...] = jnp.broadcast_to(total.astype(BF16), copies.shape)


def finish_kernel(
    features_turned, context_turned, projection, *refs
):
    *pieces, feature_grad, proj_grad, conv_grad, whole, feature_out, proj_out, conv_out, sems = refs
    parts = len(pieces) // 2
    mine, theirs = pieces[:parts], pieces[parts:]
    row = lax.axis_index(ROW)
    size, channels = mine[0].shape
    all_bins, tail = features_turned.shape[1], context_turned.shape[1]
    tile_rows = feature_grad.shape[0]
    half = half_of(parts)
    for part in range(parts):
        place = lax.bitwise_xor(quarter_of(parts), part)
        whole[pl.ds(pl.multiple_of((half * parts + place) * size, 16), size), :] = mine[part][...]
        whole[pl.ds(pl.multiple_of(((1 - half) * parts + place) * size, 16), size), :] = theirs[part][...]
    copies = [
        pltpu.make_async_copy(conv_out.at[tap : tap + 3], conv_grad.at[tap : tap + 3], sems.at[tap // 3])
        for tap in range(0, 9, 3)
    ] + [
        pltpu.make_async_copy(proj_out, proj_grad, sems.at[3]),
        pltpu.make_async_copy(feature_out, feature_grad, sems.at[4]),
    ]
    for tap in range(9):
        conv_out[tap] = whole[tap * channels : (tap + 1) * channels, :].astype(F32).T
        if tap % 3 == 2:
            copies[tap // 3].start()
    key_at = 9 * channels
    query_at = key_at + all_bins + tail
    own = features_turned[...]
    proj_out[:, :channels] = jnp.dot(own, whole[query_at : query_at + all_bins, :], preferred_element_type=F32)
    proj_out[:, channels:] = jnp.dot(
        own, whole[key_at : key_at + all_bins, :], preferred_element_type=F32
    ) + jnp.dot(context_turned[...], whole[key_at + all_bins : query_at, :], preferred_element_type=F32)
    copies[3].start()
    start = pl.multiple_of(row * tile_rows, 16)
    both = jnp.concatenate(
        [whole[pl.ds(query_at + start, tile_rows), :], whole[pl.ds(key_at + start, tile_rows), :]], axis=1
    )
    feature_out[...] = lax.dot_general(
        both, projection[...], (((1,), (1,)), ((), ())), preferred_element_type=F32
    ).astype(BF16)
    copies[4].start()
    for copy in copies:
        copy.wait()


def in_hbm(*arrays):
    return [pltpu.with_memory_space_constraint(array, pltpu.HBM) for array in arrays]


def body(
    pair_input, bin_features, context_features, proj_weight, conv_weight, valid_bins, cotangent
):
    tile_rows, band_cols, channels = pair_input.shape
    width = bin_features.shape[1]
    row_count = lax.axis_size(ROW)
    col_count = lax.axis_size("col")
    all_bins = tile_rows * row_count
    tail = context_features.shape[0]
    chips = row_count * col_count // 2
    taken = -(-(tile_rows + 2 * HALO) // 8) * 8
    vmem = pl.BlockSpec(memory_space=pltpu.VMEM)
    anywhere = pl.BlockSpec(memory_space=pl.ANY)

    def shape(*dims, dtype=BF16):
        return jax.ShapeDtypeStruct(dims, dtype)

    layers = EDGES + width // channels
    chunk = pltpu.VMEM((tile_rows, SIDE, channels), BF16)
    to_core, to_chip, to_even, to_odd, context_near, projection, conv_near, valid = pl.pallas_call(
        pack_kernel,
        out_shape=(
            shape(layers, tile_rows, channels),
            shape(layers, tile_rows, channels),
            shape(EDGES, tile_rows, channels),
            shape(EDGES, tile_rows, channels),
            shape(*context_features.shape),
            shape(*proj_weight.shape),
            shape(*conv_weight.shape),
            shape(*valid_bins.shape, dtype=jnp.int32),
        ),
        in_specs=[anywhere] * 7,
        out_specs=(vmem,) * 8,
        scratch_shapes=[
            chunk, chunk, chunk, chunk,
            pltpu.VMEM(bin_features.shape, BF16),
            pltpu.VMEM((tile_rows * SIDE, channels), F32),
            pltpu.VMEM((2, EDGES, tile_rows, channels), BF16),
            pltpu.SemaphoreType.DMA((13,)),
        ],
        compiler_params=PARAMS,
        name="pack",
    )(*in_hbm(pair_input, cotangent, bin_features, context_features, proj_weight, conv_weight, valid_bins))
    other_core = [(0, 1), (1, 0)]
    even_cols = [(i, i ^ 1) for i in range(col_count) if i ^ 1 < col_count]
    odd_cols = []
    for row in range(row_count):
        for column in range(col_count):
            partner = ((column + 1) ^ 1) - 1
            if 0 <= partner < col_count:
                odd_cols.append((row * col_count + column, row * col_count + partner))
            else:
                odd_cols.append((row * col_count + column, (row ^ 1) * col_count + column))
    odd_rows = [(i, ((i + 1) ^ 1) - 1) for i in range(1, row_count - 1)]
    ends = [(0, 3), (3, 0)] if row_count == 4 else []
    from_chip = lax.ppermute(to_chip, ROW, odd_rows + ends)
    from_odd = lax.ppermute(to_odd, ROW + ("col",), odd_cols)
    from_even = lax.ppermute(to_even, "col", even_cols)
    from_core = lax.ppermute(to_core, "core", other_core)
    near_bins = tile_rows + band_cols + 2 * MARGIN
    window, rows_valid, forward, backward, context_key = pl.pallas_call(
        weights_kernel,
        out_shape=(
            shape(near_bins, channels, dtype=F32),
            shape(taken, channels, dtype=F32),
            shape(12 * channels, 2 * channels),
            shape(12 * channels, 2 * channels),
            shape(tail, channels),
        ),
        in_specs=[vmem] * 4,
        out_specs=(vmem,) * 5,
        compiler_params=PARAMS,
        cost_estimate=pl.CostEstimate(flops=1 << 30, bytes_accessed=1 << 21, transcendentals=0),
        name="weights",
    )(valid, context_near, projection, conv_near)
    if row_count == 4:
        sources = [to_core, from_core, from_chip, lax.ppermute(from_chip, "core", other_core)]
    else:
        sources = [lax.all_gather(bin_features, ROW, axis=0, tiled=True)]

    features, query, key = pl.pallas_call(
        prepare_kernel,
        out_shape=(
            shape(all_bins, width),
            shape(tile_rows + 2 * MARGIN, channels, dtype=F32),
            shape(near_bins, channels, dtype=F32),
        ),
        in_specs=[vmem] * (2 + len(sources)),
        out_specs=(vmem,) * 3,
        scratch_shapes=[
            pltpu.VMEM((all_bins + 2 * MARGIN, channels), F32),
            pltpu.VMEM((all_bins + tail + 2 * MARGIN, channels), F32),
        ],
        compiler_params=PARAMS,
        name="prepare",
    )(projection, context_key, *sources)
    from_even, from_odd, key = lax.optimization_barrier((from_even, from_odd, key))
    corner = shape(2, EDGES, SIDE, channels)
    sides, corner_to_core, corner_to_chip = pl.pallas_call(
        corner_kernel,
        out_shape=(shape(2, EDGES, tile_rows, channels), corner, corner),
        in_specs=[vmem] * 2,
        out_specs=(vmem,) * 3,
        compiler_params=PARAMS,
        name="corners",
    )(from_even, from_odd)
    corner_chip = lax.ppermute(corner_to_chip, ROW, odd_rows + ends)
    corner_core = lax.ppermute(corner_to_core, "core", other_core)


    total_rows = 9 * channels + 2 * all_bins + tail
    staged = (row_count, col_count) == (4, 8) and total_rows % 128 == 0
    if staged:
        parts, half = 4, total_rows // 2
    else:
        parts, half = 1, -(-total_rows // (32 * chips)) * 16 * chips
    span = tile_rows * PITCH
    *inner, active = pl.pallas_call(
        inner_kernel,
        out_shape=(
            shape(span, 3 * channels), shape(span, 3 * channels), shape(span, channels),
            shape(*pair_input.shape, dtype=F32),
        ),
        in_specs=[vmem] * 8,
        out_specs=(vmem,) * 4,
        scratch_shapes=[pltpu.VMEM((span + 4 * PAD, channels), F32)] * 2,
        compiler_params=PARAMS,
        name="inner",
    )(pair_input, cotangent, sides, query, key, window, rows_valid, forward)
    active_ends, change, keep, send = pl.pallas_call(
        outer_kernel,
        out_shape=(
            shape(2, band_cols, channels, dtype=F32),
            shape(*pair_input.shape, dtype=F32),
            shape(parts, half // parts, channels, dtype=F32),
            shape(parts, half // parts, channels),
        ),
        in_specs=[vmem] * 16,
        out_specs=(vmem,) * 4,
        scratch_shapes=[
            pltpu.VMEM((2, EDGES, tile_rows, channels), BF16),
            pltpu.VMEM((2, 2, EDGES, SIDE, channels), BF16),
            pltpu.VMEM((4 * PITCH + 4 * PAD, channels), F32),
            pltpu.VMEM((4 * PITCH + 4 * PAD, channels), F32),
            pltpu.VMEM((4 * PITCH, 3 * channels), BF16),
            pltpu.VMEM((4 * PITCH, 3 * channels), BF16),
            pltpu.VMEM((2 * PITCH, channels), BF16),
            pltpu.VMEM((8, tile_rows + band_cols, channels), F32),
            pltpu.VMEM((2 * half, channels), F32),
        ],
        compiler_params=PARAMS,
        name="outer",
    )(
        pair_input, cotangent, from_core, from_chip, sides, corner_core, corner_chip, query, key, window, rows_valid,
        forward, backward, *inner,
    )
    pair_output, pair_grad, features_turned, context_turned = pl.pallas_call(
        late_kernel,
        out_shape=(
            shape(*pair_input.shape), shape(*pair_input.shape), shape(width, all_bins), shape(width, tail),
        ),
        in_specs=[vmem] * 9,
        out_specs=(vmem,) * 4,
        compiler_params=PARAMS,
        name="late",
    )(
        pair_input, cotangent, active, active_ends, change, window, rows_valid, features,
        context_near,
    )

    halves = keep + lax.ppermute(send, "core", other_core).astype(F32)
    if staged:
        def across(values, bits):
            return lax.ppermute(values, ROW + ("col",), [(index, index ^ bits) for index in range(32)])

        plane = (1 + 8, 16 + 8, 16 + 1)
        got = lax.optimization_barrier([across(halves[part].astype(BF16), bits) for part, bits in enumerate(plane, 1)])
        got = [values.astype(F32) for values in got]
        mine = (halves[0] + got[0] + got[1] + got[2]).astype(BF16)
        near, far, opposite = [across(mine, bits) for bits in (2, 4, 6)]
        far, pair_output = lax.optimization_barrier((far, pair_output))
        near, far, opposite = near.astype(F32), far.astype(F32), opposite.astype(F32)
        mine = ((mine.astype(F32) + near) + (far + opposite)).astype(BF16)
        mine = [mine] + [across(mine, bits) for bits in plane]
    else:
        piece = half // chips
        pieces = lax.all_to_all(halves.astype(BF16).reshape(chips, piece, channels), CHIPS, 0, 0)
        copies = pl.pallas_call(
            add_kernel,
            out_shape=shape(chips, piece, channels),
            in_specs=[vmem],
            out_specs=vmem,
            compiler_params=PARAMS,
            name="add",
        )(pieces)
        mine = [lax.all_to_all(copies, CHIPS, 0, 0).reshape(half, channels)]
    theirs = [lax.ppermute(part, "core", other_core) for part in mine]

    feature_grad, proj_grad, conv_grad = pl.pallas_call(
        finish_kernel,
        out_shape=(
            shape(*bin_features.shape),
            shape(*proj_weight.shape, dtype=F32),
            shape(*conv_weight.shape, dtype=F32),
        ),
        in_specs=[vmem] * (3 + 2 * len(mine)),
        out_specs=(anywhere,) * 3,
        scratch_shapes=[
            pltpu.VMEM((2 * half, channels), BF16),
            pltpu.VMEM(bin_features.shape, BF16),
            pltpu.VMEM(proj_weight.shape, F32),
            pltpu.VMEM(conv_weight.shape, F32),
            pltpu.SemaphoreType.DMA((5,)),
        ],
        compiler_params=PARAMS,
        name="finish",
    )(features_turned, context_turned, projection, *mine, *theirs)
    return (pair_output, pair_grad, feature_grad, proj_grad, conv_grad)


def solution(mesh):
    rows, cols = mesh.shape["row"], mesh.shape["col"]
    split = Mesh(mesh.devices.reshape(rows // 2, 2, cols), ("rx", "core", "col"))
    tile = P(ROW, "col", None)
    in_specs = (tile, P(ROW, None), P(), P(), P(), P(), tile)
    out_specs = (tile, tile, P(ROW, None), P(), P())
    return jax.shard_map(body, mesh=split, in_specs=in_specs, out_specs=out_specs, check_vma=False)
```

```python
import jax
import jax.numpy as jnp
from jax import lax
from jax.experimental import pallas as pl
from jax.experimental.pallas import tpu as pltpu
from jax.sharding import Mesh, PartitionSpec as P

ROW = ("rx", "core")
CHIPS = ("rx", "col")
BF16 = jnp.bfloat16
F32 = jnp.float32
HALO = 2
EDGES = HALO + 1
SIDE = 16
MARGIN = 16
PITCH = 64
PAD = 8
PARAMS = pltpu.CompilerParams(vmem_limit_bytes=20 * 1024 * 1024)


def pack_kernel(
    pair, cot, features, context_in, proj_weight_in, conv_weight_in, valid_in,
    to_core, to_chip, outgoing, to_even, to_odd, context, proj_weight, conv_weight, valid, pair_low, pair_high, cot_low, cot_high, own, work, sides, sems
):
    tile_rows, band_cols, channels = pair.shape
    odd_row = lax.rem(lax.axis_index(ROW), 2)
    odd_col = lax.rem(lax.axis_index("col"), 2)
    parts = [
        (pair.at[:, :SIDE], pair_low),
        (pair.at[:, band_cols - SIDE :], pair_high),
        (cot.at[:, :SIDE], cot_low),
        (cot.at[:, band_cols - SIDE :], cot_high),
        (features, own),
    ]
    for target, at_end in ((to_chip, odd_row), (to_core, 1 - odd_row)):
        parts.append((pair.at[pl.ds(at_end * (tile_rows - HALO), HALO)], target.at[:HALO]))
        parts.append((cot.at[pl.ds(at_end * (tile_rows - 1), 1)], target.at[HALO:EDGES]))
    parts += [(context_in, context), (proj_weight_in, proj_weight), (conv_weight_in, conv_weight), (valid_in, valid)]
    copies = [pltpu.make_async_copy(source, target, sems.at[i]) for i, (source, target) in enumerate(parts)]
    for copy in copies:
        copy.start()
    for copy in copies[:4]:
        copy.wait()
    for side, (chunk, kind) in enumerate(((pair_low, cot_low), (pair_high, cot_high))):
        for slot, source, column in (
            (0, chunk, side * (SIDE - 2)), (1, chunk, side * (SIDE - 2) + 1), (2, kind, side * (SIDE - 1)),
        ):
            if slot != 1:
                work[...] = source[...].astype(F32).reshape(tile_rows * SIDE, channels)
            sides[side, slot] = work[pl.ds(column, tile_rows, stride=SIDE), :].astype(BF16)
    to_even[...] = sides[1 - odd_col]
    to_odd[...] = sides[odd_col]
    copies[4].wait()
    for part in range(features.shape[1] // channels):
        values = own[:, part * channels : (part + 1) * channels]
        outgoing[part] = values
        to_core[EDGES + part] = values
    for copy in copies[5:]:
        copy.wait()


def corner_kernel(from_even, from_odd, sides, to_core, to_chip):
    tile_rows = from_even.shape[1]
    odd_row = lax.rem(lax.axis_index(ROW), 2)
    odd_col = lax.rem(lax.axis_index("col"), 2)
    sides[1 - odd_col] = from_even[...]
    sides[odd_col] = from_odd[...]
    for target, at_end in ((to_chip, odd_row), (to_core, 1 - odd_row)):
        start = pl.multiple_of(at_end * (tile_rows - SIDE), 16)
        target[...] = sides[:, :, pl.ds(start, SIDE), :]


def weights_kernel(
    valid, context, proj_weight, conv_weight,
    window, rows_valid, forward, backward, context_key,
):
    channels = window.shape[1]
    bins = valid.shape[0]
    band_total = context.shape[0]
    all_bins = bins - band_total
    tile_rows = all_bins // lax.axis_size(ROW)
    row_start = lax.axis_index(ROW) * tile_rows
    col_start = row_start + lax.axis_index("col") * (band_total // lax.axis_size("col"))
    flags = jnp.broadcast_to(valid[...].reshape(1, bins).astype(F32).astype(BF16), (channels, bins))
    flip = (((1,), (1,)), ((), ()))
    for target, begin, stop in ((window, col_start - MARGIN, bins), (rows_valid, row_start - HALO, all_bins)):
        shape = (target.shape[0], bins)
        bin_index = lax.broadcasted_iota(jnp.int32, shape, 1)
        chosen = jnp.logical_and(bin_index == lax.broadcasted_iota(jnp.int32, shape, 0) + begin, bin_index < stop)
        target[...] = lax.dot_general(chosen.astype(F32).astype(BF16), flags, flip, preferred_element_type=F32)
    forward[...] = jnp.zeros(forward.shape, BF16)
    backward[...] = jnp.zeros(backward.shape, BF16)
    for tap in range(9):
        row_step, step = tap // 3 - 1, tap % 3
        values = conv_weight[tap]
        turned = values.astype(F32).T.astype(BF16)
        for out in range(2):
            lanes = slice(out * channels, (out + 1) * channels)
            at = ((row_step + 1 + out) * 3 + step) * channels
            forward[at : at + channels, lanes] = values
            at = ((1 - row_step + out) * 3 + step) * channels
            backward[at : at + channels, lanes] = turned
    context_key[...] = jnp.dot(context[...], proj_weight[:, channels:], preferred_element_type=F32).astype(BF16)


def prepare_kernel(projection, context_key, *refs):
    sources, (features, query, key, query_rows, key_rows) = refs[:-5], refs[-5:]
    channels = query.shape[1]
    all_bins, tail = features.shape[0], context_key.shape[0]
    row, col = lax.axis_index(ROW), lax.axis_index("col")
    if len(sources) == 1:
        features[...] = sources[0][...]
    else:
        for source, step in zip(sources, (0, 1, 3, 2)):
            rows = source.shape[1]
            skip = source.shape[0] - features.shape[1] // channels
            start = pl.multiple_of(lax.bitwise_xor(row, step) * rows, 16)
            for part in range(source.shape[0] - skip):
                features[pl.ds(start, rows), part * channels : (part + 1) * channels] = source[skip + part]
    tile_rows = query.shape[0] - 2 * MARGIN
    row_start = row * tile_rows
    col_start = row_start + col * (key.shape[0] - 2 * MARGIN - tile_rows)
    proj = jnp.dot(features[...], projection[...], preferred_element_type=F32).astype(BF16).astype(F32)
    margin = jnp.zeros((MARGIN, channels), F32)
    for target, size in ((query_rows, all_bins), (key_rows, all_bins + tail)):
        target[:MARGIN, :] = margin
        target[MARGIN + size :, :] = margin
    query_rows[MARGIN : MARGIN + all_bins, :] = proj[:, :channels]
    key_rows[MARGIN : MARGIN + all_bins, :] = proj[:, channels:]
    key_rows[MARGIN + all_bins : MARGIN + all_bins + tail, :] = context_key[...].astype(F32)
    query[...] = query_rows[pl.ds(pl.multiple_of(row_start, 16), query.shape[0]), :]
    key[...] = key_rows[pl.ds(pl.multiple_of(col_start, 16), key.shape[0]), :]


def half_of(parts):
    core = lax.axis_index("core")
    if parts == 1:
        return core
    return lax.rem(core + lax.axis_index("rx") + lax.axis_index("col"), 2)


def quarter_of(parts):
    if parts == 1:
        return 0
    return 2 * lax.axis_index("rx") + lax.rem(lax.axis_index("col"), 2)


def spread(source, target, first, last, base, sign):
    channels = source.shape[1]
    for index in range(first, last):
        start = (index - base) * PITCH
        for step in range(3):
            target[start : start + PITCH, step * channels : (step + 1) * channels] = source[
                pl.ds(PAD + start + sign * (step - 1), PITCH), :
            ].astype(BF16)


def rows_of(sources, index):
    for array, base, held in sources:
        if index in held:
            return array[(index - base) * PITCH : (index - base + 1) * PITCH, :]
    raise IndexError(index)


def four_rows(sources, first, pairs):
    columns = []
    for step in range(4):
        parts = [rows_of(sources, first + 2 * index + step - 1) for index in range(pairs)]
        columns.append(jnp.concatenate(parts, axis=0))
    return jnp.concatenate(columns, axis=1)


def silu_parts(conv):
    sigma = 0.5 + 0.5 * jnp.tanh(0.5 * conv)
    return conv * sigma, sigma * (1.0 + conv * (1.0 - sigma))


def has_sides():
    col = lax.axis_index("col")
    return (col > 0).astype(F32), (col < lax.axis_size("col") - 1).astype(F32)


def keep_inner(values, band_cols):
    spot = lax.broadcasted_iota(jnp.int32, values.shape, 0)
    inner = jnp.logical_and(spot >= PAD, spot < PAD + band_cols)
    return jnp.where(inner, values, 0.0).astype(BF16)


def inner_kernel(
    pair, cot, sides, query, key, window, rows_valid, forward,
    mixed3, carry3, own, active,
    mixed, carry,
):
    tile_rows, band_cols, channels = pair.shape

    def place(index, column):
        return PAD + index * PITCH + PAD + column

    def mask_of(index):
        return window[pl.ds(MARGIN + index, band_cols), :] * rows_valid[pl.ds(index + HALO, 1), :]

    gap = jnp.zeros((PITCH - band_cols, channels), F32)
    mixed[:PAD, :] = jnp.zeros((PAD, channels), F32)
    mixed[PAD : 2 * PAD, :] = jnp.zeros((PAD, channels), F32)
    for index in range(tile_rows):
        mixed[pl.ds(place(index, band_cols), PITCH - band_cols), :] = gap
        carry[pl.ds(place(index, band_cols), PITCH - band_cols), :] = gap
    for index in range(tile_rows):
        mask = mask_of(index)
        value = mask * (
            pair[index].astype(F32) + query[pl.ds(MARGIN + index, 1), :] + key[pl.ds(MARGIN + index, band_cols), :]
        )
        mixed[pl.ds(place(index, 0), band_cols), :] = value
        carry[pl.ds(place(index, 0), band_cols), :] = mask * cot[index].astype(F32)
    has_low, has_high = has_sides()
    for column, side, slot, has in (
        (-2, 0, 0, has_low), (-1, 0, 1, has_low), (band_cols, 1, 0, has_high), (band_cols + 1, 1, 1, has_high),
    ):
        begin = MARGIN + column
        mask = rows_valid[pl.ds(HALO, tile_rows), :] * window[pl.ds(begin, tile_rows), :] * has
        value = sides[side, slot].astype(F32) + query[pl.ds(MARGIN, tile_rows), :] + key[pl.ds(begin, tile_rows), :]
        mixed[pl.ds(place(0, column), tile_rows, stride=PITCH), :] = mask * value
        if column in (-1, band_cols):
            carry[pl.ds(place(0, column), tile_rows, stride=PITCH), :] = mask * sides[side, HALO].astype(F32)
    spread(mixed, mixed3, 0, tile_rows, 0, 1)

    first, last = 1, tile_rows - 1
    sources = [(mixed3, 0, range(tile_rows))]
    while first < last:
        pairs = min(5, (last - first) // 2)
        conv = jnp.dot(four_rows(sources, first, pairs), forward[...], preferred_element_type=F32)
        activated, slope = silu_parts(conv)
        for offset in range(2 * pairs):
            index = first + offset
            lanes = slice(offset % 2 * channels, (offset % 2 + 1) * channels)
            at = offset // 2 * PITCH
            here = pl.ds(PAD + index * PITCH, PITCH)
            values = carry[here, :] * slope[at : at + PITCH, lanes]
            carry[here, :] = values
            own[index * PITCH : (index + 1) * PITCH, :] = keep_inner(values, band_cols)
            active[index] = activated[at + PAD : at + PAD + band_cols, lanes]
        first += 2 * pairs
    spread(carry, carry3, 1, tile_rows - 1, 0, -1)


def outer_kernel(
    pair, cot, from_core, from_chip, sides, corner_core, corner_chip, query, key, window, rows_valid, forward, backward,
    mixed3, carry3, own,
    active_ends, change, keep, send,
    near, corners, mixed, carry, mixed3_ends, carry3_ends, own_ends, skew, totals,
):
    tile_rows, band_cols, channels = pair.shape
    row, col = lax.axis_index(ROW), lax.axis_index("col")
    all_bins = lax.axis_size(ROW) * tile_rows
    tail = lax.axis_size("col") * band_cols
    row_start = row * tile_rows
    col_start = row_start + col * band_cols
    odd_row = lax.rem(row, 2)
    last = tile_rows - 1
    near[1 - odd_row] = from_core[:EDGES]
    near[odd_row] = from_chip[:EDGES]
    corners[1 - odd_row] = corner_core[...]
    corners[odd_row] = corner_chip[...]

    def place(position, column):
        return PAD + position * PITCH + PAD + column

    def mask_of(index):
        return window[pl.ds(MARGIN + index, band_cols), :] * rows_valid[pl.ds(index + HALO, 1), :]

    has = has_sides()
    mixed_rows = (-2, -1, tile_rows, tile_rows + 1)
    carry_rows = (-1, 0, last, tile_rows)
    gap = jnp.zeros((PITCH - band_cols, channels), F32)
    for array in (mixed, carry):
        array[: 2 * PAD, :] = jnp.zeros((2 * PAD, channels), F32)
        for position in range(4):
            array[pl.ds(place(position, band_cols), PITCH - band_cols), :] = gap

    def corner_of(index, side, slot):
        if index < 0:
            return corners[0, side, slot].astype(F32)[SIDE + index : SIDE + index + 1, :]
        return corners[1, side, slot].astype(F32)[index - tile_rows : index - tile_rows + 1, :]

    def pixel_mask(index, column, side):
        return rows_valid[pl.ds(index + HALO, 1), :] * window[pl.ds(MARGIN + index + column, 1), :] * has[side]

    for position, index in enumerate(mixed_rows):
        source = near[0, HALO + index] if index < 0 else near[1, index - tile_rows]
        row_query = query[pl.ds(MARGIN + index, 1), :]
        mixed[pl.ds(place(position, 0), band_cols), :] = mask_of(index) * (
            source.astype(F32) + row_query + key[pl.ds(MARGIN + index, band_cols), :]
        )
        for column, side, slot in ((-2, 0, 0), (-1, 0, 1), (band_cols, 1, 0), (band_cols + 1, 1, 1)):
            value = corner_of(index, side, slot) + row_query + key[pl.ds(MARGIN + index + column, 1), :]
            mixed[pl.ds(place(position, column), 1), :] = pixel_mask(index, column, side) * value
    for position, index in enumerate(carry_rows):
        source = near[0, HALO] if index < 0 else near[1, HALO] if index > last else cot[index]
        carry[pl.ds(place(position, 0), band_cols), :] = mask_of(index) * source.astype(F32)
        for column, side in ((-1, 0), (band_cols, 1)):
            if 0 <= index <= last:
                chunk = index // SIDE * SIDE
                value = sides[side, HALO, chunk : chunk + SIDE].astype(F32)[index - chunk : index - chunk + 1, :]
            else:
                value = corner_of(index, side, HALO)
            carry[pl.ds(place(position, column), 1), :] = pixel_mask(index, column, side) * value
    spread(mixed, mixed3_ends, 0, 4, 0, 1)
    mixed_sources = [
        (mixed3, 0, range(tile_rows)), (mixed3_ends, -2, (-2, -1)), (mixed3_ends, tile_rows - 2, (tile_rows, tile_rows + 1)),
    ]
    ends = jnp.concatenate([four_rows(mixed_sources, -1, 1), four_rows(mixed_sources, last, 1)], axis=0)
    activated, slope = silu_parts(jnp.dot(ends, forward[...], preferred_element_type=F32))
    for position, index in enumerate(carry_rows):
        lanes = slice(position % 2 * channels, (position % 2 + 1) * channels)
        at = position // 2 * PITCH
        here = pl.ds(PAD + position * PITCH, PITCH)
        values = carry[here, :] * slope[at : at + PITCH, lanes]
        carry[here, :] = values
        if 0 <= index <= last:
            half = position // 2
            own_ends[half * PITCH : (half + 1) * PITCH, :] = keep_inner(values, band_cols)
            active_ends[half] = activated[at + PAD : at + PAD + band_cols, lanes]
    spread(carry, carry3_ends, 0, 4, 0, -1)
    carry_sources = [
        (carry3, 0, range(1, last)), (carry3_ends, -1, (-1, 0)), (carry3_ends, tile_rows - 3, (last, tile_rows)),
    ]
    own_sources = [(own, 0, range(1, last)), (own_ends, 0, (0,)), (own_ends, tile_rows - 2, (last,))]

    totals[...] = jnp.zeros(totals.shape, F32)
    skew[...] = jnp.zeros(skew.shape, F32)
    pairs = 6
    query_at = 9 * channels + all_bins + tail
    query_rows = {}
    order = list(range(0, tile_rows, 2 * pairs))
    order = order[1:-1] + [order[0], order[-1]]
    for first in order:
        back = jnp.dot(four_rows(carry_sources, first, pairs), backward[...], preferred_element_type=F32)
        for offset in range(2 * pairs):
            index = first + offset
            lanes = slice(offset % 2 * channels, (offset % 2 + 1) * channels)
            at = offset // 2 * PITCH + PAD
            masked = mask_of(index) * back[at : at + band_cols, lanes]
            change[index] = masked
            query_rows[index] = jnp.sum(masked, axis=0, keepdims=True)
            skew[index % 8, index - index % 8 : index - index % 8 + band_cols, :] += masked
    per = 24
    grads = jnp.zeros((channels, 9 * channels), F32)
    for first in range(0, tile_rows, per):
        around = jnp.concatenate(
            [
                jnp.concatenate([rows_of(mixed_sources, index + step) for index in range(first, first + per)], axis=0)
                for step in (-1, 0, 1)
            ],
            axis=1,
        )
        cots = jnp.concatenate([rows_of(own_sources, index) for index in range(first, first + per)], axis=0)
        grads = grads + lax.dot_general(cots, around, (((0,), (0,)), ((), ())), preferred_element_type=F32)
    totals[pl.ds(pl.multiple_of(query_at + row_start, 16), tile_rows), :] = jnp.concatenate([query_rows[index] for index in range(tile_rows)], axis=0)
    reach = tile_rows + band_cols - 8
    for step in range(8):
        totals[pl.ds(9 * channels + col_start + step, reach), :] += skew[step, :reach, :]

    for tap in range(9):
        totals[tap * channels : (tap + 1) * channels, :] = grads[:, tap * channels : (tap + 1) * channels]
    parts, size = keep.shape[:2]
    mine = half_of(parts)
    for part in range(parts):
        place = lax.bitwise_xor(quarter_of(parts), part)
        keep[part] = totals[pl.ds(pl.multiple_of((mine * parts + place) * size, 16), size), :]
        send[part] = totals[pl.ds(pl.multiple_of(((1 - mine) * parts + place) * size, 16), size), :].astype(BF16)


def late_kernel(
    pair, cot, active, active_ends, change, window, rows_valid, features, context,
    pair_output, pair_grad, features_turned, context_turned,
):
    tile_rows, band_cols, _ = pair.shape
    last = tile_rows - 1
    for index in range(tile_rows):
        mask = window[pl.ds(MARGIN + index, band_cols), :] * rows_valid[pl.ds(index + HALO, 1), :]
        values = active_ends[0] if index == 0 else active_ends[1] if index == last else active[index]
        pair_output[index] = (pair[index].astype(F32) + mask * values).astype(BF16)
        pair_grad[index] = (cot[index].astype(F32) + change[index]).astype(BF16)
    features_turned[...] = features[...].astype(F32).T.astype(BF16)
    context_turned[...] = context[...].astype(F32).T.astype(BF16)


def add_kernel(pieces, copies):
    total = pieces[0].astype(F32)
    for index in range(1, pieces.shape[0]):
        total = total + pieces[index].astype(F32)
    copies[...] = jnp.broadcast_to(total.astype(BF16), copies.shape)


def finish_kernel(
    features_turned, context_turned, projection, *refs
):
    *pieces, feature_grad, proj_grad, conv_grad, whole, feature_out, proj_out, conv_out, sems = refs
    parts = len(pieces) // 2
    mine, theirs = pieces[:parts], pieces[parts:]
    row = lax.axis_index(ROW)
    size, channels = mine[0].shape
    all_bins, tail = features_turned.shape[1], context_turned.shape[1]
    tile_rows = feature_grad.shape[0]
    half = half_of(parts)
    for part in range(parts):
        place = lax.bitwise_xor(quarter_of(parts), part)
        whole[pl.ds(pl.multiple_of((half * parts + place) * size, 16), size), :] = mine[part][...]
        whole[pl.ds(pl.multiple_of(((1 - half) * parts + place) * size, 16), size), :] = theirs[part][...]
    copies = [
        pltpu.make_async_copy(conv_out.at[tap : tap + 3], conv_grad.at[tap : tap + 3], sems.at[tap // 3])
        for tap in range(0, 9, 3)
    ] + [
        pltpu.make_async_copy(proj_out, proj_grad, sems.at[3]),
        pltpu.make_async_copy(feature_out, feature_grad, sems.at[4]),
    ]
    for tap in range(9):
        conv_out[tap] = whole[tap * channels : (tap + 1) * channels, :].astype(F32).T
        if tap % 3 == 2:
            copies[tap // 3].start()
    key_at = 9 * channels
    query_at = key_at + all_bins + tail
    own = features_turned[...]
    proj_out[:, :channels] = jnp.dot(own, whole[query_at : query_at + all_bins, :], preferred_element_type=F32)
    proj_out[:, channels:] = jnp.dot(
        own, whole[key_at : key_at + all_bins, :], preferred_element_type=F32
    ) + jnp.dot(context_turned[...], whole[key_at + all_bins : query_at, :], preferred_element_type=F32)
    copies[3].start()
    start = pl.multiple_of(row * tile_rows, 16)
    both = jnp.concatenate(
        [whole[pl.ds(query_at + start, tile_rows), :], whole[pl.ds(key_at + start, tile_rows), :]], axis=1
    )
    feature_out[...] = lax.dot_general(
        both, projection[...], (((1,), (1,)), ((), ())), preferred_element_type=F32
    ).astype(BF16)
    copies[4].start()
    for copy in copies:
        copy.wait()


def in_hbm(*arrays):
    return [pltpu.with_memory_space_constraint(array, pltpu.HBM) for array in arrays]


def body(
    pair_input, bin_features, context_features, proj_weight, conv_weight, valid_bins, cotangent
):
    tile_rows, band_cols, channels = pair_input.shape
    width = bin_features.shape[1]
    row_count = lax.axis_size(ROW)
    col_count = lax.axis_size("col")
    all_bins = tile_rows * row_count
    tail = context_features.shape[0]
    chips = row_count * col_count // 2
    taken = -(-(tile_rows + 2 * HALO) // 8) * 8
    vmem = pl.BlockSpec(memory_space=pltpu.VMEM)
    anywhere = pl.BlockSpec(memory_space=pl.ANY)

    def shape(*dims, dtype=BF16):
        return jax.ShapeDtypeStruct(dims, dtype)

    layers = EDGES + width // channels
    chunk = pltpu.VMEM((tile_rows, SIDE, channels), BF16)
    to_core, to_chip, outgoing, to_even, to_odd, context_near, projection, conv_near, valid = pl.pallas_call(
        pack_kernel,
        out_shape=(
            shape(layers, tile_rows, channels),
            shape(EDGES, tile_rows, channels),
            shape(layers - EDGES, tile_rows, channels),
            shape(EDGES, tile_rows, channels),
            shape(EDGES, tile_rows, channels),
            shape(*context_features.shape),
            shape(*proj_weight.shape),
            shape(*conv_weight.shape),
            shape(*valid_bins.shape, dtype=jnp.int32),
        ),
        in_specs=[anywhere] * 7,
        out_specs=(vmem,) * 9,
        scratch_shapes=[
            chunk, chunk, chunk, chunk,
            pltpu.VMEM(bin_features.shape, BF16),
            pltpu.VMEM((tile_rows * SIDE, channels), F32),
            pltpu.VMEM((2, EDGES, tile_rows, channels), BF16),
            pltpu.SemaphoreType.DMA((13,)),
        ],
        compiler_params=PARAMS,
        name="pack",
    )(*in_hbm(pair_input, cotangent, bin_features, context_features, proj_weight, conv_weight, valid_bins))
    other_core = [(0, 1), (1, 0)]
    even_cols = [(i, i ^ 1) for i in range(col_count) if i ^ 1 < col_count]
    odd_cols = []
    for row in range(row_count):
        for column in range(col_count):
            partner = ((column + 1) ^ 1) - 1
            if 0 <= partner < col_count:
                odd_cols.append((row * col_count + column, row * col_count + partner))
            else:
                odd_cols.append((row * col_count + column, (row ^ 1) * col_count + column))
    odd_rows = [(i, ((i + 1) ^ 1) - 1) for i in range(1, row_count - 1)]
    ends = [(0, 3), (3, 0)] if row_count == 4 else []
    from_chip = lax.ppermute(to_chip, ROW, odd_rows + ends)
    from_odd = lax.ppermute(to_odd, ROW + ("col",), odd_cols)
    from_even = lax.ppermute(to_even, "col", even_cols)
    from_core = lax.ppermute(to_core, "core", other_core)
    near_bins = tile_rows + band_cols + 2 * MARGIN
    window, rows_valid, forward, backward, context_key = pl.pallas_call(
        weights_kernel,
        out_shape=(
            shape(near_bins, channels, dtype=F32),
            shape(taken, channels, dtype=F32),
            shape(12 * channels, 2 * channels),
            shape(12 * channels, 2 * channels),
            shape(tail, channels),
        ),
        in_specs=[vmem] * 4,
        out_specs=(vmem,) * 5,
        compiler_params=PARAMS,
        cost_estimate=pl.CostEstimate(flops=1 << 30, bytes_accessed=1 << 21, transcendentals=0),
        name="weights",
    )(valid, context_near, projection, conv_near)
    if row_count == 4:
        arrived = lax.ppermute(outgoing, ROW, odd_rows + ends)
        sources = [to_core, from_core, arrived, lax.ppermute(arrived, "core", other_core)]
    else:
        sources = [lax.all_gather(bin_features, ROW, axis=0, tiled=True)]

    features, query, key = pl.pallas_call(
        prepare_kernel,
        out_shape=(
            shape(all_bins, width),
            shape(tile_rows + 2 * MARGIN, channels, dtype=F32),
            shape(near_bins, channels, dtype=F32),
        ),
        in_specs=[vmem] * (2 + len(sources)),
        out_specs=(vmem,) * 3,
        scratch_shapes=[
            pltpu.VMEM((all_bins + 2 * MARGIN, channels), F32),
            pltpu.VMEM((all_bins + tail + 2 * MARGIN, channels), F32),
        ],
        compiler_params=PARAMS,
        name="prepare",
    )(projection, context_key, *sources)
    from_odd, from_even, from_chip, key = lax.optimization_barrier((from_odd, from_even, from_chip, key))
    corner = shape(2, EDGES, SIDE, channels)
    sides, corner_to_core, corner_to_chip = pl.pallas_call(
        corner_kernel,
        out_shape=(shape(2, EDGES, tile_rows, channels), corner, corner),
        in_specs=[vmem] * 2,
        out_specs=(vmem,) * 3,
        compiler_params=PARAMS,
        name="corners",
    )(from_even, from_odd)
    corner_chip = lax.ppermute(corner_to_chip, ROW, odd_rows + ends)
    corner_core = lax.ppermute(corner_to_core, "core", other_core)


    total_rows = 9 * channels + 2 * all_bins + tail
    staged = (row_count, col_count) == (4, 8) and total_rows % 128 == 0
    if staged:
        parts, half = 4, total_rows // 2
    else:
        parts, half = 1, -(-total_rows // (32 * chips)) * 16 * chips
    span = tile_rows * PITCH
    *inner, active = pl.pallas_call(
        inner_kernel,
        out_shape=(
            shape(span, 3 * channels), shape(span, 3 * channels), shape(span, channels),
            shape(*pair_input.shape, dtype=F32),
        ),
        in_specs=[vmem] * 8,
        out_specs=(vmem,) * 4,
        scratch_shapes=[pltpu.VMEM((span + 4 * PAD, channels), F32)] * 2,
        compiler_params=PARAMS,
        name="inner",
    )(pair_input, cotangent, sides, query, key, window, rows_valid, forward)
    active_ends, change, keep, send = pl.pallas_call(
        outer_kernel,
        out_shape=(
            shape(2, band_cols, channels, dtype=F32),
            shape(*pair_input.shape, dtype=F32),
            shape(parts, half // parts, channels, dtype=F32),
            shape(parts, half // parts, channels),
        ),
        in_specs=[vmem] * 16,
        out_specs=(vmem,) * 4,
        scratch_shapes=[
            pltpu.VMEM((2, EDGES, tile_rows, channels), BF16),
            pltpu.VMEM((2, 2, EDGES, SIDE, channels), BF16),
            pltpu.VMEM((4 * PITCH + 4 * PAD, channels), F32),
            pltpu.VMEM((4 * PITCH + 4 * PAD, channels), F32),
            pltpu.VMEM((4 * PITCH, 3 * channels), BF16),
            pltpu.VMEM((4 * PITCH, 3 * channels), BF16),
            pltpu.VMEM((2 * PITCH, channels), BF16),
            pltpu.VMEM((8, tile_rows + band_cols, channels), F32),
            pltpu.VMEM((2 * half, channels), F32),
        ],
        compiler_params=PARAMS,
        name="outer",
    )(
        pair_input, cotangent, from_core, from_chip, sides, corner_core, corner_chip, query, key, window, rows_valid,
        forward, backward, *inner,
    )
    pair_output, pair_grad, features_turned, context_turned = pl.pallas_call(
        late_kernel,
        out_shape=(
            shape(*pair_input.shape), shape(*pair_input.shape), shape(width, all_bins), shape(width, tail),
        ),
        in_specs=[vmem] * 9,
        out_specs=(vmem,) * 4,
        compiler_params=PARAMS,
        name="late",
    )(
        pair_input, cotangent, active, active_ends, change, window, rows_valid, features,
        context_near,
    )

    halves = keep + lax.ppermute(send, "core", other_core).astype(F32)
    if staged:
        def across(values, bits):
            return lax.ppermute(values, ROW + ("col",), [(index, index ^ bits) for index in range(32)])

        plane = (1 + 8, 16 + 8, 16 + 1)
        got = lax.optimization_barrier([across(halves[part].astype(BF16), bits) for part, bits in enumerate(plane, 1)])
        got = [values.astype(F32) for values in got]
        mine = (halves[0] + got[0] + got[1] + got[2]).astype(BF16)
        near, far, opposite = [across(mine, bits) for bits in (2, 4, 6)]
        far, pair_output = lax.optimization_barrier((far, pair_output))
        near, far, opposite = near.astype(F32), far.astype(F32), opposite.astype(F32)
        mine = ((mine.astype(F32) + near) + (far + opposite)).astype(BF16)
        mine = [mine] + [across(mine, bits) for bits in plane]
    else:
        piece = half // chips
        pieces = lax.all_to_all(halves.astype(BF16).reshape(chips, piece, channels), CHIPS, 0, 0)
        copies = pl.pallas_call(
            add_kernel,
            out_shape=shape(chips, piece, channels),
            in_specs=[vmem],
            out_specs=vmem,
            compiler_params=PARAMS,
            name="add",
        )(pieces)
        mine = [lax.all_to_all(copies, CHIPS, 0, 0).reshape(half, channels)]
    theirs = [lax.ppermute(part, "core", other_core) for part in mine]

    feature_grad, proj_grad, conv_grad = pl.pallas_call(
        finish_kernel,
        out_shape=(
            shape(*bin_features.shape),
            shape(*proj_weight.shape, dtype=F32),
            shape(*conv_weight.shape, dtype=F32),
        ),
        in_specs=[vmem] * (3 + 2 * len(mine)),
        out_specs=(anywhere,) * 3,
        scratch_shapes=[
            pltpu.VMEM((2 * half, channels), BF16),
            pltpu.VMEM(bin_features.shape, BF16),
            pltpu.VMEM(proj_weight.shape, F32),
            pltpu.VMEM(conv_weight.shape, F32),
            pltpu.SemaphoreType.DMA((5,)),
        ],
        compiler_params=PARAMS,
        name="finish",
    )(features_turned, context_turned, projection, *mine, *theirs)
    return (pair_output, pair_grad, feature_grad, proj_grad, conv_grad)


def solution(mesh):
    rows, cols = mesh.shape["row"], mesh.shape["col"]
    split = Mesh(mesh.devices.reshape(rows // 2, 2, cols), ("rx", "core", "col"))
    tile = P(ROW, "col", None)
    in_specs = (tile, P(ROW, None), P(), P(), P(), P(), tile)
    out_specs = (tile, tile, P(ROW, None), P(), P())
    return jax.shard_map(body, mesh=split, in_specs=in_specs, out_specs=out_specs, check_vma=False)
```
